512 devices in a mesh: branch: 4 (over x), row: 16 (over y, z_hi, core), col: 8 (over z_lo).
Axes of the slice: x: 4, y: 4, z: 16 (z_hi: 2, z_lo: 8; z = z_hi * 8 + z_lo), core: 2. Of those that a mesh axis runs over, the one named last changes fastest.
Arguments:
- feature_one: bfloat16 [512, 73728], P(('branch', 'row'), 'col'), may hold values from -6 to 6
- feature_two: bfloat16 [256, 73728], P(('branch', 'row'), 'col'), may hold values from -6 to 6
- feature_three: bfloat16 [128, 73728], P(('branch', 'row'), 'col'), may hold values from -6 to 6
- feature_four: bfloat16 [64, 73728], P(('branch', 'row'), 'col'), may hold values from -6 to 6
- output_one: bfloat16 [512, 73728], P(('branch', 'row'), 'col'), may hold values from -6 to 6
- output_two: bfloat16 [256, 73728], P(('branch', 'row'), 'col'), may hold values from -6 to 6
- output_three: bfloat16 [128, 73728], P(('branch', 'row'), 'col'), may hold values from -6 to 6
- upstream_one: bfloat16 [512, 73728], P(('branch', 'row'), 'col'), may hold values from -6 to 6
- upstream_two: bfloat16 [256, 73728], P(('branch', 'row'), 'col'), may hold values from -6 to 6
- upstream_three: bfloat16 [128, 73728], P(('branch', 'row'), 'col'), may hold values from -6 to 6
- kernel_one: bfloat16 [3, 3, 48, 48], replicated, may hold values from -0.3125 to 0.3125
- kernel_two: bfloat16 [3, 3, 96, 96], replicated, may hold values from -0.21875 to 0.21875
- kernel_three: bfloat16 [3, 3, 192, 192], replicated, may hold values from -0.15625 to 0.15625
- stride_one_two: bfloat16 [3, 3, 48, 96], replicated, may hold values from -0.3125 to 0.3125
- stride_two_three: bfloat16 [3, 3, 96, 192], replicated, may hold values from -0.21875 to 0.21875
- mixer_two_one: bfloat16 [96, 48], replicated, may hold values from -0.625 to 0.625
- mixer_three_one: bfloat16 [192, 48], replicated, may hold values from -0.4375 to 0.4375
- mixer_four_one: bfloat16 [384, 48], replicated, may hold values from -0.3125 to 0.3125
- mixer_three_two: bfloat16 [192, 96], replicated, may hold values from -0.4375 to 0.4375
- mixer_four_two: bfloat16 [384, 96], replicated, may hold values from -0.3125 to 0.3125
- mixer_four_three: bfloat16 [384, 192], replicated, may hold values from -0.3125 to 0.3125
Outputs:
- grad_one: bfloat16 [512, 73728], P(('branch', 'row'), 'col')
- grad_two: bfloat16 [256, 73728], P(('branch', 'row'), 'col')
- grad_three: bfloat16 [128, 73728], P(('branch', 'row'), 'col')
- grad_four: bfloat16 [64, 73728], P(('branch', 'row'), 'col')
- weight_grads: float32 [804096], P(('row', 'col'))
The draws below stay inside these ranges and needn't reach their ends.
All inputs are finite; a program needn't handle non-finite values.
Results may differ from the reference program's by a relative error of at most 0.008.
Values may be sent and summed in bfloat16 or wider, within the bound.
A program may use at most 64 MiB of HBM per device.

```python
import jax
import jax.numpy as jnp
from jax import lax

C1 = 48
C2 = 96
C3 = 192
C4 = 384
H4 = 64
W4 = 192


def block_scale(rng, dims, split, smallest, top_value):
    def one(position, blocks):
        draws = jax.random.uniform(jax.random.fold_in(jax.random.fold_in(rng, 6), position), (blocks,), jnp.float32, smallest / len(split), top_value / len(split))
        return jnp.repeat(jnp.exp(draws), dims[position] // blocks).reshape((-1,) + (1,) * (len(dims) - position - 1))

    level = one(*split[0])
    for cut in split[1:]:
        level = level * one(*cut)
    return level


def bell_draw(rng, extent, spread, bound, cuts=(), held_as=jnp.bfloat16):
    array = jax.random.normal(rng, extent, jnp.float32) * spread
    if len(cuts) > 0:
        array = block_scale(rng, extent, cuts, -0.22, 0.18) * array
    return jnp.clip(array, min=-bound, max=bound).astype(held_as)


def setup_inputs(seed: int = 0) -> dict:
    key_of = jax.random.split(jax.random.key(seed), 22)
    return {
        "feature_one": bell_draw(key_of[0], (8 * H4, 8 * W4 * C1), 1.0, 6.0, ((0, 64), (1, 8))),
        "feature_two": bell_draw(key_of[1], (4 * H4, 4 * W4 * C2), 1.0, 6.0, ((0, 64), (1, 8))),
        "feature_three": bell_draw(key_of[2], (2 * H4, 2 * W4 * C3), 1.0, 6.0, ((0, 64), (1, 8))),
        "feature_four": bell_draw(key_of[3], (H4, W4 * C4), 1.0, 6.0, ((0, 64), (1, 8))),
        "output_one": bell_draw(key_of[4], (8 * H4, 8 * W4 * C1), 1.0, 6.0, ((0, 64), (1, 8))),
        "output_two": bell_draw(key_of[5], (4 * H4, 4 * W4 * C2), 1.0, 6.0, ((0, 64), (1, 8))),
        "output_three": bell_draw(key_of[6], (2 * H4, 2 * W4 * C3), 1.0, 6.0, ((0, 64), (1, 8))),
        "upstream_one": bell_draw(key_of[7], (8 * H4, 8 * W4 * C1), 1.0, 6.0, ((0, 64), (1, 8))),
        "upstream_two": bell_draw(key_of[8], (4 * H4, 4 * W4 * C2), 1.0, 6.0, ((0, 64), (1, 8))),
        "upstream_three": bell_draw(key_of[9], (2 * H4, 2 * W4 * C3), 1.0, 6.0, ((0, 64), (1, 8))),
        "kernel_one": bell_draw(key_of[10], (3, 3, C1, C1), (9 * C1) ** -0.5, 0.3125),
        "kernel_two": bell_draw(key_of[11], (3, 3, C2, C2), (9 * C2) ** -0.5, 0.21875),
        "kernel_three": bell_draw(key_of[12], (3, 3, C3, C3), (9 * C3) ** -0.5, 0.15625),
        "stride_one_two": bell_draw(key_of[13], (3, 3, C1, C2), (9 * C1) ** -0.5, 0.3125),
        "stride_two_three": bell_draw(key_of[14], (3, 3, C2, C3), (9 * C2) ** -0.5, 0.21875),
        "mixer_two_one": bell_draw(key_of[15], (C2, C1), C2 ** -0.5, 0.625),
        "mixer_three_one": bell_draw(key_of[16], (C3, C1), C3 ** -0.5, 0.4375),
        "mixer_four_one": bell_draw(key_of[17], (C4, C1), C4 ** -0.5, 0.3125),
        "mixer_three_two": bell_draw(key_of[18], (C3, C2), C3 ** -0.5, 0.4375),
        "mixer_four_two": bell_draw(key_of[19], (C4, C2), C4 ** -0.5, 0.3125),
        "mixer_four_three": bell_draw(key_of[20], (C4, C3), C4 ** -0.5, 0.3125),
    }


EPSILON = 1e-06
PARITY = ((1, 1), (0, 0), (1, 0))
HIGHEST = lax.Precision.HIGHEST

def as_cells(flat, channels):
    return flat.astype(jnp.float32).reshape(flat.shape[0], flat.shape[1] // channels, channels)

def rounded(values):
    narrow = lax.optimization_barrier(values.astype(jnp.bfloat16))
    return narrow.astype(jnp.float32)

def pool_sum(field_in, factor):
    height, breadth, channels = field_in.shape
    return field_in.reshape(height // factor, factor, breadth // factor, factor, channels).sum(axis=(1, 3))

def project(field_in, mixer):
    return jnp.einsum('hwi,ji->hwj', field_in, mixer.astype(jnp.float32), precision=HIGHEST)

def mixer_grad(source, pooled):
    return jnp.einsum('hwj,hwi->ji', source, pooled, precision=HIGHEST)

def down_backward(source, grad_ext, weight):
    tile_rows = grad_ext.shape[0] - 1
    tile_cols = grad_ext.shape[1] - 1
    channels = source.shape[2]
    parts = source.reshape(tile_rows, 2, tile_cols, 2, channels)
    weight = weight.astype(jnp.float32)
    blocks = [jnp.zeros((tile_rows, tile_cols, channels), jnp.float32) for repeat in range(4)]
    kernel_rows = []
    for tap_row in range(3):
        row_parity, row_offset = PARITY[tap_row]
        kernel_row = []
        for tap_col in range(3):
            col_parity, col_offset = PARITY[tap_col]
            grad_piece = grad_ext[row_offset:row_offset + tile_rows, col_offset:col_offset + tile_cols]
            parity_part = parts[:, row_parity, :, col_parity]
            kernel_row.append(jnp.einsum('hwi,hwo->io', parity_part, grad_piece, precision=HIGHEST))
            block_slot = 2 * row_parity + col_parity
            blocks[block_slot] = blocks[block_slot] + jnp.einsum('hwo,io->hwi', grad_piece, weight[tap_row, tap_col], precision=HIGHEST)
        kernel_rows.append(jnp.stack(kernel_row))
    upper_half = jnp.stack([blocks[0], blocks[1]], axis=2)
    lower_half = jnp.stack([blocks[2], blocks[3]], axis=2)
    full_grid = jnp.stack([upper_half, lower_half], axis=1).reshape(2 * tile_rows, 2 * tile_cols, channels)
    return (full_grid, jnp.stack(kernel_rows))

def conv_backward(source, delta, weight):
    tile_rows, tile_cols = (source.shape[0], source.shape[1])
    grad_pad = jnp.pad(delta, ((1, 1), (1, 1), (0, 0)))
    weight = weight.astype(jnp.float32)
    result = jnp.zeros((tile_rows, tile_cols, weight.shape[2]), jnp.float32)
    kernel_rows = []
    for tap_row in range(3):
        kernel_row = []
        for tap_col in range(3):
            grad_piece = grad_pad[2 - tap_row:2 - tap_row + tile_rows, 2 - tap_col:2 - tap_col + tile_cols]
            result = result + jnp.einsum('hwo,io->hwi', grad_piece, weight[tap_row, tap_col], precision=HIGHEST)
            kernel_row.append(jnp.einsum('hwi,hwo->io', source, grad_piece, precision=HIGHEST))
        kernel_rows.append(jnp.stack(kernel_row))
    return (result, jnp.stack(kernel_rows))

def reference(feature_one, feature_two, feature_three, feature_four, output_one, output_two, output_three, upstream_one, upstream_two, upstream_three, kernel_one, kernel_two, kernel_three, stride_one_two, stride_two_three, mixer_two_one, mixer_three_one, mixer_four_one, mixer_three_two, mixer_four_two, mixer_four_three):
    cells_one = as_cells(feature_one, C1)
    cells_two = as_cells(feature_two, C2)
    cells_three = as_cells(feature_three, C3)
    cells_four = as_cells(feature_four, C4)
    saved_one = as_cells(output_one, C1)
    saved_two = as_cells(output_two, C2)
    saved_three = as_cells(output_three, C3)
    incoming_one = as_cells(upstream_one, C1)
    incoming_two = as_cells(upstream_two, C2)
    incoming_three = as_cells(upstream_three, C3)
    framed_two = jnp.pad(incoming_two, ((0, 1), (0, 1), (0, 0)))
    framed_three = jnp.pad(incoming_three, ((0, 1), (0, 1), (0, 0)))
    spread_one, stride_grad_one = down_backward(saved_one, framed_two, stride_one_two)
    spread_two, stride_grad_two = down_backward(saved_two, framed_three, stride_two_three)
    half_one = pool_sum(incoming_one, 2)
    quarter_one = pool_sum(half_one, 2)
    eighth_one = pool_sum(quarter_one, 2)
    half_two = pool_sum(incoming_two, 2)
    quarter_two = pool_sum(half_two, 2)
    half_three = pool_sum(incoming_three, 2)
    pooled_one_two = rounded(half_one)
    pooled_one_three = rounded(quarter_one)
    pooled_one_four = rounded(eighth_one)
    pooled_two_three = rounded(half_two)
    pooled_two_four = rounded(quarter_two)
    pooled_three_four = rounded(half_three)
    delta_one = rounded(incoming_one + spread_one)
    delta_two = rounded(incoming_two + project(pooled_one_two, mixer_two_one) + spread_two)
    delta_three = rounded(incoming_three + project(pooled_one_three, mixer_three_one) + project(pooled_two_three, mixer_three_two))
    back_four = project(pooled_one_four, mixer_four_one) + project(pooled_two_four, mixer_four_two) + project(pooled_three_four, mixer_four_three)
    back_one, kernel_grad_one = conv_backward(cells_one, delta_one, kernel_one)
    back_two, kernel_grad_two = conv_backward(cells_two, delta_two, kernel_two)
    back_three, kernel_grad_three = conv_backward(cells_three, delta_three, kernel_three)
    pieces = (kernel_grad_one, kernel_grad_two, kernel_grad_three, stride_grad_one, stride_grad_two, mixer_grad(saved_two, pooled_one_two), mixer_grad(saved_three, pooled_one_three), mixer_grad(cells_four, pooled_one_four), mixer_grad(saved_three, pooled_two_three), mixer_grad(cells_four, pooled_two_four), mixer_grad(cells_four, pooled_three_four))
    flat = jnp.concatenate([piece_grad.reshape(-1) for piece_grad in pieces])
    spread_rms = jnp.sqrt(jnp.mean(flat * flat) + EPSILON)
    weight_grads = flat * jnp.minimum(jnp.float32(1.0), 1.0 / spread_rms)
    return (back_one.astype(jnp.bfloat16).reshape(feature_one.shape), back_two.astype(jnp.bfloat16).reshape(feature_two.shape), back_three.astype(jnp.bfloat16).reshape(feature_three.shape), back_four.astype(jnp.bfloat16).reshape(feature_four.shape), weight_grads)
```

```python
import functools

import jax
import jax.numpy as jnp
from jax import lax
from jax.experimental import pallas as pl
from jax.experimental.pallas import tpu as pltpu
from jax.sharding import PartitionSpec as P

EPSILON = 1e-06
MESH = pl.DeviceIdType.MESH
TOTAL = 804096
SHARE = 6282
WINDOW = 64
FLAT_ROWS = 6296


def share_place(share):
    row, col = divmod(share, 8)
    core, z_hi, y = row % 2, (row // 2) % 2, row // 4
    half, quarter = divmod(col, 4)
    return ((core * 4 + y) * 4 + quarter) * 4 + z_hi * 2 + half


def pack_shares(flat_ref, packed_ref):
    for share in range(128):
        start = SHARE * share // 1024 * 8
        place = share_place(share) * WINDOW
        packed_ref[place : place + WINDOW, :] = flat_ref[start : start + WINDOW, :].astype(jnp.bfloat16)


def reduce_kernel(
    packed_ref,
    out_ref,
    from_core,
    sum_core,
    from_plane,
    sum_plane,
    from_line,
    share_buf,
    square_buf,
    from_near,
    near_buf,
    from_far,
    core_sems,
    plane_send,
    plane_recv,
    line_send,
    line_recv,
    share_send,
    share_recv,
    near_send,
    near_recv,
    far_send,
    far_recv,
):
    x = lax.axis_index("branch")
    row = lax.axis_index("row")
    col = lax.axis_index("col")
    core, z_hi, y = row % 2, (row // 2) % 2, row // 4
    z = z_hi * 8 + col
    partner = (x, row + 1 - 2 * core, col)

    def plane_peer(step):
        there = (x * 4 + y + step) % 16
        return there, (there // 4, (there % 4) * 4 + z_hi * 2 + core, col)

    def line_peer(step):
        there = (z + step) % 16
        return (x, y * 4 + (there // 8) * 2 + core, there % 8)

    def near_peer(step):
        there = (y * 2 + core + step) % 8
        return (x, (there // 2) * 4 + z_hi * 2 + there % 2, col)

    def greet(peer):
        pl.semaphore_signal(barrier, inc=1, device_id=peer, device_id_type=MESH)

    barrier = pltpu.get_barrier_semaphore()
    greet(partner)

    @pl.loop(1, 16)
    def _(step):
        greet(plane_peer(step)[1])
        greet(line_peer(step))

    @pl.loop(1, 8)
    def _(step):
        greet(near_peer(step))

    pl.semaphore_wait(barrier, 38)

    def remote(src, dst, send_sem, recv_sem, peer):
        return pltpu.make_async_remote_copy(
            src_ref=src, dst_ref=dst, send_sem=send_sem, recv_sem=recv_sem,
            device_id=peer, device_id_type=MESH,
        )

    half = 64 * WINDOW
    across = remote(
        packed_ref.at[pl.ds(pl.multiple_of((1 - core) * half, half), half)],
        from_core, core_sems.at[0], core_sems.at[1], partner,
    )
    across.start()
    across.wait()

    @pl.loop(0, 16)
    def _(block):
        start = pl.multiple_of(block * 256, 256)
        mine = packed_ref[pl.ds(pl.multiple_of(core * half, half) + start, 256), :]
        theirs = from_core[pl.ds(start, 256), :]
        sum_core[pl.ds(start, 256), :] = (mine.astype(jnp.float32) + theirs.astype(jnp.float32)).astype(jnp.bfloat16)

    def plane_copy(step):
        there, peer = plane_peer(step)
        place = (there % 4) * 4 + there // 4
        return remote(
            sum_core.at[pl.ds(pl.multiple_of(place * 256, 256), 256)],
            from_plane.at[step - 1], plane_send.at[step - 1], plane_recv.at[step - 1], peer,
        )

    @pl.loop(1, 16)
    def _(step):
        plane_copy(step).start()

    @pl.loop(1, 16)
    def _(step):
        plane_copy(step).wait()

    @pl.loop(0, 4)
    def _(block):
        start = pl.multiple_of(block * WINDOW, WINDOW)
        own = pl.multiple_of((y * 4 + x) * 256 + start, WINDOW)
        total = sum_core[pl.ds(own, WINDOW), :].astype(jnp.float32)
        for step in range(15):
            total = total + from_plane[step, pl.ds(start, WINDOW), :].astype(jnp.float32)
        sum_plane[pl.ds(start, WINDOW), :] = total.astype(jnp.bfloat16)

    def line_copy(block):
        target = (block // 2) * 8 + (block % 2) * 4 + x
        step = (z - target + 16) % 16
        slot = (step + 15) % 16
        return step, remote(
            sum_plane.at[pl.ds(pl.multiple_of(block * WINDOW, WINDOW), WINDOW)],
            from_line.at[slot], line_send.at[block], line_recv.at[slot],
            (x, y * 4 + (target // 8) * 2 + core, target % 8),
        )

    for block in range(4):
        step, copy = line_copy(block)

        @pl.when(step != 0)
        def _():
            copy.start()

    owner_x = col % 4
    owner = owner_x == x

    def share_copy(step):
        return remote(
            share_buf, share_buf, share_send.at[step - 1], share_recv.at[0],
            ((x + step) % 4, row, col),
        )

    @pl.when(owner)
    def _():
        @pl.loop(0, 15)
        def _(slot):
            remote(
                sum_plane.at[pl.ds(0, WINDOW)], from_line.at[slot], line_send.at[0], line_recv.at[slot], partner
            ).wait_recv()

        own = pl.multiple_of((z_hi * 2 + col // 4) * WINDOW, WINDOW)
        total = sum_plane[pl.ds(own, WINDOW), :].astype(jnp.float32)
        for slot in range(15):
            total = total + from_line[slot].astype(jnp.float32)
        share_buf[...] = total
        for step in range(1, 4):
            share_copy(step).start()

    @pl.when(jnp.logical_not(owner))
    def _():
        share_copy(1).wait_recv()

    offset = (SHARE * (row * 8 + col)) % 1024
    place = lax.broadcasted_iota(jnp.int32, (WINDOW, 128), 0) * 128 + lax.broadcasted_iota(jnp.int32, (WINDOW, 128), 1)
    inside = jnp.logical_and(place >= offset, place < offset + SHARE)
    share = share_buf[...]
    squares = jnp.where(inside, share * share, 0.0)
    square_buf[...] = squares.reshape(8, 8, 128).sum(axis=0)

    def near_copy(step):
        return remote(
            square_buf, from_near.at[step - 1], near_send.at[step - 1], near_recv.at[step - 1], near_peer(step)
        )

    @pl.loop(1, 8)
    def _(step):
        near_copy(step).start()

    @pl.loop(1, 8)
    def _(step):
        near_copy(step).wait()

    near_buf[...] = square_buf[...] + from_near[...].sum(axis=0)

    def far_copy(step):
        return remote(
            near_buf, from_far.at[step - 1], far_send.at[step - 1], far_recv.at[step - 1], line_peer(step)
        )

    @pl.loop(1, 16)
    def _(step):
        far_copy(step).start()

    @pl.loop(1, 16)
    def _(step):
        far_copy(step).wait()

    total_squares = jnp.sum(near_buf[...] + from_far[...].sum(axis=0), keepdims=True)
    spread_rms = jnp.sqrt(total_squares / TOTAL + EPSILON)
    out_ref[...] = share_buf[...] * jnp.minimum(jnp.float32(1.0), 1.0 / spread_rms)

    for block in range(4):
        step, copy = line_copy(block)

        @pl.when(step != 0)
        def _():
            copy.wait_send()

    @pl.when(owner)
    def _():
        for step in range(1, 4):
            share_copy(step).wait_send()


def reduce_shares(packed):
    dma = pltpu.SemaphoreType.DMA
    window = pl.pallas_call(
        reduce_kernel,
        out_shape=jax.ShapeDtypeStruct((WINDOW, 128), jnp.float32),
        in_specs=[pl.BlockSpec(memory_space=pltpu.VMEM)],
        out_specs=pl.BlockSpec(memory_space=pltpu.VMEM),
        scratch_shapes=[
            pltpu.VMEM((64 * WINDOW, 128), jnp.bfloat16),
            pltpu.VMEM((64 * WINDOW, 128), jnp.bfloat16),
            pltpu.VMEM((15, 4 * WINDOW, 128), jnp.bfloat16),
            pltpu.VMEM((4 * WINDOW, 128), jnp.bfloat16),
            pltpu.VMEM((15, WINDOW, 128), jnp.bfloat16),
            pltpu.VMEM((WINDOW, 128), jnp.float32),
            pltpu.VMEM((8, 128), jnp.float32),
            pltpu.VMEM((7, 8, 128), jnp.float32),
            pltpu.VMEM((8, 128), jnp.float32),
            pltpu.VMEM((15, 8, 128), jnp.float32),
            dma((2,)),
            dma((15,)),
            dma((15,)),
            dma((4,)),
            dma((15,)),
            dma((3,)),
            dma((1,)),
            dma((7,)),
            dma((7,)),
            dma((15,)),
            dma((15,)),
        ],
        compiler_params=pltpu.CompilerParams(
            collective_id=0, has_side_effects=True, vmem_limit_bytes=32 * 1024 * 1024
        ),
        name="reduce_shares",
    )(packed)
    offset = (SHARE * lax.axis_index(("row", "col"))) % 1024
    return lax.dynamic_slice(window.reshape(WINDOW * 128), (offset,), (SHARE,))


PARITY = ((1, 1), (0, 0), (1, 0))


def passed_along(value, axis, steps):
    count = lax.axis_size(axis)
    leading, last = (max(0, -steps), min(count, count - steps))
    return lax.ppermute(value, axis, [(source, source + steps) for source in range(leading, last)])


def with_halo(cells, sides, width):
    for axis, dim in sides:
        count = lax.axis_size(axis)
        ends = count - 1
        head = lax.slice_in_dim(cells, 0, width, axis=dim)
        tail = lax.slice_in_dim(cells, cells.shape[dim] - width, cells.shape[dim], axis=dim)
        cells = jnp.concatenate(
            [
                lax.ppermute(tail, axis, [(i, (i + 1) % count) for i in range(ends)]),
                cells,
                lax.ppermute(head, axis, [((i + 1) % count, i) for i in range(ends)]),
            ],
            axis=dim,
        )
    return cells


def as_cells(flat, channels):
    return flat.reshape(flat.shape[0], flat.shape[1] // channels, channels)


def pool_sum(field_in, factor):
    height, breadth, channels = field_in.shape
    return field_in.reshape(height // factor, factor, breadth // factor, factor, channels).sum(
        axis=(1, 3), dtype=jnp.float32
    )


def project(field_in, mixer):
    return jnp.einsum("hwi,ji->hwj", field_in, mixer, preferred_element_type=jnp.float32)


def mixer_grad(source, pooled):
    return jnp.einsum("hwj,hwi->ji", source, pooled, preferred_element_type=jnp.float32)


def extend_next(field_in):
    below = passed_along(field_in[:1], ("branch", "row"), -1)
    taller = jnp.concatenate([field_in, below], axis=0)
    beside = passed_along(taller[:, :1], "col", -1)
    return jnp.concatenate([taller, beside], axis=1)


def with_frame(field_in):
    return with_halo(field_in, ((("branch", "row"), 0), ("col", 1)), 1)


def down_backward(source, grad_ext, weight):
    tile_rows = grad_ext.shape[0] - 1
    tile_cols = grad_ext.shape[1] - 1
    channels = source.shape[2]
    parts = source.reshape(tile_rows, 2, tile_cols, 2, channels)
    blocks = [jnp.zeros((tile_rows, tile_cols, channels), jnp.float32) for repeat in range(4)]
    kernel_rows = []
    for tap_row in range(3):
        row_parity, row_offset = PARITY[tap_row]
        kernel_row = []
        for tap_col in range(3):
            col_parity, col_offset = PARITY[tap_col]
            grad_piece = grad_ext[
                row_offset : row_offset + tile_rows, col_offset : col_offset + tile_cols
            ]
            parity_part = parts[:, row_parity, :, col_parity]
            kernel_row.append(
                jnp.einsum(
                    "hwi,hwo->io", parity_part, grad_piece, preferred_element_type=jnp.float32
                )
            )
            block_slot = 2 * row_parity + col_parity
            blocks[block_slot] = blocks[block_slot] + jnp.einsum(
                "hwo,io->hwi",
                grad_piece,
                weight[tap_row, tap_col],
                preferred_element_type=jnp.float32,
            )
        kernel_rows.append(jnp.stack(kernel_row))
    upper_half = jnp.stack([blocks[0], blocks[1]], axis=2)
    lower_half = jnp.stack([blocks[2], blocks[3]], axis=2)
    full_grid = jnp.stack([upper_half, lower_half], axis=1).reshape(
        2 * tile_rows, 2 * tile_cols, channels
    )
    return (full_grid, jnp.stack(kernel_rows))


def conv_backward(source, grad_pad, weight):
    tile_rows, tile_cols = (source.shape[0], source.shape[1])
    result = jnp.zeros((tile_rows, tile_cols, weight.shape[2]), jnp.float32)
    kernel_rows = []
    for tap_row in range(3):
        kernel_row = []
        for tap_col in range(3):
            grad_piece = grad_pad[
                2 - tap_row : 2 - tap_row + tile_rows, 2 - tap_col : 2 - tap_col + tile_cols
            ]
            result = result + jnp.einsum(
                "hwo,io->hwi",
                grad_piece,
                weight[tap_row, tap_col],
                preferred_element_type=jnp.float32,
            )
            kernel_row.append(
                jnp.einsum("hwi,hwo->io", source, grad_piece, preferred_element_type=jnp.float32)
            )
        kernel_rows.append(jnp.stack(kernel_row))
    return (result, jnp.stack(kernel_rows))


def local(
    feature_one,
    feature_two,
    feature_three,
    feature_four,
    output_one,
    output_two,
    output_three,
    upstream_one,
    upstream_two,
    upstream_three,
    kernel_one,
    kernel_two,
    kernel_three,
    stride_one_two,
    stride_two_three,
    mixer_two_one,
    mixer_three_one,
    mixer_four_one,
    mixer_three_two,
    mixer_four_two,
    mixer_four_three,
):
    width_one = kernel_one.shape[2]
    width_two = kernel_two.shape[2]
    width_three = kernel_three.shape[2]
    width_four = mixer_four_one.shape[0]
    cells_one = as_cells(feature_one, width_one)
    cells_two = as_cells(feature_two, width_two)
    cells_three = as_cells(feature_three, width_three)
    cells_four = as_cells(feature_four, width_four)
    saved_one = as_cells(output_one, width_one)
    saved_two = as_cells(output_two, width_two)
    saved_three = as_cells(output_three, width_three)
    incoming_one = as_cells(upstream_one, width_one)
    incoming_two = as_cells(upstream_two, width_two)
    incoming_three = as_cells(upstream_three, width_three)
    framed_two = extend_next(incoming_two)
    framed_three = extend_next(incoming_three)
    spread_one, stride_grad_one = down_backward(saved_one, framed_two, stride_one_two)
    spread_two, stride_grad_two = down_backward(saved_two, framed_three, stride_two_three)
    half_one = pool_sum(incoming_one, 2)
    quarter_one = pool_sum(half_one, 2)
    eighth_one = pool_sum(quarter_one, 2)
    half_two = pool_sum(incoming_two, 2)
    quarter_two = pool_sum(half_two, 2)
    half_three = pool_sum(incoming_three, 2)
    pooled_one_two = half_one.astype(jnp.bfloat16)
    pooled_one_three = quarter_one.astype(jnp.bfloat16)
    pooled_one_four = eighth_one.astype(jnp.bfloat16)
    pooled_two_three = half_two.astype(jnp.bfloat16)
    pooled_two_four = quarter_two.astype(jnp.bfloat16)
    pooled_three_four = half_three.astype(jnp.bfloat16)
    delta_one = (incoming_one + spread_one).astype(jnp.bfloat16)
    delta_two = (incoming_two + project(pooled_one_two, mixer_two_one) + spread_two).astype(
        jnp.bfloat16
    )
    delta_three = (
        incoming_three
        + project(pooled_one_three, mixer_three_one)
        + project(pooled_two_three, mixer_three_two)
    ).astype(jnp.bfloat16)
    back_four = (
        project(pooled_one_four, mixer_four_one)
        + project(pooled_two_four, mixer_four_two)
        + project(pooled_three_four, mixer_four_three)
    )
    back_one, kernel_grad_one = conv_backward(cells_one, with_frame(delta_one), kernel_one)
    back_two, kernel_grad_two = conv_backward(cells_two, with_frame(delta_two), kernel_two)
    back_three, kernel_grad_three = conv_backward(
        cells_three, with_frame(delta_three), kernel_three
    )
    pieces = (
        kernel_grad_one,
        kernel_grad_two,
        kernel_grad_three,
        stride_grad_one,
        stride_grad_two,
        mixer_grad(saved_two, pooled_one_two),
        mixer_grad(saved_three, pooled_one_three),
        mixer_grad(cells_four, pooled_one_four),
        mixer_grad(saved_three, pooled_two_three),
        mixer_grad(cells_four, pooled_two_four),
        mixer_grad(cells_four, pooled_three_four),
    )
    flat = jnp.concatenate(
        [piece_grad.reshape(-1) for piece_grad in pieces]
        + [jnp.zeros((FLAT_ROWS * 128 - TOTAL,), jnp.float32)]
    ).reshape(FLAT_ROWS, 128)
    packed = pl.pallas_call(
        pack_shares,
        out_shape=jax.ShapeDtypeStruct((128 * WINDOW, 128), jnp.bfloat16),
        in_specs=[pl.BlockSpec(memory_space=pltpu.VMEM)],
        out_specs=pl.BlockSpec(memory_space=pltpu.VMEM),
        compiler_params=pltpu.CompilerParams(vmem_limit_bytes=32 * 1024 * 1024),
        name="pack_shares",
    )(flat)
    weight_grads = reduce_shares(packed)
    return (
        back_one.astype(jnp.bfloat16).reshape(feature_one.shape),
        back_two.astype(jnp.bfloat16).reshape(feature_two.shape),
        back_three.astype(jnp.bfloat16).reshape(feature_three.shape),
        back_four.astype(jnp.bfloat16).reshape(feature_four.shape),
        weight_grads,
    )


def solution(mesh):
    in_specs = (
        P(("branch", "row"), "col"),
        P(("branch", "row"), "col"),
        P(("branch", "row"), "col"),
        P(("branch", "row"), "col"),
        P(("branch", "row"), "col"),
        P(("branch", "row"), "col"),
        P(("branch", "row"), "col"),
        P(("branch", "row"), "col"),
        P(("branch", "row"), "col"),
        P(("branch", "row"), "col"),
        P(),
        P(),
        P(),
        P(),
        P(),
        P(),
        P(),
        P(),
        P(),
        P(),
        P(),
    )
    out_specs = (
        P(("branch", "row"), "col"),
        P(("branch", "row"), "col"),
        P(("branch", "row"), "col"),
        P(("branch", "row"), "col"),
        P(("row", "col")),
    )
    return jax.shard_map(local, mesh=mesh, in_specs=in_specs, out_specs=out_specs, check_vma=False)
```

```python
import jax
import jax.numpy as jnp
import numpy as np
from jax import lax
from jax.experimental import pallas as pl
from jax.experimental.pallas import tpu as pltpu
from jax.sharding import PartitionSpec as P

EPSILON = 1e-06
MESH = pl.DeviceIdType.MESH
TOTAL = 804096
SHARE = 6282
WINDOW = 64
FLAT_ROWS = 6296


def share_place(share):
    row, col = divmod(share, 8)
    core, z_hi, y = row % 2, (row // 2) % 2, row // 4
    half, quarter = divmod(col, 4)
    return ((core * 4 + y) * 4 + quarter) * 4 + z_hi * 2 + half


def pack_shares(flat_ref, packed_ref):
    for share in range(128):
        start = SHARE * share // 1024 * 8
        place = share_place(share) * WINDOW
        packed_ref[place : place + WINDOW, :] = flat_ref[start : start + WINDOW, :].astype(jnp.bfloat16)


def reduce_kernel(
    packed_ref,
    out_ref,
    from_core,
    sum_core,
    from_plane,
    sum_plane,
    from_line,
    share_buf,
    square_buf,
    from_near,
    near_buf,
    from_far,
    core_sems,
    plane_send,
    plane_recv,
    line_send,
    line_recv,
    share_send,
    share_recv,
    near_send,
    near_recv,
    far_send,
    far_recv,
):
    x = lax.axis_index("branch")
    row = lax.axis_index("row")
    col = lax.axis_index("col")
    core, z_hi, y = row % 2, (row // 2) % 2, row // 4
    z = z_hi * 8 + col
    partner = (x, row + 1 - 2 * core, col)

    def plane_peer(step):
        there = (x * 4 + y + step) % 16
        return there, (there // 4, (there % 4) * 4 + z_hi * 2 + core, col)

    def line_peer(step):
        there = (z + step) % 16
        return (x, y * 4 + (there // 8) * 2 + core, there % 8)

    def near_peer(step):
        there = (y * 2 + core + step) % 8
        return (x, (there // 2) * 4 + z_hi * 2 + there % 2, col)

    def greet(peer):
        pl.semaphore_signal(barrier, inc=1, device_id=peer, device_id_type=MESH)

    barrier = pltpu.get_barrier_semaphore()
    greet(partner)

    @pl.loop(1, 16)
    def _(step):
        greet(plane_peer(step)[1])
        greet(line_peer(step))

    @pl.loop(1, 8)
    def _(step):
        greet(near_peer(step))

    pl.semaphore_wait(barrier, 38)

    def remote(src, dst, send_sem, recv_sem, peer):
        return pltpu.make_async_remote_copy(
            src_ref=src, dst_ref=dst, send_sem=send_sem, recv_sem=recv_sem,
            device_id=peer, device_id_type=MESH,
        )

    half = 64 * WINDOW
    across = remote(
        packed_ref.at[pl.ds(pl.multiple_of((1 - core) * half, half), half)],
        from_core, core_sems.at[0], core_sems.at[1], partner,
    )
    across.start()
    across.wait()

    @pl.loop(0, 16)
    def _(block):
        start = pl.multiple_of(block * 256, 256)
        mine = packed_ref[pl.ds(pl.multiple_of(core * half, half) + start, 256), :]
        theirs = from_core[pl.ds(start, 256), :]
        sum_core[pl.ds(start, 256), :] = (mine.astype(jnp.float32) + theirs.astype(jnp.float32)).astype(jnp.bfloat16)

    def plane_copy(step):
        there, peer = plane_peer(step)
        place = (there % 4) * 4 + there // 4
        return remote(
            sum_core.at[pl.ds(pl.multiple_of(place * 256, 256), 256)],
            from_plane.at[step - 1], plane_send.at[step - 1], plane_recv.at[step - 1], peer,
        )

    @pl.loop(1, 16)
    def _(step):
        plane_copy(step).start()

    @pl.loop(1, 16)
    def _(step):
        plane_copy(step).wait()

    @pl.loop(0, 4)
    def _(block):
        start = pl.multiple_of(block * WINDOW, WINDOW)
        own = pl.multiple_of((y * 4 + x) * 256 + start, WINDOW)
        total = sum_core[pl.ds(own, WINDOW), :].astype(jnp.float32)
        for step in range(15):
            total = total + from_plane[step, pl.ds(start, WINDOW), :].astype(jnp.float32)
        sum_plane[pl.ds(start, WINDOW), :] = total.astype(jnp.bfloat16)

    def line_copy(block):
        target = (block // 2) * 8 + (block % 2) * 4 + x
        step = (z - target + 16) % 16
        slot = (step + 15) % 16
        return step, remote(
            sum_plane.at[pl.ds(pl.multiple_of(block * WINDOW, WINDOW), WINDOW)],
            from_line.at[slot], line_send.at[block], line_recv.at[slot],
            (x, y * 4 + (target // 8) * 2 + core, target % 8),
        )

    for block in range(4):
        step, copy = line_copy(block)

        @pl.when(step != 0)
        def _():
            copy.start()

    owner_x = col % 4
    owner = owner_x == x

    def share_copy(step):
        return remote(
            share_buf, share_buf, share_send.at[step - 1], share_recv.at[0],
            ((x + step) % 4, row, col),
        )

    @pl.when(owner)
    def _():
        @pl.loop(0, 15)
        def _(slot):
            remote(
                sum_plane.at[pl.ds(0, WINDOW)], from_line.at[slot], line_send.at[0], line_recv.at[slot], partner
            ).wait_recv()

        own = pl.multiple_of((z_hi * 2 + col // 4) * WINDOW, WINDOW)
        total = sum_plane[pl.ds(own, WINDOW), :].astype(jnp.float32)
        for slot in range(15):
            total = total + from_line[slot].astype(jnp.float32)
        share_buf[...] = total
        for step in range(1, 4):
            share_copy(step).start()

    @pl.when(jnp.logical_not(owner))
    def _():
        share_copy(1).wait_recv()

    offset = (SHARE * (row * 8 + col)) % 1024
    place = lax.broadcasted_iota(jnp.int32, (WINDOW, 128), 0) * 128 + lax.broadcasted_iota(jnp.int32, (WINDOW, 128), 1)
    inside = jnp.logical_and(place >= offset, place < offset + SHARE)
    share = share_buf[...]
    squares = jnp.where(inside, share * share, 0.0)
    square_buf[...] = squares.reshape(8, 8, 128).sum(axis=0)

    def near_copy(step):
        return remote(
            square_buf, from_near.at[step - 1], near_send.at[step - 1], near_recv.at[step - 1], near_peer(step)
        )

    @pl.loop(1, 8)
    def _(step):
        near_copy(step).start()

    @pl.loop(1, 8)
    def _(step):
        near_copy(step).wait()

    near_buf[...] = square_buf[...] + from_near[...].sum(axis=0)

    def far_copy(step):
        return remote(
            near_buf, from_far.at[step - 1], far_send.at[step - 1], far_recv.at[step - 1], line_peer(step)
        )

    @pl.loop(1, 16)
    def _(step):
        far_copy(step).start()

    @pl.loop(1, 16)
    def _(step):
        far_copy(step).wait()

    total_squares = jnp.sum(near_buf[...] + from_far[...].sum(axis=0), keepdims=True)
    spread_rms = jnp.sqrt(total_squares / TOTAL + EPSILON)
    out_ref[...] = share_buf[...] * jnp.minimum(jnp.float32(1.0), 1.0 / spread_rms)

    for block in range(4):
        step, copy = line_copy(block)

        @pl.when(step != 0)
        def _():
            copy.wait_send()

    @pl.when(owner)
    def _():
        for step in range(1, 4):
            share_copy(step).wait_send()


def reduce_shares(packed):
    dma = pltpu.SemaphoreType.DMA
    window = pl.pallas_call(
        reduce_kernel,
        out_shape=jax.ShapeDtypeStruct((WINDOW, 128), jnp.float32),
        in_specs=[pl.BlockSpec(memory_space=pltpu.VMEM)],
        out_specs=pl.BlockSpec(memory_space=pltpu.VMEM),
        scratch_shapes=[
            pltpu.VMEM((64 * WINDOW, 128), jnp.bfloat16),
            pltpu.VMEM((64 * WINDOW, 128), jnp.bfloat16),
            pltpu.VMEM((15, 4 * WINDOW, 128), jnp.bfloat16),
            pltpu.VMEM((4 * WINDOW, 128), jnp.bfloat16),
            pltpu.VMEM((15, WINDOW, 128), jnp.bfloat16),
            pltpu.VMEM((WINDOW, 128), jnp.float32),
            pltpu.VMEM((8, 128), jnp.float32),
            pltpu.VMEM((7, 8, 128), jnp.float32),
            pltpu.VMEM((8, 128), jnp.float32),
            pltpu.VMEM((15, 8, 128), jnp.float32),
            dma((2,)),
            dma((15,)),
            dma((15,)),
            dma((4,)),
            dma((15,)),
            dma((3,)),
            dma((1,)),
            dma((7,)),
            dma((7,)),
            dma((15,)),
            dma((15,)),
        ],
        compiler_params=pltpu.CompilerParams(
            collective_id=0, has_side_effects=True, vmem_limit_bytes=32 * 1024 * 1024
        ),
        name="reduce_shares",
    )(packed)
    offset = (SHARE * lax.axis_index(("row", "col"))) % 1024
    return lax.dynamic_slice(window.reshape(WINDOW * 128), (offset,), (SHARE,))


GROUP = 384
CELLS = 24
PIECES = (
    (48, 0, 0, 432), (96, 162, 0, 864), (192, 810, 0, 1728), (96, 3402, 864, 432), (192, 3726, 1728, 864),
    (48, 5022, 432, 96), (48, 5058, 528, 192), (48, 5130, 720, 384), (96, 5274, 1296, 192),
    (96, 5418, 1488, 384), (192, 5706, 2592, 384),
)
BF16 = jnp.bfloat16
F32 = jnp.float32


def dot(left, right, left_dim=1, right_dim=0):
    return lax.dot_general(left, right, (((left_dim,), (right_dim,)), ((), ())), preferred_element_type=F32)


def lanes_of(rows, lanes):
    return lax.broadcasted_iota(jnp.int32, (rows, lanes), 1)


def halo_kernel(u1_ref, u2_ref, u3_ref, rows_ref, sides_ref, corners_ref, send_rows, send_sides, send_corners,
                recv_rows, recv_sides, recv_corners, send_sems, recv_sems):
    x = lax.axis_index("branch")
    row = lax.axis_index("row")
    col = lax.axis_index("col")
    line = x * 16 + row

    def peer(down, right):
        there = (line + down + 64) % 64
        return (there // 16, there % 16, (col + right + 8) % 8)

    routes = (
        (0, 1, 0, send_rows.at[0], recv_rows.at[0]),
        (1, -1, 0, send_rows.at[1], recv_rows.at[1]),
        (2, 0, 1, send_sides.at[0], recv_sides.at[0]),
        (3, 0, -1, send_sides.at[1], recv_sides.at[1]),
        (4, 1, 1, send_corners.at[0], recv_corners.at[0]),
        (5, 1, -1, send_corners.at[1], recv_corners.at[1]),
        (6, -1, 1, send_corners.at[2], recv_corners.at[2]),
        (7, -1, -1, send_corners.at[3], recv_corners.at[3]),
    )
    barrier = pltpu.get_barrier_semaphore()
    for slot, down, right, src, dst in routes:
        pl.semaphore_signal(barrier, inc=1, device_id=peer(down, right), device_id_type=MESH)

    u1 = u1_ref[...].astype(F32)
    u2 = u2_ref[...].astype(F32)
    u3 = u3_ref[...].astype(F32)
    wide = CELLS * GROUP
    last = wide - GROUP
    blank = jnp.zeros((1, wide), F32)
    bottom = jnp.concatenate([u1[4:8], u2[2:4], u3[1:2], blank], axis=0)
    top = jnp.concatenate([u2[0:2], u3[0:1], blank, u1[0:4]], axis=0)
    empty = jnp.zeros((8, GROUP), F32)
    for index, part in enumerate((bottom, top)):
        send_rows[index] = jnp.concatenate([part[:, : wide // 2], part[:, wide // 2 :]], axis=0).astype(BF16)
        send_corners[2 * index] = jnp.concatenate([part[:, last:], empty], axis=0).astype(BF16)
        send_corners[2 * index + 1] = jnp.concatenate([part[:, :GROUP], empty], axis=0).astype(BF16)
    for index, start in enumerate((last, 0)):
        send_sides[index] = jnp.concatenate(
            [u1[:, start : start + GROUP], u2[:, start : start + GROUP], u3[:, start : start + GROUP], empty[:2]], axis=0
        ).astype(BF16)

    pl.semaphore_wait(barrier, 8)

    def copy(route):
        slot, down, right, src, dst = route
        return pltpu.make_async_remote_copy(
            src_ref=src, dst_ref=dst, send_sem=send_sems.at[slot], recv_sem=recv_sems.at[slot],
            device_id=peer(down, right), device_id_type=MESH,
        )

    for route in routes:
        copy(route).start()
    for route in routes:
        copy(route).wait()

    above = jnp.where(line > 0, 1.0, 0.0)
    below = jnp.where(line < 63, 1.0, 0.0)
    left = jnp.where(col > 0, 1.0, 0.0)
    right = jnp.where(col < 7, 1.0, 0.0)
    rows_ref[0] = (recv_rows[0].astype(F32) * above).astype(BF16)
    rows_ref[1] = (recv_rows[1].astype(F32) * below).astype(BF16)
    sides_ref[0] = (recv_sides[0].astype(F32) * left).astype(BF16)
    sides_ref[1] = (recv_sides[1].astype(F32) * right).astype(BF16)
    corners_ref[0] = (recv_corners[0].astype(F32) * (above * left)).astype(BF16)
    corners_ref[1] = (recv_corners[1].astype(F32) * (above * right)).astype(BF16)
    corners_ref[2] = (recv_corners[2].astype(F32) * (below * left)).astype(BF16)
    corners_ref[3] = (recv_corners[3].astype(F32) * (below * right)).astype(BF16)


def exchange_halo(u1, u2, u3):
    shapes = ((2, 16, CELLS * GROUP // 2), (2, 16, GROUP), (4, 16, GROUP))
    whole = pl.BlockSpec(memory_space=pltpu.VMEM)
    return pl.pallas_call(
        halo_kernel,
        out_shape=[jax.ShapeDtypeStruct(shape, BF16) for shape in shapes],
        in_specs=[whole] * 3,
        out_specs=[whole] * 3,
        scratch_shapes=[pltpu.VMEM(shape, BF16) for shape in shapes + shapes]
        + [pltpu.SemaphoreType.DMA((8,)), pltpu.SemaphoreType.DMA((8,))],
        compiler_params=pltpu.CompilerParams(
            collective_id=1, has_side_effects=True, vmem_limit_bytes=32 * 1024 * 1024
        ),
        name="exchange_halo",
    )(u1, u2, u3)


def banded(weights, repeat, width, rows, blocks, dst):
    wide = dot(weights, repeat)
    lane = lanes_of(rows, repeat.shape[1])
    for block, pieces in enumerate(blocks):
        value = jnp.zeros((rows, repeat.shape[1]), F32)
        for tap, start in pieces:
            inside = jnp.logical_and(lane >= start, lane < start + width)
            value = jnp.where(inside, wide[tap * rows : (tap + 1) * rows], value)
        dst[block * rows : (block + 1) * rows, :] = value.astype(BF16)


def conv_blocks(tap_row, width, base):
    return [[(tap_row * 3 + tap, base + width * (n + 1 - tap)) for tap in range(3)] for n in range(GROUP // width)]


def down_blocks(tap_row, width):
    blocks = []
    for j in range(2 * (GROUP // width)):
        if j % 2 == 0:
            blocks.append([(tap_row * 3 + 1, width * (j // 2))])
        else:
            blocks.append([(tap_row * 3 + 2, width * (j // 2)), (tap_row * 3, width * (j // 2 + 1))])
    return blocks


def mixer_blocks(width, count):
    return [[(0, width * j)] for j in range(count)]


def window(value, start, width):
    first, end = start // 128, -(-(start + width) // 128)
    part = value[:, first * 128 : end * 128]
    shift = start - first * 128
    if shift:
        part = pltpu.roll(part, (end - first) * 128 - shift, 1)
    return part[:, : -(-width // 128) * 128]


def place(src, flat, width, flat_base, src_base, count):
    stride = GROUP // width
    rows = count // stride
    lane = lanes_of(rows, 128)
    held = {}
    for tile in range(3):
        value = None
        for j in range(stride):
            for part in range(-(-width // 128)):
                low = max(width * j + 128 * part, 128 * tile)
                high = min(width * j + min(width, 128 * part + 128), 128 * tile + 128)
                if low >= high:
                    continue
                if (j, part) not in held:
                    held[j, part] = src[part, pl.ds(src_base + j, rows, stride=stride), :]
                piece = held[j, part]
                shift = (width * j + 128 * part - 128 * tile) % 128
                if shift:
                    piece = pltpu.roll(piece, shift, 1)
                value = piece if value is None else jnp.where(lane >= low - 128 * tile, piece, value)
        flat[pl.ds(flat_base + tile, rows, stride=3), :] = value


def backward_kernel(
    rows_ref, sides_ref, corners_ref, f1_ref, f2_ref, f3_ref, f4_ref, o1_ref, o2_ref, o3_ref, u1_ref, u2_ref, u3_ref,
    k1_ref, k2_ref, k3_ref, s12_ref, s23_ref, m21_ref, m31_ref, m41_ref, m32_ref, m42_ref, m43_ref,
    rep1_ref, rep2_ref, rep3_ref, rep12_ref, rep23_ref, rep48_ref, rep96_ref, pool1_ref, pool2_ref, pool3_ref,
    g1_ref, g2_ref, g3_ref, g4_ref, packed_ref,
    ext1, ext2, ext3, v1, v2, v3, del1, del2, del3, pad_f2, pad_f3, pad_o1, pad_o2, pad_o3, rows_f4,
    band1, band2, band3, band12, band23, band21, band31, band32, res2, res3, w48, w96, w192, flat,
):
    half = CELLS // 2

    def lanes(g):
        return slice(GROUP * g, GROUP * (g + 1))

    u1, u2, u3 = (ref[...].astype(F32) for ref in (u1_ref, u2_ref, u3_ref))
    above, below = rows_ref[0].astype(F32), rows_ref[1].astype(F32)
    sides = [sides_ref[i].astype(F32) for i in range(2)]
    corners = [corners_ref[i].astype(F32) for i in range(4)]
    for g in range(CELLS + 2):
        if g == 0 or g == CELLS + 1:
            side = sides[0 if g == 0 else 1]
            mid = side[0:8], side[8:12], side[12:14]
            up = corners[0 if g == 0 else 1]
            down = corners[2 if g == 0 else 3]
        else:
            at = lanes(g - 1)
            mid = u1[:, at], u2[:, at], u3[:, at]
            row0 = 8 * ((g - 1) // half)
            there = lanes((g - 1) % half)
            up, down = above[row0 : row0 + 8, there], below[row0 : row0 + 8, there]
        ext1[g, 0:4, :] = up[0:4]
        ext1[g, 4:12, :] = mid[0]
        ext1[g, 12:16, :] = down[4:8]
        ext2[8 * g : 8 * g + 2, :] = up[4:6]
        ext2[8 * g + 2 : 8 * g + 6, :] = mid[1]
        ext2[8 * g + 6 : 8 * g + 8, :] = down[0:2]
        ext3[4 * g : 4 * g + 1, :] = up[6:7]
        ext3[4 * g + 1 : 4 * g + 3, :] = mid[2]
        ext3[4 * g + 3 : 4 * g + 4, :] = down[2:3]
    ext2[8 * (CELLS + 2) :, :] = jnp.zeros((8, GROUP), F32)
    ext3[4 * (CELLS + 2) :, :] = jnp.zeros((8, GROUP), F32)

    for ref in (pad_f2, pad_f3, pad_o1, pad_o2, pad_o3):
        ref[...] = jnp.zeros_like(ref)
    f2, f3, o1, o2, o3, f4 = (ref[...].astype(F32) for ref in (f2_ref, f3_ref, o1_ref, o2_ref, o3_ref, f4_ref))
    for g in range(CELLS):
        at = lanes(g)
        pad_f2[8 * g + 2 : 8 * g + 6, :] = f2[:, at]
        pad_f3[4 * g + 1 : 4 * g + 3, :] = f3[:, at]
        for tile in range(3):
            part = slice(GROUP * g + 128 * tile, GROUP * g + 128 * tile + 128)
            pad_o1[tile, 16 * g + 4 : 16 * g + 12, :] = o1[:, part]
            pad_o2[tile, 8 * g + 2 : 8 * g + 6, :] = o2[:, part]
        pad_o3[4 * g + 1 : 4 * g + 3, :] = o3[:, at]
        rows_f4[g : g + 1, :] = f4[:, at]

    for a in range(3):
        banded(k1_ref[...], rep1_ref[...], 48, 48, conv_blocks(a, 48, 128), band1.at[a])
        banded(k2_ref[...], rep2_ref[...], 96, 96, conv_blocks(a, 96, 128), band2.at[a])
        banded(k3_ref[...], rep3_ref[...], 192, 192, conv_blocks(a, 192, 256), band3.at[a])
        banded(s12_ref[...], rep12_ref[...], 96, 48, down_blocks(a, 96), band12.at[a])
        banded(s23_ref[...], rep23_ref[...], 192, 96, down_blocks(a, 192), band23.at[a])
    banded(m21_ref[...], rep48_ref[...], 48, 96, mixer_blocks(48, 4), band21)
    banded(m31_ref[...], rep48_ref[:, :128], 48, 192, mixer_blocks(48, 2), band31)
    banded(m32_ref[...], rep96_ref[...], 96, 192, mixer_blocks(96, 2), band32)

    tall1, tall2, tall3 = 16 * (CELLS + 2), 8 * (CELLS + 2), 4 * (CELLS + 2)
    def tiled_store(ref, value, rows=slice(None)):
        for tile in range(value.shape[1] // 128):
            ref[tile, rows, :] = value[:, 128 * tile : 128 * tile + 128]

    def strided(ref, tiles, start, count, stride):
        parts = [ref[tile, pl.ds(start, count, stride=stride), :] for tile in tiles]
        return parts[0] if len(parts) == 1 else jnp.concatenate(parts, axis=1)

    tiled_store(v1, dot(ext1[...].reshape(tall1, GROUP).astype(BF16), pool1_ref[...]))
    tiled_store(v2, dot(ext2[0:tall2, :].astype(BF16), pool2_ref[...]))
    tiled_store(v3, dot(ext3[0:tall3, :].astype(BF16), pool3_ref[...]))

    def strided_sum(ref, picks, count, stride, tiles):
        total = None
        for pick in picks:
            piece = strided(ref, tiles, pick, count, stride)
            total = piece if total is None else total + piece
        return total.astype(BF16)

    p12 = strided_sum(v1, range(2), tall2, 2, (0, 1))
    p13 = strided_sum(v1, range(4), tall3, 4, (2,))
    p14 = strided_sum(v1, range(16 + 4, 16 + 12), CELLS, 16, (3,))
    p23 = strided_sum(v2, range(2), tall3, 2, (0, 1))
    p24 = strided_sum(v2, range(8 + 2, 8 + 6), CELLS, 8, (2,))
    p34 = strided_sum(v3, range(4 + 1, 4 + 3), CELLS, 4, (0, 1))

    line = lax.axis_index("branch") * 16 + lax.axis_index("row")
    col = lax.axis_index("col")
    top, bottom = jnp.where(line > 0, 1.0, 0.0), jnp.where(line < 63, 1.0, 0.0)
    left, right = jnp.where(col > 0, 1.0, 0.0), jnp.where(col < 7, 1.0, 0.0)

    def rim_mask(rows, inner):
        place_row = lax.broadcasted_iota(jnp.int32, (CELLS + 2, rows, GROUP), 1)
        place_col = lax.broadcasted_iota(jnp.int32, (CELLS + 2, rows, GROUP), 0)
        start, end = (rows - inner) // 2, (rows + inner) // 2
        by_row = jnp.where(place_row == start - 1, top, jnp.where(place_row == end, bottom, 1.0))
        by_row = jnp.where(jnp.logical_and(place_row >= start - 1, place_row <= end), by_row, 0.0)
        by_col = jnp.where(place_col == 0, left, jnp.where(place_col == CELLS + 1, right, 1.0))
        return by_row * by_col

    def rolled(value):
        return pltpu.roll(value, value.shape[0] - 1, 0)

    x2 = jnp.concatenate([ext2[0:tall2, :], ext2[8 : tall2 + 8, 0:128]], axis=1).astype(BF16)
    tiled_store(v1, dot(x2, band12[1], 1, 1), pl.ds(0, tall2, stride=2))
    tiled_store(v1, dot(x2, band12[2], 1, 1) + rolled(dot(x2, band12[0], 1, 1)), pl.ds(1, tall2, stride=2))
    spread1 = jnp.concatenate([v1[tile] for tile in range(3)], axis=1)
    delta1 = ext1[...] + spread1.reshape(CELLS + 2, 16, GROUP)
    del1[...] = (delta1 * rim_mask(16, 8)).astype(BF16).astype(F32)

    x3 = jnp.concatenate([ext3[0:tall3, :], ext3[4 : tall3 + 4, 0:256]], axis=1).astype(BF16)
    tiled_store(v2, dot(x3, band23[1], 1, 1), pl.ds(0, tall3, stride=2))
    tiled_store(v2, dot(x3, band23[2], 1, 1) + rolled(dot(x3, band23[0], 1, 1)), pl.ds(1, tall3, stride=2))
    spread2 = jnp.concatenate([v2[tile] for tile in range(3)], axis=1)
    delta2 = ext2[0:tall2, :] + dot(p12, band21[...], 1, 1) + spread2
    del2[8 : 8 + tall2, :] = (delta2 * rim_mask(8, 4).reshape(tall2, GROUP)).astype(BF16).astype(F32)

    delta3 = ext3[0:tall3, :] + dot(p13, band31[...], 1, 1) + dot(p23, band32[...], 1, 1)
    place_row = lax.broadcasted_iota(jnp.int32, (tall3, GROUP), 0)
    in_group = jnp.bitwise_and(place_row, 3)
    by_row = jnp.where(in_group == 0, top, jnp.where(in_group == 3, bottom, 1.0))
    by_col = jnp.where(place_row < 4, left, jnp.where(place_row >= 4 * (CELLS + 1), right, 1.0))
    del3[8 : 8 + tall3, :] = (delta3 * (by_row * by_col)).astype(BF16).astype(F32)
    for ref in (del2, del3):
        ref[0:8, :] = jnp.zeros((8, GROUP), F32)
        ref[ref.shape[0] - 8 :, :] = jnp.zeros((8, GROUP), F32)

    def fold(grads, width, base, a, dst):
        total = None
        for n in range(GROUP // width):
            part = window(grads[n * width : (n + 1) * width, :], base + width * (n - 1), 3 * width)
            total = part if total is None else total + part
        for tap in range(3):
            start = (a * 3 + tap) * width
            tiled_store(dst, window(total, width * (2 - tap), width), slice(start, start + width))

    f1 = f1_ref[...]
    f1 = jnp.concatenate([f1[:, lanes(g)].astype(F32) for g in range(CELLS)], axis=0).astype(BF16)
    back = None
    for a in range(3):
        at = slice(5 - a, 13 - a)
        x1 = jnp.concatenate(
            [del1[0:CELLS, at, 256:GROUP], del1[1 : CELLS + 1, at, :], del1[2 : CELLS + 2, at, 0:128]], axis=2
        ).reshape(8 * CELLS, 640).astype(BF16)
        part = dot(x1, band1[a], 1, 1)
        back = part if back is None else back + part
        fold(dot(f1, x1, 0, 0), 48, 128, a, w48)
    for g in range(CELLS):
        g1_ref[:, lanes(g)] = back[8 * g : 8 * g + 8].astype(BF16)

    f2x = pad_f2[...].astype(BF16)
    back = None
    for a in range(3):
        at = 8 + 1 - a
        n = 8 * CELLS
        x2d = jnp.concatenate(
            [del2[at : at + n, 256:GROUP], del2[at + 8 : at + 8 + n, :], del2[at + 16 : at + 16 + n, 0:128]], axis=1
        ).astype(BF16)
        part = dot(x2d, band2[a], 1, 1)
        back = part if back is None else back + part
        fold(dot(f2x, x2d, 0, 0), 96, 128, a, w96)
    res2[...] = back
    for g in range(CELLS):
        g2_ref[:, lanes(g)] = res2[8 * g + 2 : 8 * g + 6, :].astype(BF16)

    f3x = pad_f3[...].astype(BF16)
    back = None
    for a in range(3):
        at = 8 + 1 - a
        n = 4 * CELLS
        x3d = jnp.concatenate(
            [del3[at : at + n, 128:GROUP], del3[at + 4 : at + 4 + n, :], del3[at + 8 : at + 8 + n, 0:256]], axis=1
        ).astype(BF16)
        part = dot(x3d, band3[a], 1, 1)
        back = part if back is None else back + part
        fold(dot(f3x, x3d, 0, 0), 192, 256, a, w192)
    res3[...] = back
    for g in range(CELLS):
        g3_ref[:, lanes(g)] = res3[4 * g + 1 : 4 * g + 3, :].astype(BF16)

    def fold_down(grads, width, rows, a, base, dst):
        for b in range(3):
            total = None
            for j in range(1 if b != 1 else 0, 2 * (GROUP // width), 2):
                p = (j + 1 - b) // 2
                part = window(grads[j * rows : (j + 1) * rows, :], width * p, width)
                total = part if total is None else total + part
            start = base + (a * 3 + b) * rows
            tiled_store(dst, total, slice(start, start + rows))

    def down_grads(saved, ext, skip, count, head, width, rows, base, dst):
        even = strided(saved, range(3), 0, count, 2).astype(BF16)
        odd = strided(saved, range(3), 1, count, 2).astype(BF16)
        for a in range(3):
            at = skip + (1 if a == 0 else 0)
            xs = jnp.concatenate(
                [ext[at : at + count, :], ext[at + skip : at + skip + count, 0:head]], axis=1
            ).astype(BF16)
            fold_down(dot(even if a == 1 else odd, xs, 0, 0), width, rows, a, base, dst)

    down_grads(pad_o1, ext2, 8, 8 * CELLS, 128, 96, 48, 864, w96)
    down_grads(pad_o2, ext3, 4, 4 * CELLS, 256, 192, 96, 1728, w192)

    def fold_mixer(grads, width, rows, base, dst):
        total = None
        for j in range(GROUP // rows):
            part = window(grads[j * rows : (j + 1) * rows, :], width * j, width)
            total = part if total is None else total + part
        tiled_store(dst, total, slice(base, base + rows))

    o2x = jnp.concatenate([pad_o2[tile] for tile in range(3)], axis=1).astype(BF16)
    o3x = pad_o3[...].astype(BF16)
    f4x = rows_f4[...].astype(BF16)
    inner2, inner3 = slice(8, 8 + 8 * CELLS), slice(4, 4 + 4 * CELLS)
    fold_mixer(dot(o2x, p12[inner2], 0, 0), 48, 96, 432, w48)
    fold_mixer(dot(o3x, p13[inner3], 0, 0), 48, 192, 528, w48)
    fold_mixer(dot(f4x, p14, 0, 0), 48, 384, 720, w48)
    fold_mixer(dot(o3x, p23[inner3], 0, 0), 96, 192, 1296, w96)
    fold_mixer(dot(f4x, p24, 0, 0), 96, 384, 1488, w96)
    fold_mixer(dot(f4x, p34, 0, 0), 192, 384, 2592, w192)
    back4 = (
        dot(p14[:, 0:48], m41_ref[...], 1, 1) + dot(p24[:, 0:96], m42_ref[...], 1, 1) + dot(p34[:, 0:192], m43_ref[...], 1, 1)
    )
    for g in range(CELLS):
        g4_ref[:, lanes(g)] = back4[g : g + 1].astype(BF16)

    for width, flat_base, src_base, count in PIECES:
        place({48: w48, 96: w96, 192: w192}[width], flat, width, flat_base, src_base, count)
    flat[6282:FLAT_ROWS, :] = jnp.zeros((FLAT_ROWS - 6282, 128), F32)
    pack_shares(flat, packed_ref)


def repeats(width, lanes, base=0):
    lane = np.arange(lanes)[None, :]
    return ((lane - base) % width == np.arange(width)[:, None]).astype(np.float32)


def pools(width, factors, parts):
    blocks = []
    for factor, lanes in zip(factors, parts):
        block = np.zeros((GROUP, lanes), np.float32)
        for lane in range(GROUP):
            block[lane, lane // (width * factor) * width + lane % width] = 1.0
        blocks.append(block)
    return np.concatenate(blocks, axis=1)


def local(f1, f2, f3, f4, o1, o2, o3, u1, u2, u3, k1, k2, k3, s12, s23, m21, m31, m41, m32, m42, m43):
    rows, sides, corners = exchange_halo(u1, u2, u3)
    constants = [
        jnp.asarray(value, BF16)
        for value in (
            repeats(48, 640, 128), repeats(96, 640, 128), repeats(192, 896, 256), repeats(96, 512), repeats(192, 640),
            repeats(48, 256), repeats(96, 256),
            pools(48, (2, 4, 8), (256, 128, 128)), pools(96, (2, 4), (256, 128)), pools(192, (2,), (256,)),
        )
    ]
    whole = pl.BlockSpec(memory_space=pltpu.VMEM)
    inputs = [
        rows, sides, corners, f1, f2, f3, f4, o1, o2, o3, u1, u2, u3,
        k1.reshape(432, 48), k2.reshape(864, 96), k3.reshape(1728, 192), s12.reshape(432, 96), s23.reshape(864, 192),
        m21, m31, m41, m32, m42, m43,
    ] + constants

    def f32(*shape):
        return pltpu.VMEM(shape, F32)

    def bf16(*shape):
        return pltpu.VMEM(shape, BF16)

    ext = CELLS + 2
    grad_one, grad_two, grad_three, grad_four, packed = pl.pallas_call(
        backward_kernel,
        out_shape=[jax.ShapeDtypeStruct(value.shape, BF16) for value in (f1, f2, f3, f4)]
        + [jax.ShapeDtypeStruct((128 * WINDOW, 128), BF16)],
        in_specs=[whole] * len(inputs),
        out_specs=[whole] * 5,
        scratch_shapes=[
            f32(ext, 16, GROUP), f32(8 * ext + 8, GROUP), f32(4 * ext + 8, GROUP),
            f32(4, 16 * ext, 128), f32(3, 8 * ext, 128), f32(2, 4 * ext, 128),
            f32(ext, 16, GROUP), f32(8 * ext + 16, GROUP), f32(4 * ext + 16, GROUP),
            f32(8 * CELLS, GROUP), f32(4 * CELLS, GROUP), f32(3, 16 * CELLS, 128), f32(3, 8 * CELLS, 128),
            f32(4 * CELLS, GROUP), f32(CELLS, GROUP),
            bf16(3, GROUP, 640), bf16(3, GROUP, 640), bf16(3, GROUP, 896), bf16(3, GROUP, 512), bf16(3, GROUP, 640),
            bf16(GROUP, 256), bf16(GROUP, 128), bf16(GROUP, 256),
            f32(8 * CELLS, GROUP), f32(4 * CELLS, GROUP),
            f32(1, 1104, 128), f32(1, 1872, 128), f32(2, 2976, 128), f32(FLAT_ROWS, 128),
        ],
        compiler_params=pltpu.CompilerParams(vmem_limit_bytes=56 * 1024 * 1024),
        name="backward",
    )(*inputs)
    return grad_one, grad_two, grad_three, grad_four, reduce_shares(packed)


def solution(mesh):
    in_specs = (
        P(("branch", "row"), "col"),
        P(("branch", "row"), "col"),
        P(("branch", "row"), "col"),
        P(("branch", "row"), "col"),
        P(("branch", "row"), "col"),
        P(("branch", "row"), "col"),
        P(("branch", "row"), "col"),
        P(("branch", "row"), "col"),
        P(("branch", "row"), "col"),
        P(("branch", "row"), "col"),
        P(),
        P(),
        P(),
        P(),
        P(),
        P(),
        P(),
        P(),
        P(),
        P(),
        P(),
    )
    out_specs = (
        P(("branch", "row"), "col"),
        P(("branch", "row"), "col"),
        P(("branch", "row"), "col"),
        P(("branch", "row"), "col"),
        P(("row", "col")),
    )
    return jax.shard_map(local, mesh=mesh, in_specs=in_specs, out_specs=out_specs, check_vma=False)
```

```python
import jax
import jax.numpy as jnp
import numpy as np
from jax import lax
from jax.experimental import pallas as pl
from jax.experimental.pallas import tpu as pltpu
from jax.sharding import PartitionSpec as P

EPSILON = 1e-06
MESH = pl.DeviceIdType.MESH
TOTAL = 804096
SHARE = 6282
WINDOW = 64
FLAT_ROWS = 6296


def share_place(share):
    row, col = divmod(share, 8)
    core, z_hi, y = row % 2, (row // 2) % 2, row // 4
    half, quarter = divmod(col, 4)
    return ((core * 4 + y) * 4 + quarter) * 4 + z_hi * 2 + half


def pack_shares(flat_ref, packed_ref):
    for share in range(128):
        start = SHARE * share // 1024 * 8
        place = share_place(share) * WINDOW
        packed_ref[place : place + WINDOW, :] = flat_ref[start : start + WINDOW, :].astype(jnp.bfloat16)


def reduce_stages(
    packed_ref,
    out_ref,
    from_core,
    sum_core,
    from_plane,
    sum_plane,
    from_line,
    share_buf,
    square_buf,
    from_near,
    near_buf,
    from_far,
    core_sems,
    plane_send,
    plane_recv,
    line_send,
    line_recv,
    share_send,
    share_recv,
    near_send,
    near_recv,
    far_send,
    far_recv,
):
    x = lax.axis_index("branch")
    row = lax.axis_index("row")
    col = lax.axis_index("col")
    core, z_hi, y = row % 2, (row // 2) % 2, row // 4
    z = z_hi * 8 + col
    partner = (x, row + 1 - 2 * core, col)

    def plane_peer(step):
        there = (x * 4 + y + step) % 16
        return there, (there // 4, (there % 4) * 4 + z_hi * 2 + core, col)

    def line_peer(step):
        there = (z + step) % 16
        return (x, y * 4 + (there // 8) * 2 + core, there % 8)

    def near_peer(step):
        there = (y * 2 + core + step) % 8
        return (x, (there // 2) * 4 + z_hi * 2 + there % 2, col)

    def remote(src, dst, send_sem, recv_sem, peer):
        return pltpu.make_async_remote_copy(
            src_ref=src, dst_ref=dst, send_sem=send_sem, recv_sem=recv_sem,
            device_id=peer, device_id_type=MESH,
        )

    half = 64 * WINDOW
    across = remote(
        packed_ref.at[pl.ds(pl.multiple_of((1 - core) * half, half), half)],
        from_core, core_sems.at[0], core_sems.at[1], partner,
    )
    across.start()
    across.wait()

    @pl.loop(0, 16)
    def _(block):
        start = pl.multiple_of(block * 256, 256)
        mine = packed_ref[pl.ds(pl.multiple_of(core * half, half) + start, 256), :]
        theirs = from_core[pl.ds(start, 256), :]
        sum_core[pl.ds(start, 256), :] = (mine.astype(jnp.float32) + theirs.astype(jnp.float32)).astype(jnp.bfloat16)

    def plane_copy(step):
        there, peer = plane_peer(step)
        place = (there % 4) * 4 + there // 4
        return remote(
            sum_core.at[pl.ds(pl.multiple_of(place * 256, 256), 256)],
            from_plane.at[step - 1], plane_send.at[step - 1], plane_recv.at[step - 1], peer,
        )

    @pl.loop(1, 16)
    def _(step):
        plane_copy(step).start()

    @pl.loop(1, 16)
    def _(step):
        plane_copy(step).wait()

    @pl.loop(0, 4)
    def _(block):
        start = pl.multiple_of(block * WINDOW, WINDOW)
        own = pl.multiple_of((y * 4 + x) * 256 + start, WINDOW)
        total = sum_core[pl.ds(own, WINDOW), :].astype(jnp.float32)
        for step in range(15):
            total = total + from_plane[step, pl.ds(start, WINDOW), :].astype(jnp.float32)
        sum_plane[pl.ds(start, WINDOW), :] = total.astype(jnp.bfloat16)

    def line_copy(block):
        target = (block // 2) * 8 + (block % 2) * 4 + x
        step = (z - target + 16) % 16
        slot = (step + 15) % 16
        return step, remote(
            sum_plane.at[pl.ds(pl.multiple_of(block * WINDOW, WINDOW), WINDOW)],
            from_line.at[slot], line_send.at[block], line_recv.at[slot],
            (x, y * 4 + (target // 8) * 2 + core, target % 8),
        )

    for block in range(4):
        step, copy = line_copy(block)

        @pl.when(step != 0)
        def _():
            copy.start()

    owner_x = col % 4
    owner = owner_x == x

    def share_copy(step):
        return remote(
            share_buf, share_buf, share_send.at[step - 1], share_recv.at[0],
            ((x + step) % 4, row, col),
        )

    @pl.when(owner)
    def _():
        @pl.loop(0, 15)
        def _(slot):
            remote(
                sum_plane.at[pl.ds(0, WINDOW)], from_line.at[slot], line_send.at[0], line_recv.at[slot], partner
            ).wait_recv()

        own = pl.multiple_of((z_hi * 2 + col // 4) * WINDOW, WINDOW)
        total = sum_plane[pl.ds(own, WINDOW), :].astype(jnp.float32)
        for slot in range(15):
            total = total + from_line[slot].astype(jnp.float32)
        share_buf[...] = total
        for step in range(1, 4):
            share_copy(step).start()

    @pl.when(jnp.logical_not(owner))
    def _():
        share_copy(1).wait_recv()

    offset = (SHARE * (row * 8 + col)) % 1024
    place = lax.broadcasted_iota(jnp.int32, (WINDOW, 128), 0) * 128 + lax.broadcasted_iota(jnp.int32, (WINDOW, 128), 1)
    inside = jnp.logical_and(place >= offset, place < offset + SHARE)
    share = share_buf[...]
    squares = jnp.where(inside, share * share, 0.0)
    square_buf[...] = squares.reshape(8, 8, 128).sum(axis=0)

    def near_copy(step):
        return remote(
            square_buf, from_near.at[step - 1], near_send.at[step - 1], near_recv.at[step - 1], near_peer(step)
        )

    @pl.loop(1, 8)
    def _(step):
        near_copy(step).start()

    @pl.loop(1, 8)
    def _(step):
        near_copy(step).wait()

    near_buf[...] = square_buf[...] + from_near[...].sum(axis=0)

    def far_copy(step):
        return remote(
            near_buf, from_far.at[step - 1], far_send.at[step - 1], far_recv.at[step - 1], line_peer(step)
        )

    @pl.loop(1, 16)
    def _(step):
        far_copy(step).start()

    @pl.loop(1, 16)
    def _(step):
        far_copy(step).wait()

    total_squares = jnp.sum(near_buf[...] + from_far[...].sum(axis=0), keepdims=True)
    spread_rms = jnp.sqrt(total_squares / TOTAL + EPSILON)
    out_ref[...] = share_buf[...] * jnp.minimum(jnp.float32(1.0), 1.0 / spread_rms)

    for block in range(4):
        step, copy = line_copy(block)

        @pl.when(step != 0)
        def _():
            copy.wait_send()

    @pl.when(owner)
    def _():
        for step in range(1, 4):
            share_copy(step).wait_send()


GROUP = 384
CELLS = 24
PIECES = (
    (48, 0, 0, 432), (96, 162, 0, 864), (192, 810, 0, 1728), (96, 3402, 864, 432), (192, 3726, 1728, 864),
    (48, 5022, 432, 96), (48, 5058, 528, 192), (48, 5130, 720, 384), (96, 5274, 1296, 192),
    (96, 5418, 1488, 384), (192, 5706, 2592, 384),
)
BF16 = jnp.bfloat16
F32 = jnp.float32


def dot(left, right, left_dim=1, right_dim=0):
    return lax.dot_general(left, right, (((left_dim,), (right_dim,)), ((), ())), preferred_element_type=F32)


def lanes_of(rows, lanes):
    return lax.broadcasted_iota(jnp.int32, (rows, lanes), 1)


def fill_packets(u1, u2, u3, send_rows, send_sides, send_corners):
    wide = CELLS * GROUP
    last = wide - GROUP
    blank = jnp.zeros((1, wide), F32)
    bottom = jnp.concatenate([u1[4:8], u2[2:4], u3[1:2], blank], axis=0)
    top = jnp.concatenate([u2[0:2], u3[0:1], blank, u1[0:4]], axis=0)
    empty = jnp.zeros((8, GROUP), F32)
    for index, part in enumerate((bottom, top)):
        send_rows[index] = jnp.concatenate([part[:, : wide // 2], part[:, wide // 2 :]], axis=0).astype(BF16)
        send_corners[2 * index] = jnp.concatenate([part[:, last:], empty], axis=0).astype(BF16)
        send_corners[2 * index + 1] = jnp.concatenate([part[:, :GROUP], empty], axis=0).astype(BF16)
    for index, start in enumerate((last, 0)):
        send_sides[index] = jnp.concatenate(
            [u1[:, start : start + GROUP], u2[:, start : start + GROUP], u3[:, start : start + GROUP], empty[:2]], axis=0
        ).astype(BF16)


def banded(weights, repeat, width, rows, blocks, dst):
    wide = dot(weights, repeat)
    lane = lanes_of(rows, repeat.shape[1])
    for block, pieces in enumerate(blocks):
        value = jnp.zeros((rows, repeat.shape[1]), F32)
        for tap, start in pieces:
            inside = jnp.logical_and(lane >= start, lane < start + width)
            value = jnp.where(inside, wide[tap * rows : (tap + 1) * rows], value)
        dst[block * rows : (block + 1) * rows, :] = value.astype(BF16)


def conv_blocks(tap_row, width, base):
    return [[(tap_row * 3 + tap, base + width * (n + 1 - tap)) for tap in range(3)] for n in range(GROUP // width)]


def down_blocks(tap_row, width):
    blocks = []
    for j in range(2 * (GROUP // width)):
        if j % 2 == 0:
            blocks.append([(tap_row * 3 + 1, width * (j // 2))])
        else:
            blocks.append([(tap_row * 3 + 2, width * (j // 2)), (tap_row * 3, width * (j // 2 + 1))])
    return blocks


def mixer_blocks(width, count):
    return [[(0, width * j)] for j in range(count)]


def window(value, start, width):
    first, end = start // 128, -(-(start + width) // 128)
    part = value[:, first * 128 : end * 128]
    shift = start - first * 128
    if shift:
        part = pltpu.roll(part, (end - first) * 128 - shift, 1)
    return part[:, : -(-width // 128) * 128]


def place(src, flat, width, flat_base, src_base, count):
    stride = GROUP // width
    rows = count // stride
    lane = lanes_of(rows, 128)
    held = {}
    for tile in range(3):
        value = None
        for j in range(stride):
            for part in range(-(-width // 128)):
                low = max(width * j + 128 * part, 128 * tile)
                high = min(width * j + min(width, 128 * part + 128), 128 * tile + 128)
                if low >= high:
                    continue
                if (j, part) not in held:
                    held[j, part] = src[part, pl.ds(src_base + j, rows, stride=stride), :]
                piece = held[j, part]
                shift = (width * j + 128 * part - 128 * tile) % 128
                if shift:
                    piece = pltpu.roll(piece, shift, 1)
                value = piece if value is None else jnp.where(lane >= low - 128 * tile, piece, value)
        flat[pl.ds(flat_base + tile, rows, stride=3), :] = value


def backward_kernel(
    f1_ref, f2_ref, f3_ref, f4_ref, o1_ref, o2_ref, o3_ref, u1_ref, u2_ref, u3_ref,
    k1_ref, k2_ref, k3_ref, s12_ref, s23_ref, m21_ref, m31_ref, m41_ref, m32_ref, m42_ref, m43_ref,
    rep1_ref, rep2_ref, rep3_ref, rep12_ref, rep23_ref, rep96_ref, rep192_ref, pool1_ref, pool2_ref, pool3_ref,
    g1_ref, g2_ref, g3_ref, g4_ref, share_ref,
    packed_ref, send_rows, send_sides, send_corners, recv_rows, recv_sides, recv_corners, halo_send, halo_recv,
    ext1, ext2, ext3, v1, v2, v3, del1, del2, del3, pad_f2, pad_f3, pad_o1, pad_o2, pad_o3, rows_f4,
    band1, band2, band3, band12, band23, band21, band31, band32, res2, res3, w48, w96, w192, flat, *reduce_refs,
):
    half = CELLS // 2

    def lanes(g):
        return slice(GROUP * g, GROUP * (g + 1))

    x = lax.axis_index("branch")
    row = lax.axis_index("row")
    col = lax.axis_index("col")
    core, z_hi, y = row % 2, (row // 2) % 2, row // 4
    z = z_hi * 8 + col
    line = x * 16 + row

    def peer(down, right):
        there = (line + down + 64) % 64
        return (there // 16, there % 16, (col + right + 8) % 8)

    routes = (
        (0, 1, 0, send_rows.at[0], recv_rows.at[0]),
        (1, -1, 0, send_rows.at[1], recv_rows.at[1]),
        (2, 0, 1, send_sides.at[0], recv_sides.at[0]),
        (3, 0, -1, send_sides.at[1], recv_sides.at[1]),
        (4, 1, 1, send_corners.at[0], recv_corners.at[0]),
        (5, 1, -1, send_corners.at[1], recv_corners.at[1]),
        (6, -1, 1, send_corners.at[2], recv_corners.at[2]),
        (7, -1, -1, send_corners.at[3], recv_corners.at[3]),
    )

    def plane_peer(step):
        there = (x * 4 + y + step) % 16
        return there, (there // 4, (there % 4) * 4 + z_hi * 2 + core, col)

    def line_peer(step):
        there = (z + step) % 16
        return (x, y * 4 + (there // 8) * 2 + core, there % 8)

    def near_peer(step):
        there = (y * 2 + core + step) % 8
        return (x, (there // 2) * 4 + z_hi * 2 + there % 2, col)

    def greet(peer):
        pl.semaphore_signal(barrier, inc=1, device_id=peer, device_id_type=MESH)

    barrier = pltpu.get_barrier_semaphore()
    for route in routes:
        greet(peer(route[1], route[2]))
    greet((x, row + 1 - 2 * core, col))

    @pl.loop(1, 16)
    def _(step):
        greet(plane_peer(step)[1])
        greet(line_peer(step))

    @pl.loop(1, 8)
    def _(step):
        greet(near_peer(step))

    u1, u2, u3 = (ref[...].astype(F32) for ref in (u1_ref, u2_ref, u3_ref))
    fill_packets(u1, u2, u3, send_rows, send_sides, send_corners)
    pl.semaphore_wait(barrier, 46)

    def halo_copy(route):
        slot, down, right, src, dst = route
        return pltpu.make_async_remote_copy(
            src_ref=src, dst_ref=dst, send_sem=halo_send.at[slot], recv_sem=halo_recv.at[slot],
            device_id=peer(down, right), device_id_type=MESH,
        )

    for route in routes:
        halo_copy(route).start()

    for ref in (pad_f2, pad_f3, pad_o1, pad_o2, pad_o3):
        ref[...] = jnp.zeros_like(ref)
    f2, f3, o1, o2, o3, f4 = (ref[...].astype(F32) for ref in (f2_ref, f3_ref, o1_ref, o2_ref, o3_ref, f4_ref))
    for g in range(CELLS):
        at = lanes(g)
        pad_f2[8 * g + 2 : 8 * g + 6, :] = f2[:, at]
        pad_f3[4 * g + 1 : 4 * g + 3, :] = f3[:, at]
        for tile in range(3):
            part = slice(GROUP * g + 128 * tile, GROUP * g + 128 * tile + 128)
            pad_o1[tile, 16 * g + 4 : 16 * g + 12, :] = o1[:, part]
            pad_o2[tile, 8 * g + 2 : 8 * g + 6, :] = o2[:, part]
        pad_o3[4 * g + 1 : 4 * g + 3, :] = o3[:, at]
        rows_f4[g : g + 1, :] = f4[:, at]

    for a in range(3):
        banded(k1_ref[...], rep1_ref[...], 48, 48, conv_blocks(a, 48, 128), band1.at[a])
        banded(k2_ref[...], rep2_ref[...], 96, 96, conv_blocks(a, 96, 128), band2.at[a])
        banded(k3_ref[...], rep3_ref[...], 192, 192, conv_blocks(a, 192, 256), band3.at[a])
        banded(s12_ref[...], rep12_ref[...], 96, 48, down_blocks(a, 96), band12.at[a])
        banded(s23_ref[...], rep23_ref[...], 192, 96, down_blocks(a, 192), band23.at[a])
    banded(m21_ref[...], rep96_ref[...], 96, 48, mixer_blocks(96, 4), band21)
    banded(m31_ref[...], rep192_ref[...], 192, 48, mixer_blocks(192, 2), band31)
    banded(m32_ref[...], rep96_ref[:, :256], 96, 192, mixer_blocks(96, 2), band32)

    for route in routes:
        halo_copy(route).wait()
    top, bottom = jnp.where(line > 0, 1.0, 0.0), jnp.where(line < 63, 1.0, 0.0)
    left, right = jnp.where(col > 0, 1.0, 0.0), jnp.where(col < 7, 1.0, 0.0)
    above, below = recv_rows[0].astype(F32) * top, recv_rows[1].astype(F32) * bottom
    sides = [recv_sides[0].astype(F32) * left, recv_sides[1].astype(F32) * right]
    corners = [
        recv_corners[0].astype(F32) * (top * left), recv_corners[1].astype(F32) * (top * right),
        recv_corners[2].astype(F32) * (bottom * left), recv_corners[3].astype(F32) * (bottom * right),
    ]
    for g in range(CELLS + 2):
        if g == 0 or g == CELLS + 1:
            side = sides[0 if g == 0 else 1]
            mid = side[0:8], side[8:12], side[12:14]
            up = corners[0 if g == 0 else 1]
            down = corners[2 if g == 0 else 3]
        else:
            at = lanes(g - 1)
            mid = u1[:, at], u2[:, at], u3[:, at]
            row0 = 8 * ((g - 1) // half)
            there = lanes((g - 1) % half)
            up, down = above[row0 : row0 + 8, there], below[row0 : row0 + 8, there]
        ext1[g, 0:4, :] = up[0:4]
        ext1[g, 4:12, :] = mid[0]
        ext1[g, 12:16, :] = down[4:8]
        ext2[8 * g : 8 * g + 2, :] = up[4:6]
        ext2[8 * g + 2 : 8 * g + 6, :] = mid[1]
        ext2[8 * g + 6 : 8 * g + 8, :] = down[0:2]
        ext3[4 * g : 4 * g + 1, :] = up[6:7]
        ext3[4 * g + 1 : 4 * g + 3, :] = mid[2]
        ext3[4 * g + 3 : 4 * g + 4, :] = down[2:3]
    ext2[8 * (CELLS + 2) :, :] = jnp.zeros((8, GROUP), F32)
    ext3[4 * (CELLS + 2) :, :] = jnp.zeros((8, GROUP), F32)

    tall1, tall2, tall3 = 16 * (CELLS + 2), 8 * (CELLS + 2), 4 * (CELLS + 2)
    def tiled_store(ref, value, rows=slice(None)):
        for tile in range(value.shape[1] // 128):
            ref[tile, rows, :] = value[:, 128 * tile : 128 * tile + 128]

    def strided(ref, tiles, start, count, stride):
        parts = [ref[tile, pl.ds(start, count, stride=stride), :] for tile in tiles]
        return parts[0] if len(parts) == 1 else jnp.concatenate(parts, axis=1)

    tiled_store(v1, dot(ext1[...].reshape(tall1, GROUP).astype(BF16), pool1_ref[...]))
    tiled_store(v2, dot(ext2[0:tall2, :].astype(BF16), pool2_ref[...]))
    tiled_store(v3, dot(ext3[0:tall3, :].astype(BF16), pool3_ref[...]))

    def strided_sum(ref, picks, count, stride, tiles):
        total = None
        for pick in picks:
            piece = strided(ref, tiles, pick, count, stride)
            total = piece if total is None else total + piece
        return total.astype(BF16)

    p12 = strided_sum(v1, range(2), tall2, 2, (0, 1))
    p13 = strided_sum(v1, range(4), tall3, 4, (2,))
    p14 = strided_sum(v1, range(16 + 4, 16 + 12), CELLS, 16, (3,))
    p23 = strided_sum(v2, range(2), tall3, 2, (0, 1))
    p24 = strided_sum(v2, range(8 + 2, 8 + 6), CELLS, 8, (2,))
    p34 = strided_sum(v3, range(4 + 1, 4 + 3), CELLS, 4, (0, 1))

    def rim_mask(rows, inner):
        place_row = lax.broadcasted_iota(jnp.int32, (CELLS + 2, rows, GROUP), 1)
        place_col = lax.broadcasted_iota(jnp.int32, (CELLS + 2, rows, GROUP), 0)
        start, end = (rows - inner) // 2, (rows + inner) // 2
        by_row = jnp.where(place_row == start - 1, top, jnp.where(place_row == end, bottom, 1.0))
        by_row = jnp.where(jnp.logical_and(place_row >= start - 1, place_row <= end), by_row, 0.0)
        by_col = jnp.where(place_col == 0, left, jnp.where(place_col == CELLS + 1, right, 1.0))
        return by_row * by_col

    def rolled(value):
        return pltpu.roll(value, value.shape[0] - 1, 0)

    x2 = jnp.concatenate([ext2[0:tall2, :], ext2[8 : tall2 + 8, 0:128]], axis=1).astype(BF16)
    tiled_store(v1, dot(x2, band12[1], 1, 1), pl.ds(0, tall2, stride=2))
    tiled_store(v1, dot(x2, band12[2], 1, 1) + rolled(dot(x2, band12[0], 1, 1)), pl.ds(1, tall2, stride=2))
    spread1 = jnp.concatenate([v1[tile] for tile in range(3)], axis=1)
    delta1 = ext1[...] + spread1.reshape(CELLS + 2, 16, GROUP)
    del1[...] = (delta1 * rim_mask(16, 8)).astype(BF16).astype(F32)

    x3 = jnp.concatenate([ext3[0:tall3, :], ext3[4 : tall3 + 4, 0:256]], axis=1).astype(BF16)
    tiled_store(v2, dot(x3, band23[1], 1, 1), pl.ds(0, tall3, stride=2))
    tiled_store(v2, dot(x3, band23[2], 1, 1) + rolled(dot(x3, band23[0], 1, 1)), pl.ds(1, tall3, stride=2))
    spread2 = jnp.concatenate([v2[tile] for tile in range(3)], axis=1)
    delta2 = ext2[0:tall2, :] + dot(p12[:, 0:192], band21[...]) + spread2
    del2[8 : 8 + tall2, :] = (delta2 * rim_mask(8, 4).reshape(tall2, GROUP)).astype(BF16).astype(F32)

    delta3 = ext3[0:tall3, :] + dot(p13[:, 0:96], band31[...]) + dot(p23, band32[...], 1, 1)
    place_row = lax.broadcasted_iota(jnp.int32, (tall3, GROUP), 0)
    in_group = jnp.bitwise_and(place_row, 3)
    by_row = jnp.where(in_group == 0, top, jnp.where(in_group == 3, bottom, 1.0))
    by_col = jnp.where(place_row < 4, left, jnp.where(place_row >= 4 * (CELLS + 1), right, 1.0))
    del3[8 : 8 + tall3, :] = (delta3 * (by_row * by_col)).astype(BF16).astype(F32)
    for ref in (del2, del3):
        ref[0:8, :] = jnp.zeros((8, GROUP), F32)
        ref[ref.shape[0] - 8 :, :] = jnp.zeros((8, GROUP), F32)

    def fold(grads, width, base, a, dst):
        total = None
        for n in range(GROUP // width):
            part = window(grads[n * width : (n + 1) * width, :], base + width * (n - 1), 3 * width)
            total = part if total is None else total + part
        for tap in range(3):
            start = (a * 3 + tap) * width
            tiled_store(dst, window(total, width * (2 - tap), width), slice(start, start + width))

    f1 = f1_ref[...]
    f1 = jnp.concatenate([f1[:, lanes(g)].astype(F32) for g in range(CELLS)], axis=0).astype(BF16)
    back = None
    for a in range(3):
        at = slice(5 - a, 13 - a)
        x1 = jnp.concatenate(
            [del1[0:CELLS, at, 256:GROUP], del1[1 : CELLS + 1, at, :], del1[2 : CELLS + 2, at, 0:128]], axis=2
        ).reshape(8 * CELLS, 640).astype(BF16)
        part = dot(x1, band1[a], 1, 1)
        back = part if back is None else back + part
        fold(dot(f1, x1, 0, 0), 48, 128, a, w48)
    for g in range(CELLS):
        g1_ref[:, lanes(g)] = back[8 * g : 8 * g + 8].astype(BF16)

    f2x = pad_f2[...].astype(BF16)
    back = None
    for a in range(3):
        at = 8 + 1 - a
        n = 8 * CELLS
        x2d = jnp.concatenate(
            [del2[at : at + n, 256:GROUP], del2[at + 8 : at + 8 + n, :], del2[at + 16 : at + 16 + n, 0:128]], axis=1
        ).astype(BF16)
        part = dot(x2d, band2[a], 1, 1)
        back = part if back is None else back + part
        fold(dot(f2x, x2d, 0, 0), 96, 128, a, w96)
    res2[...] = back
    for g in range(CELLS):
        g2_ref[:, lanes(g)] = res2[8 * g + 2 : 8 * g + 6, :].astype(BF16)

    f3x = pad_f3[...].astype(BF16)
    back = None
    for a in range(3):
        at = 8 + 1 - a
        n = 4 * CELLS
        x3d = jnp.concatenate(
            [del3[at : at + n, 128:GROUP], del3[at + 4 : at + 4 + n, :], del3[at + 8 : at + 8 + n, 0:256]], axis=1
        ).astype(BF16)
        part = dot(x3d, band3[a], 1, 1)
        back = part if back is None else back + part
        fold(dot(f3x, x3d, 0, 0), 192, 256, a, w192)
    res3[...] = back
    for g in range(CELLS):
        g3_ref[:, lanes(g)] = res3[4 * g + 1 : 4 * g + 3, :].astype(BF16)

    def fold_down(grads, width, rows, a, base, dst):
        for b in range(3):
            total = None
            for j in range(1 if b != 1 else 0, 2 * (GROUP // width), 2):
                p = (j + 1 - b) // 2
                part = window(grads[j * rows : (j + 1) * rows, :], width * p, width)
                total = part if total is None else total + part
            start = base + (a * 3 + b) * rows
            tiled_store(dst, total, slice(start, start + rows))

    def down_grads(saved, ext, skip, count, head, width, rows, base, dst):
        even = strided(saved, range(3), 0, count, 2).astype(BF16)
        odd = strided(saved, range(3), 1, count, 2).astype(BF16)
        for a in range(3):
            at = skip + (1 if a == 0 else 0)
            xs = jnp.concatenate(
                [ext[at : at + count, :], ext[at + skip : at + skip + count, 0:head]], axis=1
            ).astype(BF16)
            fold_down(dot(even if a == 1 else odd, xs, 0, 0), width, rows, a, base, dst)

    down_grads(pad_o1, ext2, 8, 8 * CELLS, 128, 96, 48, 864, w96)
    down_grads(pad_o2, ext3, 4, 4 * CELLS, 256, 192, 96, 1728, w192)

    def fold_mixer(grads, width, rows, base, dst):
        total = None
        for j in range(GROUP // rows):
            part = window(grads[j * rows : (j + 1) * rows, :], width * j, width)
            total = part if total is None else total + part
        tiled_store(dst, total, slice(base, base + rows))

    o2x = jnp.concatenate([pad_o2[tile] for tile in range(3)], axis=1).astype(BF16)
    o3x = pad_o3[...].astype(BF16)
    f4x = rows_f4[...].astype(BF16)
    inner2, inner3 = slice(8, 8 + 8 * CELLS), slice(4, 4 + 4 * CELLS)
    fold_mixer(dot(o2x, p12[inner2], 0, 0), 48, 96, 432, w48)
    fold_mixer(dot(o3x, p13[inner3], 0, 0), 48, 192, 528, w48)
    fold_mixer(dot(f4x, p14, 0, 0), 48, 384, 720, w48)
    fold_mixer(dot(o3x, p23[inner3], 0, 0), 96, 192, 1296, w96)
    fold_mixer(dot(f4x, p24, 0, 0), 96, 384, 1488, w96)
    fold_mixer(dot(f4x, p34, 0, 0), 192, 384, 2592, w192)
    back4 = (
        dot(p14[:, 0:48], m41_ref[...]) + dot(p24[:, 0:96], m42_ref[...]) + dot(p34[:, 0:192], m43_ref[...])
    )
    for g in range(CELLS):
        g4_ref[:, lanes(g)] = back4[g : g + 1].astype(BF16)

    for width, flat_base, src_base, count in PIECES:
        place({48: w48, 96: w96, 192: w192}[width], flat, width, flat_base, src_base, count)
    flat[6282:FLAT_ROWS, :] = jnp.zeros((FLAT_ROWS - 6282, 128), F32)
    pack_shares(flat, packed_ref)
    reduce_stages(packed_ref, share_ref, *reduce_refs)


def repeats(width, lanes, base=0):
    lane = np.arange(lanes)[None, :]
    return ((lane - base) % width == np.arange(width)[:, None]).astype(np.float32)


def pools(width, factors, parts):
    blocks = []
    for factor, lanes in zip(factors, parts):
        block = np.zeros((GROUP, lanes), np.float32)
        for lane in range(GROUP):
            block[lane, lane // (width * factor) * width + lane % width] = 1.0
        blocks.append(block)
    return np.concatenate(blocks, axis=1)


def local(f1, f2, f3, f4, o1, o2, o3, u1, u2, u3, k1, k2, k3, s12, s23, m21, m31, m41, m32, m42, m43):
    constants = [
        jnp.asarray(value, BF16)
        for value in (
            repeats(48, 640, 128), repeats(96, 640, 128), repeats(192, 896, 256), repeats(96, 512), repeats(192, 640),
            repeats(96, 384), repeats(192, 384),
            pools(48, (2, 4, 8), (256, 128, 128)), pools(96, (2, 4), (256, 128)), pools(192, (2,), (256,)),
        )
    ]
    whole = pl.BlockSpec(memory_space=pltpu.VMEM)
    inputs = [
        f1, f2, f3, f4, o1, o2, o3, u1, u2, u3,
        k1.reshape(432, 48), k2.reshape(864, 96), k3.reshape(1728, 192), s12.reshape(432, 96), s23.reshape(864, 192),
        m21.T, m31.T, m41.T, m32, m42.T, m43.T,
    ] + constants

    def f32(*shape):
        return pltpu.VMEM(shape, F32)

    def bf16(*shape):
        return pltpu.VMEM(shape, BF16)

    ext = CELLS + 2
    dma = pltpu.SemaphoreType.DMA
    packets = ((2, 16, CELLS * GROUP // 2), (2, 16, GROUP), (4, 16, GROUP))
    grad_one, grad_two, grad_three, grad_four, share = pl.pallas_call(
        backward_kernel,
        out_shape=[jax.ShapeDtypeStruct(value.shape, BF16) for value in (f1, f2, f3, f4)]
        + [jax.ShapeDtypeStruct((WINDOW, 128), F32)],
        in_specs=[whole] * len(inputs),
        out_specs=[whole] * 5,
        scratch_shapes=[
            bf16(128 * WINDOW, 128), *(bf16(*shape) for shape in packets + packets), dma((8,)), dma((8,)),
            f32(ext, 16, GROUP), f32(8 * ext + 8, GROUP), f32(4 * ext + 8, GROUP),
            f32(4, 16 * ext, 128), f32(3, 8 * ext, 128), f32(2, 4 * ext, 128),
            f32(ext, 16, GROUP), f32(8 * ext + 16, GROUP), f32(4 * ext + 16, GROUP),
            f32(8 * CELLS, GROUP), f32(4 * CELLS, GROUP), f32(3, 16 * CELLS, 128), f32(3, 8 * CELLS, 128),
            f32(4 * CELLS, GROUP), f32(CELLS, GROUP),
            bf16(3, GROUP, 640), bf16(3, GROUP, 640), bf16(3, GROUP, 896), bf16(3, GROUP, 512), bf16(3, GROUP, 640),
            bf16(192, GROUP), bf16(96, GROUP), bf16(GROUP, 256),
            f32(8 * CELLS, GROUP), f32(4 * CELLS, GROUP),
            f32(1, 1104, 128), f32(1, 1872, 128), f32(2, 2976, 128), f32(FLAT_ROWS, 128),
            pltpu.VMEM((64 * WINDOW, 128), jnp.bfloat16),
            pltpu.VMEM((64 * WINDOW, 128), jnp.bfloat16),
            pltpu.VMEM((15, 4 * WINDOW, 128), jnp.bfloat16),
            pltpu.VMEM((4 * WINDOW, 128), jnp.bfloat16),
            pltpu.VMEM((15, WINDOW, 128), jnp.bfloat16),
            pltpu.VMEM((WINDOW, 128), jnp.float32),
            pltpu.VMEM((8, 128), jnp.float32),
            pltpu.VMEM((7, 8, 128), jnp.float32),
            pltpu.VMEM((8, 128), jnp.float32),
            pltpu.VMEM((15, 8, 128), jnp.float32),
            dma((2,)),
            dma((15,)),
            dma((15,)),
            dma((4,)),
            dma((15,)),
            dma((3,)),
            dma((1,)),
            dma((7,)),
            dma((7,)),
            dma((15,)),
            dma((15,)),
        ],
        compiler_params=pltpu.CompilerParams(
            collective_id=0, has_side_effects=True, vmem_limit_bytes=48 * 1024 * 1024
        ),
        name="backward",
    )(*inputs)
    offset = (SHARE * lax.axis_index(("row", "col"))) % 1024
    weight_grads = lax.dynamic_slice(share.reshape(WINDOW * 128), (offset,), (SHARE,))
    return grad_one, grad_two, grad_three, grad_four, weight_grads


def solution(mesh):
    in_specs = (
        P(("branch", "row"), "col"),
        P(("branch", "row"), "col"),
        P(("branch", "row"), "col"),
        P(("branch", "row"), "col"),
        P(("branch", "row"), "col"),
        P(("branch", "row"), "col"),
        P(("branch", "row"), "col"),
        P(("branch", "row"), "col"),
        P(("branch", "row"), "col"),
        P(("branch", "row"), "col"),
        P(),
        P(),
        P(),
        P(),
        P(),
        P(),
        P(),
        P(),
        P(),
        P(),
        P(),
    )
    out_specs = (
        P(("branch", "row"), "col"),
        P(("branch", "row"), "col"),
        P(("branch", "row"), "col"),
        P(("branch", "row"), "col"),
        P(("row", "col")),
    )
    return jax.shard_map(local, mesh=mesh, in_specs=in_specs, out_specs=out_specs, check_vma=False)
```

```python
import jax
import jax.numpy as jnp
import numpy as np
from jax import lax
from jax.experimental import pallas as pl
from jax.experimental.pallas import tpu as pltpu
from jax.sharding import PartitionSpec as P

EPSILON = 1e-06
MESH = pl.DeviceIdType.MESH
BF16 = jnp.bfloat16
F32 = jnp.float32
TOTAL = 804096
SHARE = 6282
WINDOW = 64
FLAT_ROWS = 6296


def share_place(share):
    row, col = divmod(share, 8)
    core, z_hi, y = row % 2, (row // 2) % 2, row // 4
    half, quarter = divmod(col, 4)
    return ((y * 2 + core) * 4 + quarter) * 4 + z_hi * 2 + half


def pack_shares(flat_ref, packed_ref, block):
    for share in range(32 * block, 32 * block + 32):
        start = SHARE * share // 1024 * 8
        place = share_place(share) * WINDOW
        packed_ref[place : place + WINDOW, :] = flat_ref[start : start + WINDOW, :].astype(jnp.bfloat16)


BLOCK = 16 * WINDOW
PART = 4 * WINDOW


class Reduction:
    def __init__(self, packed, where, from_core, sum_core, from_x, sum_x, from_y, core_send, core_recv, x_send, x_recv, y_send, y_recv):
        self.packed, self.where = packed, where
        self.from_core, self.sum_core, self.from_x, self.sum_x, self.from_y = from_core, sum_core, from_x, sum_x, from_y
        self.core_send, self.core_recv = core_send, core_recv
        self.x_send, self.x_recv, self.y_send, self.y_recv = x_send, x_recv, y_send, y_recv

    def core_copy(self, block):
        x, row, col = self.where
        core = row % 2
        start = pl.multiple_of((block * 2 + 1 - core) * BLOCK, BLOCK)
        return remote(
            self.packed.at[pl.ds(start, BLOCK)], self.from_core.at[pl.ds(block * BLOCK, BLOCK)],
            self.core_send.at[block], self.core_recv.at[block], (x, row + 1 - 2 * core, col),
        )

    def x_copy(self, block, step):
        x, row, col = self.where
        there = (x + step) % 4
        start = pl.multiple_of(block * BLOCK + there * PART, PART)
        slot = block * 3 + step - 1
        return remote(
            self.sum_core.at[pl.ds(start, PART)], self.from_x.at[slot], self.x_send.at[slot], self.x_recv.at[slot],
            (there, row, col),
        )

    def y_copy(self, block):
        x, row, col = self.where
        y = row // 4
        step = (block - y + 4) % 4
        return remote(
            self.sum_x.at[pl.ds(block * PART, PART)], self.from_y.at[step], self.y_send.at[step], self.y_recv.at[step],
            (x, block * 4 + row % 4, col),
        )

    def leave(self, block):
        self.core_copy(block).start()

    def along_x(self, block):
        core = self.where[1] % 2
        self.core_copy(block).wait()

        @pl.loop(0, 4)
        def _(part):
            mine = pl.multiple_of((block * 2 + core) * BLOCK + part * PART, PART)
            place = pl.multiple_of(block * BLOCK + part * PART, PART)
            total = self.packed[pl.ds(mine, PART), :].astype(F32) + self.from_core[pl.ds(place, PART), :].astype(F32)
            self.sum_core[pl.ds(place, PART), :] = total.astype(BF16)

        for step in range(1, 4):
            self.x_copy(block, step).start()

    def along_y(self, block):
        x, row, col = self.where
        for step in range(1, 4):
            self.x_copy(block, step).wait()
        own = pl.multiple_of(block * BLOCK + x * PART, PART)
        total = self.sum_core[pl.ds(own, PART), :].astype(F32)
        for step in range(3):
            total = total + self.from_x[block * 3 + step].astype(F32)
        self.sum_x[block * PART : (block + 1) * PART, :] = total.astype(BF16)

        @pl.when(row // 4 != block)
        def _():
            self.y_copy(block).start()

    def plane_sum(self, sum_plane):
        y = self.where[1] // 4
        for step in range(1, 4):
            remote(
                self.sum_x.at[pl.ds(0, PART)], self.from_y.at[step], self.y_send.at[step], self.y_recv.at[step], self.where
            ).wait_recv()
        total = self.sum_x[pl.ds(pl.multiple_of(y * PART, PART), PART), :].astype(F32)
        for step in range(1, 4):
            total = total + self.from_y[step].astype(F32)
        sum_plane[...] = total.astype(BF16)
        for step in range(1, 4):
            remote(
                self.sum_x.at[pl.ds(0, PART)], self.from_y.at[step], self.y_send.at[step], self.y_recv.at[step], self.where
            ).wait_send()


def remote(src, dst, send_sem, recv_sem, peer):
    return pltpu.make_async_remote_copy(
        src_ref=src, dst_ref=dst, send_sem=send_sem, recv_sem=recv_sem, device_id=peer, device_id_type=MESH
    )


def finish_shares(
    out_ref,
    sum_plane,
    from_line,
    share_buf,
    square_buf,
    from_near,
    near_buf,
    from_far,
    line_send,
    line_recv,
    share_send,
    share_recv,
    near_send,
    near_recv,
    far_send,
    far_recv,
):
    x = lax.axis_index("branch")
    row = lax.axis_index("row")
    col = lax.axis_index("col")
    core, z_hi, y = row % 2, (row // 2) % 2, row // 4
    z = z_hi * 8 + col
    partner = (x, row + 1 - 2 * core, col)

    def line_peer(step):
        there = (z + step) % 16
        return (x, y * 4 + (there // 8) * 2 + core, there % 8)

    def near_peer(step):
        there = (y * 2 + core + step) % 8
        return (x, (there // 2) * 4 + z_hi * 2 + there % 2, col)

    def line_copy(block):
        target = (block // 2) * 8 + (block % 2) * 4 + x
        step = (z - target + 16) % 16
        slot = (step + 15) % 16
        return step, remote(
            sum_plane.at[pl.ds(pl.multiple_of(block * WINDOW, WINDOW), WINDOW)],
            from_line.at[slot], line_send.at[block], line_recv.at[slot],
            (x, y * 4 + (target // 8) * 2 + core, target % 8),
        )

    for block in range(4):
        step, copy = line_copy(block)

        @pl.when(step != 0)
        def _():
            copy.start()

    owner_x = col % 4
    owner = owner_x == x

    def share_copy(step):
        return remote(
            share_buf, share_buf, share_send.at[step - 1], share_recv.at[0],
            ((x + step) % 4, row, col),
        )

    @pl.when(owner)
    def _():
        @pl.loop(0, 15)
        def _(slot):
            remote(
                sum_plane.at[pl.ds(0, WINDOW)], from_line.at[slot], line_send.at[0], line_recv.at[slot], partner
            ).wait_recv()

        own = pl.multiple_of((z_hi * 2 + col // 4) * WINDOW, WINDOW)
        total = sum_plane[pl.ds(own, WINDOW), :].astype(jnp.float32)
        for slot in range(15):
            total = total + from_line[slot].astype(jnp.float32)
        share_buf[...] = total
        for step in range(1, 4):
            share_copy(step).start()

    @pl.when(jnp.logical_not(owner))
    def _():
        share_copy(1).wait_recv()

    offset = (SHARE * (row * 8 + col)) % 1024
    place = lax.broadcasted_iota(jnp.int32, (WINDOW, 128), 0) * 128 + lax.broadcasted_iota(jnp.int32, (WINDOW, 128), 1)
    inside = jnp.logical_and(place >= offset, place < offset + SHARE)
    share = share_buf[...]
    squares = jnp.where(inside, share * share, 0.0)
    square_buf[...] = squares.reshape(8, 8, 128).sum(axis=0)

    def near_copy(step):
        return remote(
            square_buf, from_near.at[step - 1], near_send.at[step - 1], near_recv.at[step - 1], near_peer(step)
        )

    @pl.loop(1, 8)
    def _(step):
        near_copy(step).start()

    @pl.loop(1, 8)
    def _(step):
        near_copy(step).wait()

    near_buf[...] = square_buf[...] + from_near[...].sum(axis=0)

    def far_copy(step):
        return remote(
            near_buf, from_far.at[step - 1], far_send.at[step - 1], far_recv.at[step - 1], line_peer(step)
        )

    @pl.loop(1, 16)
    def _(step):
        far_copy(step).start()

    @pl.loop(1, 16)
    def _(step):
        far_copy(step).wait()

    total_squares = jnp.sum(near_buf[...] + from_far[...].sum(axis=0), keepdims=True)
    spread_rms = jnp.sqrt(total_squares / TOTAL + EPSILON)
    out_ref[...] = share_buf[...] * jnp.minimum(jnp.float32(1.0), 1.0 / spread_rms)

    for block in range(4):
        step, copy = line_copy(block)

        @pl.when(step != 0)
        def _():
            copy.wait_send()

    @pl.when(owner)
    def _():
        for step in range(1, 4):
            share_copy(step).wait_send()


GROUP = 384
CELLS = 24
PIECES = (
    (48, 0, 0, 432), (96, 162, 0, 864), (192, 810, 0, 1728), (96, 3402, 864, 432), (192, 3726, 1728, 864),
    (48, 5022, 432, 96), (48, 5058, 528, 192), (48, 5130, 720, 384), (96, 5274, 1296, 192),
    (96, 5418, 1488, 384), (192, 5706, 2592, 384),
)


def dot(left, right, left_dim=1, right_dim=0):
    return lax.dot_general(left, right, (((left_dim,), (right_dim,)), ((), ())), preferred_element_type=F32)


def lanes_of(rows, lanes):
    return lax.broadcasted_iota(jnp.int32, (rows, lanes), 1)


def fill_packets(u1, u2, u3, send_rows, send_sides, send_corners):
    wide = CELLS * GROUP
    last = wide - GROUP
    blank = jnp.zeros((1, wide), F32)
    bottom = jnp.concatenate([u1[4:8], u2[2:4], u3[1:2], blank], axis=0)
    top = jnp.concatenate([u2[0:2], u3[0:1], blank, u1[0:4]], axis=0)
    empty = jnp.zeros((8, GROUP), F32)
    for index, part in enumerate((bottom, top)):
        send_rows[index] = jnp.concatenate([part[:, : wide // 2], part[:, wide // 2 :]], axis=0).astype(BF16)
        send_corners[2 * index] = jnp.concatenate([part[:, last:], empty], axis=0).astype(BF16)
        send_corners[2 * index + 1] = jnp.concatenate([part[:, :GROUP], empty], axis=0).astype(BF16)
    for index, start in enumerate((last, 0)):
        send_sides[index] = jnp.concatenate(
            [u1[:, start : start + GROUP], u2[:, start : start + GROUP], u3[:, start : start + GROUP], empty[:2]], axis=0
        ).astype(BF16)


def banded(weights, repeat, width, rows, blocks, dst):
    wide = dot(weights, repeat)
    lane = lanes_of(rows, repeat.shape[1])
    for block, pieces in enumerate(blocks):
        value = jnp.zeros((rows, repeat.shape[1]), F32)
        for tap, start in pieces:
            inside = jnp.logical_and(lane >= start, lane < start + width)
            value = jnp.where(inside, wide[tap * rows : (tap + 1) * rows], value)
        dst[block * rows : (block + 1) * rows, :] = value.astype(BF16)


def conv_blocks(width, base):
    return [[(tap, base + width * (n + 1 - tap)) for tap in range(3)] for n in range(GROUP // width)]


def down_blocks(width):
    blocks = []
    for j in range(2 * (GROUP // width)):
        if j % 2 == 0:
            blocks.append([(1, width * (j // 2))])
        else:
            blocks.append([(2, width * (j // 2)), (0, width * (j // 2 + 1))])
    return blocks


def mixer_blocks(width, count):
    return [[(0, width * j)] for j in range(count)]


def window(value, start, width):
    first, end = start // 128, -(-(start + width) // 128)
    part = value[:, first * 128 : end * 128]
    shift = start - first * 128
    if shift:
        part = pltpu.roll(part, (end - first) * 128 - shift, 1)
    return part[:, : -(-width // 128) * 128]


def place(src, flat, width, flat_base, src_base, count):
    stride = GROUP // width
    rows = count // stride
    lane = lanes_of(rows, 128)
    held = {}
    for tile in range(3):
        value = None
        for j in range(stride):
            for part in range(-(-width // 128)):
                low = max(width * j + 128 * part, 128 * tile)
                high = min(width * j + min(width, 128 * part + 128), 128 * tile + 128)
                if low >= high:
                    continue
                if (j, part) not in held:
                    held[j, part] = src[part, pl.ds(src_base + j, rows, stride=stride), :]
                piece = held[j, part]
                shift = (width * j + 128 * part - 128 * tile) % 128
                if shift:
                    piece = pltpu.roll(piece, shift, 1)
                value = piece if value is None else jnp.where(lane >= low - 128 * tile, piece, value)
        flat[pl.ds(flat_base + tile, rows, stride=3), :] = value


def backward_kernel(
    f1_ref, f2_ref, f3_ref, f4_ref, o1_ref, o2_ref, o3_ref, u1_ref, u2_ref, u3_ref,
    k1_ref, k2_ref, k3_ref, s12_ref, s23_ref, m21_ref, m31_ref, m41_ref, m32_ref, m42_ref, m43_ref,
    rep1_ref, rep2_ref, rep3_ref, rep12_ref, rep23_ref, rep96_ref, rep192_ref, pool1_ref, pool2_ref, pool3_ref,
    g1_ref, g2_ref, g3_ref, g4_ref, share_ref,
    packed_ref, send_rows, send_sides, send_corners, recv_rows, recv_sides, recv_corners, halo_send, halo_recv,
    ext1, ext2, ext3, v1, v2, v3, del1, del2, del3, pad_f2, pad_f3, pad_o1, pad_o2, pad_o3, rows_f4,
    band1, band2, band3, band12, band23, band21, band31, band32, res2, res3, w48, w96, w192, flat, *reduce_refs,
):
    half = CELLS // 2

    def lanes(g):
        return slice(GROUP * g, GROUP * (g + 1))

    x = lax.axis_index("branch")
    row = lax.axis_index("row")
    col = lax.axis_index("col")
    core, z_hi, y = row % 2, (row // 2) % 2, row // 4
    z = z_hi * 8 + col
    line = x * 16 + row

    def peer(down, right):
        there = (line + down + 64) % 64
        return (there // 16, there % 16, (col + right + 8) % 8)

    routes = (
        (0, 1, 0, send_rows.at[0], recv_rows.at[0]),
        (1, -1, 0, send_rows.at[1], recv_rows.at[1]),
        (2, 0, 1, send_sides.at[0], recv_sides.at[0]),
        (3, 0, -1, send_sides.at[1], recv_sides.at[1]),
        (4, 1, 1, send_corners.at[0], recv_corners.at[0]),
        (5, 1, -1, send_corners.at[1], recv_corners.at[1]),
        (6, -1, 1, send_corners.at[2], recv_corners.at[2]),
        (7, -1, -1, send_corners.at[3], recv_corners.at[3]),
    )

    def line_peer(step):
        there = (z + step) % 16
        return (x, y * 4 + (there // 8) * 2 + core, there % 8)

    def near_peer(step):
        there = (y * 2 + core + step) % 8
        return (x, (there // 2) * 4 + z_hi * 2 + there % 2, col)

    def greet(peer):
        pl.semaphore_signal(barrier, inc=1, device_id=peer, device_id_type=MESH)

    barrier = pltpu.get_barrier_semaphore()
    for route in routes:
        greet(peer(route[1], route[2]))
    for step in range(1, 4):
        greet(((x + step) % 4, row, col))

    @pl.loop(1, 16)
    def _(step):
        greet(line_peer(step))

    @pl.loop(1, 8)
    def _(step):
        greet(near_peer(step))

    u1, u2, u3 = (ref[...].astype(F32) for ref in (u1_ref, u2_ref, u3_ref))
    fill_packets(u1, u2, u3, send_rows, send_sides, send_corners)
    pl.semaphore_wait(barrier, 33)

    def halo_copy(route):
        slot, down, right, src, dst = route
        return pltpu.make_async_remote_copy(
            src_ref=src, dst_ref=dst, send_sem=halo_send.at[slot], recv_sem=halo_recv.at[slot],
            device_id=peer(down, right), device_id_type=MESH,
        )

    for route in routes:
        halo_copy(route).start()

    for ref in (ext1, ext2, ext3):
        ref[...] = jnp.zeros_like(ref)
    for g in range(CELLS):
        at = lanes(g)
        ext1[g + 1, 4:12, :] = u1[:, at]
        ext2[8 * g + 10 : 8 * g + 14, :] = u2[:, at]
        ext3[4 * g + 5 : 4 * g + 7, :] = u3[:, at]

    for ref in (pad_f2, pad_f3, pad_o1, pad_o2, pad_o3):
        ref[...] = jnp.zeros_like(ref)
    f2, f3, o1, o2, o3, f4 = (ref[...].astype(F32) for ref in (f2_ref, f3_ref, o1_ref, o2_ref, o3_ref, f4_ref))
    for g in range(CELLS):
        at = lanes(g)
        pad_f2[8 * g + 2 : 8 * g + 6, :] = f2[:, at]
        pad_f3[4 * g + 1 : 4 * g + 3, :] = f3[:, at]
        for tile in range(3):
            part = slice(GROUP * g + 128 * tile, GROUP * g + 128 * tile + 128)
            pad_o1[tile, 16 * g + 4 : 16 * g + 12, :] = o1[:, part]
            pad_o2[tile, 8 * g + 2 : 8 * g + 6, :] = o2[:, part]
        pad_o3[4 * g + 1 : 4 * g + 3, :] = o3[:, at]
        rows_f4[g : g + 1, :] = f4[:, at]

    for a in range(3):
        banded(k1_ref[144 * a : 144 * a + 144, :], rep1_ref[...], 48, 48, conv_blocks(48, 128), band1.at[a])
        banded(k2_ref[288 * a : 288 * a + 288, :], rep2_ref[...], 96, 96, conv_blocks(96, 128), band2.at[a])
        banded(k3_ref[576 * a : 576 * a + 576, :], rep3_ref[...], 192, 192, conv_blocks(192, 256), band3.at[a])
        banded(s12_ref[144 * a : 144 * a + 144, :], rep12_ref[...], 96, 48, down_blocks(96), band12.at[a])
        banded(s23_ref[288 * a : 288 * a + 288, :], rep23_ref[...], 192, 96, down_blocks(192), band23.at[a])
    banded(m21_ref[...], rep96_ref[...], 96, 48, mixer_blocks(96, 4), band21)
    banded(m31_ref[...], rep192_ref[...], 192, 48, mixer_blocks(192, 2), band31)
    banded(m32_ref[...], rep96_ref[:, :256], 96, 192, mixer_blocks(96, 2), band32)

    tall1, tall2, tall3 = 16 * (CELLS + 2), 8 * (CELLS + 2), 4 * (CELLS + 2)
    def tiled_store(ref, value, rows=slice(None)):
        for tile in range(value.shape[1] // 128):
            ref[tile, rows, :] = value[:, 128 * tile : 128 * tile + 128]

    def strided(ref, tiles, start, count, stride):
        parts = [ref[tile, pl.ds(start, count, stride=stride), :] for tile in tiles]
        return parts[0] if len(parts) == 1 else jnp.concatenate(parts, axis=1)

    def strided_sum(ref, picks, count, stride, tiles):
        total = None
        for pick in picks:
            piece = strided(ref, tiles, pick, count, stride)
            total = piece if total is None else total + piece
        return total.astype(BF16)

    tiled_store(v1, dot(ext1[...].reshape(tall1, GROUP).astype(BF16), pool1_ref[...]))
    tiled_store(v2, dot(ext2[0:tall2, :].astype(BF16), pool2_ref[...]))
    tiled_store(v3, dot(ext3[0:tall3, :].astype(BF16), pool3_ref[...]))

    p12 = strided_sum(v1, range(2), tall2, 2, (0, 1))
    p13 = strided_sum(v1, range(4), tall3, 4, (2,))
    p14 = strided_sum(v1, range(16 + 4, 16 + 12), CELLS, 16, (3,))
    p23 = strided_sum(v2, range(2), tall3, 2, (0, 1))
    p24 = strided_sum(v2, range(8 + 2, 8 + 6), CELLS, 8, (2,))
    p34 = strided_sum(v3, range(4 + 1, 4 + 3), CELLS, 4, (0, 1))

    def fold_mixer(grads, width, rows, base, dst):
        total = None
        for j in range(GROUP // rows):
            part = window(grads[j * rows : (j + 1) * rows, :], width * j, width)
            total = part if total is None else total + part
        tiled_store(dst, total, slice(base, base + rows))

    o2x = jnp.concatenate([pad_o2[tile] for tile in range(3)], axis=1).astype(BF16)
    o3x = pad_o3[...].astype(BF16)
    f4x = rows_f4[...].astype(BF16)
    inner2, inner3 = slice(8, 8 + 8 * CELLS), slice(4, 4 + 4 * CELLS)
    fold_mixer(dot(o2x, p12[inner2], 0, 0), 48, 96, 432, w48)
    fold_mixer(dot(o3x, p13[inner3], 0, 0), 48, 192, 528, w48)
    fold_mixer(dot(f4x, p14, 0, 0), 48, 384, 720, w48)
    fold_mixer(dot(o3x, p23[inner3], 0, 0), 96, 192, 1296, w96)
    fold_mixer(dot(f4x, p24, 0, 0), 96, 384, 1488, w96)
    fold_mixer(dot(f4x, p34, 0, 0), 192, 384, 2592, w192)
    back4 = (
        dot(p14[:, 0:48], m41_ref[...]) + dot(p24[:, 0:96], m42_ref[...]) + dot(p34[:, 0:192], m43_ref[...])
    )
    for g in range(CELLS):
        g4_ref[:, lanes(g)] = back4[g : g + 1].astype(BF16)

    for route in routes:
        halo_copy(route).wait()
    top, bottom = jnp.where(line > 0, 1.0, 0.0), jnp.where(line < 63, 1.0, 0.0)
    left, right = jnp.where(col > 0, 1.0, 0.0), jnp.where(col < 7, 1.0, 0.0)
    above, below = recv_rows[0].astype(F32) * top, recv_rows[1].astype(F32) * bottom
    sides = [recv_sides[0].astype(F32) * left, recv_sides[1].astype(F32) * right]
    corners = [
        recv_corners[0].astype(F32) * (top * left), recv_corners[1].astype(F32) * (top * right),
        recv_corners[2].astype(F32) * (bottom * left), recv_corners[3].astype(F32) * (bottom * right),
    ]
    for g in range(CELLS + 2):
        if g == 0 or g == CELLS + 1:
            side = sides[0 if g == 0 else 1]
            ext1[g, 4:12, :] = side[0:8]
            ext2[8 * g + 2 : 8 * g + 6, :] = side[8:12]
            ext3[4 * g + 1 : 4 * g + 3, :] = side[12:14]
            up = corners[0 if g == 0 else 1]
            down = corners[2 if g == 0 else 3]
        else:
            row0 = 8 * ((g - 1) // half)
            there = lanes((g - 1) % half)
            up, down = above[row0 : row0 + 8, there], below[row0 : row0 + 8, there]
        ext1[g, 0:4, :] = up[0:4]
        ext1[g, 12:16, :] = down[4:8]
        ext2[8 * g : 8 * g + 2, :] = up[4:6]
        ext2[8 * g + 6 : 8 * g + 8, :] = down[0:2]
        ext3[4 * g : 4 * g + 1, :] = up[6:7]
        ext3[4 * g + 3 : 4 * g + 4, :] = down[2:3]


    tiled_store(v1, dot(ext1[...].reshape(tall1, GROUP).astype(BF16), pool1_ref[...]))
    tiled_store(v2, dot(ext2[0:tall2, :].astype(BF16), pool2_ref[...]))
    p12 = strided_sum(v1, range(2), tall2, 2, (0, 1))
    p13 = strided_sum(v1, range(4), tall3, 4, (2,))
    p23 = strided_sum(v2, range(2), tall3, 2, (0, 1))

    def fold_down(grads, width, rows, a, base, dst):
        for b in range(3):
            total = None
            for j in range(1 if b != 1 else 0, 2 * (GROUP // width), 2):
                p = (j + 1 - b) // 2
                part = window(grads[j * rows : (j + 1) * rows, :], width * p, width)
                total = part if total is None else total + part
            start = base + (a * 3 + b) * rows
            tiled_store(dst, total, slice(start, start + rows))

    def down_grads(saved, ext, skip, count, head, width, rows, base, dst):
        even = strided(saved, range(3), 0, count, 2).astype(BF16)
        odd = strided(saved, range(3), 1, count, 2).astype(BF16)
        for a in range(3):
            at = skip + (1 if a == 0 else 0)
            xs = jnp.concatenate(
                [ext[at : at + count, :], ext[at + skip : at + skip + count, 0:head]], axis=1
            ).astype(BF16)
            fold_down(dot(even if a == 1 else odd, xs, 0, 0), width, rows, a, base, dst)

    down_grads(pad_o1, ext2, 8, 8 * CELLS, 128, 96, 48, 864, w96)
    down_grads(pad_o2, ext3, 4, 4 * CELLS, 256, 192, 96, 1728, w192)

    reduction = Reduction(packed_ref, (x, row, col), *reduce_refs[:11])
    flat[6282:FLAT_ROWS, :] = jnp.zeros((FLAT_ROWS - 6282, 128), F32)

    def settle(pieces, blocks):
        for piece in pieces:
            width, flat_base, src_base, count = PIECES[piece]
            place({48: w48, 96: w96, 192: w192}[width], flat, width, flat_base, src_base, count)
        for block in blocks:
            pack_shares(flat, packed_ref, block)
            reduction.leave(block)

    settle((3, 4, 5, 6, 7, 8, 9, 10), (3,))

    def rim_mask(rows, inner):
        place_row = lax.broadcasted_iota(jnp.int32, (CELLS + 2, rows, GROUP), 1)
        place_col = lax.broadcasted_iota(jnp.int32, (CELLS + 2, rows, GROUP), 0)
        start, end = (rows - inner) // 2, (rows + inner) // 2
        by_row = jnp.where(place_row == start - 1, top, jnp.where(place_row == end, bottom, 1.0))
        by_row = jnp.where(jnp.logical_and(place_row >= start - 1, place_row <= end), by_row, 0.0)
        by_col = jnp.where(place_col == 0, left, jnp.where(place_col == CELLS + 1, right, 1.0))
        return by_row * by_col

    def rolled(value):
        return pltpu.roll(value, value.shape[0] - 1, 0)

    x2 = jnp.concatenate([ext2[0:tall2, :], ext2[8 : tall2 + 8, 0:128]], axis=1).astype(BF16)
    tiled_store(v1, dot(x2, band12[1], 1, 1), pl.ds(0, tall2, stride=2))
    tiled_store(v1, dot(x2, band12[2], 1, 1) + rolled(dot(x2, band12[0], 1, 1)), pl.ds(1, tall2, stride=2))
    spread1 = jnp.concatenate([v1[tile] for tile in range(3)], axis=1)
    delta1 = ext1[...] + spread1.reshape(CELLS + 2, 16, GROUP)
    del1[...] = (delta1 * rim_mask(16, 8)).astype(BF16).astype(F32)

    x3 = jnp.concatenate([ext3[0:tall3, :], ext3[4 : tall3 + 4, 0:256]], axis=1).astype(BF16)
    tiled_store(v2, dot(x3, band23[1], 1, 1), pl.ds(0, tall3, stride=2))
    tiled_store(v2, dot(x3, band23[2], 1, 1) + rolled(dot(x3, band23[0], 1, 1)), pl.ds(1, tall3, stride=2))
    spread2 = jnp.concatenate([v2[tile] for tile in range(3)], axis=1)
    delta2 = ext2[0:tall2, :] + dot(p12[:, 0:192], band21[...]) + spread2
    del2[8 : 8 + tall2, :] = (delta2 * rim_mask(8, 4).reshape(tall2, GROUP)).astype(BF16).astype(F32)

    delta3 = ext3[0:tall3, :] + dot(p13[:, 0:96], band31[...]) + dot(p23, band32[...], 1, 1)
    place_row = lax.broadcasted_iota(jnp.int32, (tall3, GROUP), 0)
    in_group = jnp.bitwise_and(place_row, 3)
    by_row = jnp.where(in_group == 0, top, jnp.where(in_group == 3, bottom, 1.0))
    by_col = jnp.where(place_row < 4, left, jnp.where(place_row >= 4 * (CELLS + 1), right, 1.0))
    del3[8 : 8 + tall3, :] = (delta3 * (by_row * by_col)).astype(BF16).astype(F32)
    for ref in (del2, del3):
        ref[0:8, :] = jnp.zeros((8, GROUP), F32)
        ref[ref.shape[0] - 8 :, :] = jnp.zeros((8, GROUP), F32)

    reduction.along_x(3)

    def fold(grads, width, base, a, dst):
        total = None
        for n in range(GROUP // width):
            part = window(grads[n * width : (n + 1) * width, :], base + width * (n - 1), 3 * width)
            total = part if total is None else total + part
        for tap in range(3):
            start = (a * 3 + tap) * width
            tiled_store(dst, window(total, width * (2 - tap), width), slice(start, start + width))

    f3x = pad_f3[...].astype(BF16)
    back = None
    for a in range(3):
        at = 8 + 1 - a
        n = 4 * CELLS
        x3d = jnp.concatenate(
            [del3[at : at + n, 128:GROUP], del3[at + 4 : at + 4 + n, :], del3[at + 8 : at + 8 + n, 0:256]], axis=1
        ).astype(BF16)
        part = dot(x3d, band3[a], 1, 1)
        back = part if back is None else back + part
        fold(dot(f3x, x3d, 0, 0), 192, 256, a, w192)
    res3[...] = back
    for g in range(CELLS):
        g3_ref[:, lanes(g)] = res3[4 * g + 1 : 4 * g + 3, :].astype(BF16)

    settle((2,), (2, 1))

    f2x = pad_f2[...].astype(BF16)
    back = None
    for a in range(3):
        at = 8 + 1 - a
        n = 8 * CELLS
        x2d = jnp.concatenate(
            [del2[at : at + n, 256:GROUP], del2[at + 8 : at + 8 + n, :], del2[at + 16 : at + 16 + n, 0:128]], axis=1
        ).astype(BF16)
        part = dot(x2d, band2[a], 1, 1)
        back = part if back is None else back + part
        fold(dot(f2x, x2d, 0, 0), 96, 128, a, w96)
    res2[...] = back
    for g in range(CELLS):
        g2_ref[:, lanes(g)] = res2[8 * g + 2 : 8 * g + 6, :].astype(BF16)

    reduction.along_x(2)
    reduction.along_x(1)

    f1 = f1_ref[...]
    f1 = jnp.concatenate([f1[:, lanes(g)].astype(F32) for g in range(CELLS)], axis=0).astype(BF16)
    back = None
    for a in range(3):
        at = slice(5 - a, 13 - a)
        x1 = jnp.concatenate(
            [del1[0:CELLS, at, 256:GROUP], del1[1 : CELLS + 1, at, :], del1[2 : CELLS + 2, at, 0:128]], axis=2
        ).reshape(8 * CELLS, 640).astype(BF16)
        part = dot(x1, band1[a], 1, 1)
        back = part if back is None else back + part
        fold(dot(f1, x1, 0, 0), 48, 128, a, w48)
    for g in range(CELLS):
        g1_ref[:, lanes(g)] = back[8 * g : 8 * g + 8].astype(BF16)

    settle((0, 1), (0,))
    reduction.along_x(0)
    for block in (3, 2, 1, 0):
        reduction.along_y(block)
    reduction.plane_sum(reduce_refs[11])
    finish_shares(share_ref, *reduce_refs[11:])


def repeats(width, lanes, base=0):
    lane = np.arange(lanes)[None, :]
    return ((lane - base) % width == np.arange(width)[:, None]).astype(np.float32)


def pools(width, factors, parts):
    blocks = []
    for factor, lanes in zip(factors, parts):
        block = np.zeros((GROUP, lanes), np.float32)
        for lane in range(GROUP):
            block[lane, lane // (width * factor) * width + lane % width] = 1.0
        blocks.append(block)
    return np.concatenate(blocks, axis=1)


def local(f1, f2, f3, f4, o1, o2, o3, u1, u2, u3, k1, k2, k3, s12, s23, m21, m31, m41, m32, m42, m43):
    constants = [
        jnp.asarray(value, BF16)
        for value in (
            repeats(48, 640, 128), repeats(96, 640, 128), repeats(192, 896, 256), repeats(96, 512), repeats(192, 640),
            repeats(96, 384), repeats(192, 384),
            pools(48, (2, 4, 8), (256, 128, 128)), pools(96, (2, 4), (256, 128)), pools(192, (2,), (256,)),
        )
    ]
    whole = pl.BlockSpec(memory_space=pltpu.VMEM)
    inputs = [
        f1, f2, f3, f4, o1, o2, o3, u1, u2, u3,
        k1.reshape(432, 48), k2.reshape(864, 96), k3.reshape(1728, 192), s12.reshape(432, 96), s23.reshape(864, 192),
        m21.T, m31.T, m41.T, m32, m42.T, m43.T,
    ] + constants

    def f32(*shape):
        return pltpu.VMEM(shape, F32)

    def bf16(*shape):
        return pltpu.VMEM(shape, BF16)

    ext = CELLS + 2
    dma = pltpu.SemaphoreType.DMA
    packets = ((2, 16, CELLS * GROUP // 2), (2, 16, GROUP), (4, 16, GROUP))
    grad_one, grad_two, grad_three, grad_four, share = pl.pallas_call(
        backward_kernel,
        out_shape=[jax.ShapeDtypeStruct(value.shape, BF16) for value in (f1, f2, f3, f4)]
        + [jax.ShapeDtypeStruct((WINDOW, 128), F32)],
        in_specs=[whole] * len(inputs),
        out_specs=[whole] * 5,
        scratch_shapes=[
            bf16(128 * WINDOW, 128), *(bf16(*shape) for shape in packets + packets), dma((8,)), dma((8,)),
            f32(ext, 16, GROUP), f32(8 * ext + 8, GROUP), f32(4 * ext + 8, GROUP),
            f32(4, 16 * ext, 128), f32(3, 8 * ext, 128), f32(2, 4 * ext, 128),
            f32(ext, 16, GROUP), f32(8 * ext + 16, GROUP), f32(4 * ext + 16, GROUP),
            f32(8 * CELLS, GROUP), f32(4 * CELLS, GROUP), f32(3, 16 * CELLS, 128), f32(3, 8 * CELLS, 128),
            f32(4 * CELLS, GROUP), f32(CELLS, GROUP),
            bf16(3, GROUP, 640), bf16(3, GROUP, 640), bf16(3, GROUP, 896), bf16(3, GROUP, 512), bf16(3, GROUP, 640),
            bf16(192, GROUP), bf16(96, GROUP), bf16(GROUP, 256),
            f32(8 * CELLS, GROUP), f32(4 * CELLS, GROUP),
            f32(1, 1104, 128), f32(1, 1872, 128), f32(2, 2976, 128), f32(FLAT_ROWS, 128),
            bf16(4 * BLOCK, 128), bf16(4 * BLOCK, 128), bf16(12, PART, 128), bf16(4 * PART, 128), bf16(4, PART, 128),
            dma((4,)), dma((4,)), dma((12,)), dma((12,)), dma((4,)), dma((4,)),
            bf16(PART, 128), bf16(15, WINDOW, 128), f32(WINDOW, 128), f32(8, 128), f32(7, 8, 128), f32(8, 128), f32(15, 8, 128),
            dma((4,)), dma((15,)), dma((3,)), dma((1,)), dma((7,)), dma((7,)), dma((15,)), dma((15,)),
        ],
        compiler_params=pltpu.CompilerParams(
            collective_id=0, has_side_effects=True, vmem_limit_bytes=56 * 1024 * 1024
        ),
        name="backward",
    )(*inputs)
    offset = (SHARE * lax.axis_index(("row", "col"))) % 1024
    weight_grads = lax.dynamic_slice(share.reshape(WINDOW * 128), (offset,), (SHARE,))
    return grad_one, grad_two, grad_three, grad_four, weight_grads


def solution(mesh):
    in_specs = (
        P(("branch", "row"), "col"),
        P(("branch", "row"), "col"),
        P(("branch", "row"), "col"),
        P(("branch", "row"), "col"),
        P(("branch", "row"), "col"),
        P(("branch", "row"), "col"),
        P(("branch", "row"), "col"),
        P(("branch", "row"), "col"),
        P(("branch", "row"), "col"),
        P(("branch", "row"), "col"),
        P(),
        P(),
        P(),
        P(),
        P(),
        P(),
        P(),
        P(),
        P(),
        P(),
        P(),
    )
    out_specs = (
        P(("branch", "row"), "col"),
        P(("branch", "row"), "col"),
        P(("branch", "row"), "col"),
        P(("branch", "row"), "col"),
        P(("row", "col")),
    )
    return jax.shard_map(local, mesh=mesh, in_specs=in_specs, out_specs=out_specs, check_vma=False)
```

```python
import jax
import jax.numpy as jnp
import numpy as np
from jax import lax
from jax.experimental import pallas as pl
from jax.experimental.pallas import tpu as pltpu
from jax.sharding import PartitionSpec as P

EPSILON = 1e-06
MESH = pl.DeviceIdType.MESH
BF16 = jnp.bfloat16
F32 = jnp.float32
TOTAL = 804096
SHARE = 6282
WINDOW = 64
FLAT_ROWS = 6296


def share_place(share):
    row, col = divmod(share, 8)
    core, z_hi, y = row % 2, (row // 2) % 2, row // 4
    half, quarter = divmod(col, 4)
    return (((y * 2 + core) * 2 + z_hi) * 4 + quarter) * 2 + half


def pack_shares(flat_ref, packed_ref, block):
    for share in range(32 * block, 32 * block + 32):
        start = SHARE * share // 1024 * 8
        place = share_place(share) * WINDOW
        packed_ref[place : place + WINDOW, :] = flat_ref[start : start + WINDOW, :].astype(jnp.bfloat16)


BLOCK = 16 * WINDOW
HALF = 8 * WINDOW
PART = 2 * WINDOW


class Reduction:
    def __init__(self, packed, where, from_core, sum_core, x_first, sum_x, y_second, y_first, sum_y, x_second, sems):
        self.packed, self.where, self.from_core, self.sum_core = packed, where, from_core, sum_core
        self.x_first, self.sum_x, self.y_second = x_first, sum_x, y_second
        self.y_first, self.sum_y, self.x_second = y_first, sum_y, x_second
        self.sems = sems

    def core_copy(self, block):
        x, row, col = self.where
        start = pl.multiple_of((block * 2 + 1 - row % 2) * BLOCK, BLOCK)
        send, recv = self.sems[0:2]
        return remote(
            self.packed.at[pl.ds(start, BLOCK)], self.from_core.at[pl.ds(block * BLOCK, BLOCK)],
            send.at[block], recv.at[block], (x, row + 1 - 2 * (row % 2), col),
        )

    def x_first_copy(self, block, step):
        x, row, col = self.where
        there = (x + step) % 4
        start = pl.multiple_of(block * BLOCK + there * PART, PART)
        slot = block * 3 + step - 1
        send, recv = self.sems[2:4]
        return remote(
            self.sum_core.at[pl.ds(start, PART)], self.x_first.at[slot], send.at[slot], recv.at[slot], (there, row, col)
        )

    def y_first_copy(self, block):
        x, row, col = self.where
        step = (block - row // 4 + 4) % 4
        send, recv = self.sems[4:6]
        return remote(
            self.sum_core.at[pl.ds(block * BLOCK + HALF, HALF)], self.y_first.at[step], send.at[step], recv.at[step],
            (x, block * 4 + row % 4, col),
        )

    def y_second_copy(self, block):
        x, row, col = self.where
        step = (block - row // 4 + 4) % 4
        send, recv = self.sems[6:8]
        return remote(
            self.sum_x.at[pl.ds(block * PART, PART)], self.y_second.at[step], send.at[step], recv.at[step],
            (x, block * 4 + row % 4, col),
        )

    def x_second_copy(self, step):
        x, row, col = self.where
        there = (x + step) % 4
        send, recv = self.sems[8:10]
        return remote(
            self.sum_y.at[pl.ds(pl.multiple_of(there * PART, PART), PART)], self.x_second.at[step - 1],
            send.at[step - 1], recv.at[step - 1], (there, row, col),
        )

    def leave(self, block):
        self.core_copy(block).start()

    def spread(self, block):
        core, y = self.where[1] % 2, self.where[1] // 4
        self.core_copy(block).wait()
        for half in range(2):

            @pl.loop(0, 2)
            def _(part):
                mine = pl.multiple_of((block * 2 + core) * BLOCK + half * HALF + part * (HALF // 2), HALF // 2)
                place = pl.multiple_of(block * BLOCK + half * HALF + part * (HALF // 2), HALF // 2)
                total = self.packed[pl.ds(mine, HALF // 2), :].astype(F32)
                total = total + self.from_core[pl.ds(place, HALF // 2), :].astype(F32)
                self.sum_core[pl.ds(place, HALF // 2), :] = total.astype(BF16)

            if half == 0:
                for step in range(1, 4):
                    self.x_first_copy(block, step).start()
            else:

                @pl.when(y != block)
                def _():
                    self.y_first_copy(block).start()

    def turn_to_y(self, block):
        x, row, col = self.where
        for step in range(1, 4):
            self.x_first_copy(block, step).wait()
        own = pl.multiple_of(block * BLOCK + x * PART, PART)
        total = self.sum_core[pl.ds(own, PART), :].astype(F32)
        for step in range(3):
            total = total + self.x_first[block * 3 + step].astype(F32)
        self.sum_x[block * PART : (block + 1) * PART, :] = total.astype(BF16)

        @pl.when(row // 4 != block)
        def _():
            self.y_second_copy(block).start()

    def waiting(self, src, slots, step, sems):
        send, recv = sems
        return remote(src, slots.at[step], send.at[step], recv.at[step], self.where)

    def turn_to_x(self):
        y = self.where[1] // 4
        for step in range(1, 4):
            self.waiting(self.sum_core.at[pl.ds(0, HALF)], self.y_first, step, self.sems[4:6]).wait_recv()

        @pl.loop(0, 4)
        def _(part):
            own = pl.multiple_of(y * BLOCK + HALF + part * PART, PART)
            at = pl.ds(pl.multiple_of(part * PART, PART), PART)
            total = self.sum_core[pl.ds(own, PART), :].astype(F32)
            for step in range(1, 4):
                total = total + self.y_first[step, at, :].astype(F32)
            self.sum_y[at, :] = total.astype(BF16)

        for step in range(1, 4):
            self.x_second_copy(step).start()

    def plane_sum(self, sum_plane):
        x, y = self.where[0], self.where[1] // 4
        for step in range(1, 4):
            self.waiting(self.sum_x.at[pl.ds(0, PART)], self.y_second, step, self.sems[6:8]).wait_recv()
        total = self.sum_x[pl.ds(pl.multiple_of(y * PART, PART), PART), :].astype(F32)
        for step in range(1, 4):
            total = total + self.y_second[step].astype(F32)
        sum_plane[0:PART, :] = total.astype(BF16)
        for step in range(1, 4):
            self.x_second_copy(step).wait()
        total = self.sum_y[pl.ds(pl.multiple_of(x * PART, PART), PART), :].astype(F32)
        for step in range(3):
            total = total + self.x_second[step].astype(F32)
        sum_plane[PART:, :] = total.astype(BF16)

    def close(self):
        for step in range(1, 4):
            self.waiting(self.sum_core.at[pl.ds(0, HALF)], self.y_first, step, self.sems[4:6]).wait_send()
            self.waiting(self.sum_x.at[pl.ds(0, PART)], self.y_second, step, self.sems[6:8]).wait_send()


def remote(src, dst, send_sem, recv_sem, peer):
    return pltpu.make_async_remote_copy(
        src_ref=src, dst_ref=dst, send_sem=send_sem, recv_sem=recv_sem, device_id=peer, device_id_type=MESH
    )


def finish_shares(
    out_ref,
    sum_plane,
    from_line,
    share_buf,
    square_buf,
    from_far,
    far_buf,
    from_plane,
    line_send,
    line_recv,
    share_send,
    share_recv,
    far_send,
    far_recv,
    plane_send,
    plane_recv,
):
    x = lax.axis_index("branch")
    row = lax.axis_index("row")
    col = lax.axis_index("col")
    core, z_hi, y = row % 2, (row // 2) % 2, row // 4
    z = z_hi * 8 + col
    partner = (x, row + 1 - 2 * core, col)

    def line_peer(step):
        there = (z + step) % 16
        return (x, y * 4 + (there // 8) * 2 + core, there % 8)

    def plane_peer(step):
        there = (x * 8 + y * 2 + core + step) % 32
        return (there // 8, (there % 8) // 2 * 4 + z_hi * 2 + there % 2, col)

    def far_copy(step):
        return remote(square_buf, from_far.at[step - 1], far_send.at[step - 1], far_recv.at[step - 1], line_peer(step))

    def line_copy(block):
        target = (block // 2) * 8 + (block % 2) * 4 + x
        step = (z - target + 16) % 16
        slot = (step + 15) % 16
        return step, remote(
            sum_plane.at[pl.ds(pl.multiple_of(block * WINDOW, WINDOW), WINDOW)],
            from_line.at[slot], line_send.at[block], line_recv.at[slot],
            (x, y * 4 + (target // 8) * 2 + core, target % 8),
        )

    for block in range(4):
        step, copy = line_copy(block)

        @pl.when(step != 0)
        def _():
            copy.start()

    owner_x = col % 4
    owner = owner_x == x

    def share_copy(step):
        return remote(
            share_buf, share_buf, share_send.at[step - 1], share_recv.at[0],
            ((x + step) % 4, row, col),
        )

    @pl.when(owner)
    def _():
        @pl.loop(0, 15)
        def _(slot):
            remote(
                sum_plane.at[pl.ds(0, WINDOW)], from_line.at[slot], line_send.at[0], line_recv.at[slot], partner
            ).wait_recv()

        own = pl.multiple_of((z_hi * 2 + col // 4) * WINDOW, WINDOW)
        total = sum_plane[pl.ds(own, WINDOW), :].astype(jnp.float32)
        for slot in range(15):
            total = total + from_line[slot].astype(jnp.float32)
        share_buf[...] = total
        offset = (SHARE * (row * 8 + col)) % 1024
        place = lax.broadcasted_iota(jnp.int32, (WINDOW, 128), 0) * 128 + lax.broadcasted_iota(
            jnp.int32, (WINDOW, 128), 1
        )
        inside = jnp.logical_and(place >= offset, place < offset + SHARE)
        square_buf[...] = jnp.where(inside, total * total, 0.0).reshape(8, 8, 128).sum(axis=0)

        @pl.loop(1, 16)
        def _(step):
            far_copy(step).start()

        for step in range(1, 4):
            share_copy(step).start()

    @pl.when(jnp.logical_not(owner))
    def _():
        square_buf[...] = jnp.zeros((8, 128), F32)

    far_buf[...] = square_buf[...]
    for index in range(4):
        source = 4 * index + x
        step = (z - source + 16) % 16

        @pl.when(step != 0)
        def _():
            slot = (step + 15) % 16
            remote(square_buf, from_far.at[slot], far_send.at[0], far_recv.at[slot], partner).wait_recv()
            far_buf[...] += from_far[slot]

    def plane_copy(step):
        return remote(far_buf, from_plane.at[step - 1], plane_send.at[step - 1], plane_recv.at[step - 1], plane_peer(step))

    @pl.loop(1, 32)
    def _(step):
        plane_copy(step).start()

    @pl.when(jnp.logical_not(owner))
    def _():
        share_copy(1).wait_recv()

    @pl.loop(1, 32)
    def _(step):
        plane_copy(step).wait()

    total_squares = jnp.sum(far_buf[...] + from_plane[...].sum(axis=0), keepdims=True)
    spread_rms = jnp.sqrt(total_squares / TOTAL + EPSILON)
    out_ref[...] = share_buf[...] * jnp.minimum(jnp.float32(1.0), 1.0 / spread_rms)

    for block in range(4):
        step, copy = line_copy(block)

        @pl.when(step != 0)
        def _():
            copy.wait_send()

    @pl.when(owner)
    def _():
        @pl.loop(1, 16)
        def _(step):
            far_copy(step).wait_send()

        for step in range(1, 4):
            share_copy(step).wait_send()


GROUP = 384
LATE = 28
CELLS = 24
PIECES = (
    (48, 0, 0, 432), (96, 162, 0, 864), (192, 810, 0, 1728), (96, 3402, 864, 432), (192, 3726, 1728, 864),
    (48, 5022, 432, 96), (48, 5058, 528, 192), (48, 5130, 720, 384), (96, 5274, 1296, 192),
    (96, 5418, 1488, 384), (192, 5706, 2592, 384),
)


def dot(left, right, left_dim=1, right_dim=0):
    return lax.dot_general(left, right, (((left_dim,), (right_dim,)), ((), ())), preferred_element_type=F32)


def lanes_of(rows, lanes):
    return lax.broadcasted_iota(jnp.int32, (rows, lanes), 1)


def packet_rows(up):
    maps = (
        (0, 3, 16, (11, 4), (3, 12)), (1, 3, 8, (5, 2), (1, 6)), (2, 3, 4, (2, 1), (0, 3)),
        (3, 2, 8, (5, 2), (1, 6)), (4, 1, 4, (2, 1), (0, 3)), (5, 2, 4, (2, 1), (0, 3)),
    )
    return [
        (index, tile, rows, leaves[up], lands[up]) for index, tiles, rows, leaves, lands in maps for tile in range(tiles)
    ]


def fill_packets(maps, send_rows, send_corners):
    for up in range(2):
        parts = [
            maps[index][tile, pl.ds(rows + leaves, CELLS, stride=rows), :]
            for index, tile, rows, leaves, lands in packet_rows(up)
        ]
        send_rows[up] = jnp.concatenate(parts, axis=0).astype(BF16)
        blank = [jnp.zeros((2, 128), F32)]
        send_corners[2 * up] = jnp.concatenate([part[CELLS - 1 : CELLS] for part in parts] + blank, axis=0).astype(BF16)
        send_corners[2 * up + 1] = jnp.concatenate([part[0:1] for part in parts] + blank, axis=0).astype(BF16)


def fill_sides(u1, u2, u3, send_sides):
    for index, start in enumerate(((CELLS - 1) * GROUP, 0)):
        parts = [value[:, start : start + GROUP] for value in (u1, u2, u3)] + [jnp.zeros((2, GROUP), F32)]
        send_sides[index] = jnp.concatenate(parts, axis=0).astype(BF16)


def banded(weights, repeat, width, rows, blocks, dst):
    wide = dot(weights, repeat)
    lane = lanes_of(rows, repeat.shape[1])
    for block, pieces in enumerate(blocks):
        value = jnp.zeros((rows, repeat.shape[1]), F32)
        for tap, start in pieces:
            inside = jnp.logical_and(lane >= start, lane < start + width)
            value = jnp.where(inside, wide[tap * rows : (tap + 1) * rows], value)
        dst[block * rows : (block + 1) * rows, :] = value.astype(BF16)


def conv_blocks(width, base):
    return [[(tap, base + width * (n + 1 - tap)) for tap in range(3)] for n in range(GROUP // width)]


def down_blocks(width):
    blocks = []
    for j in range(2 * (GROUP // width)):
        if j % 2 == 0:
            blocks.append([(1, width * (j // 2))])
        else:
            blocks.append([(2, width * (j // 2)), (0, width * (j // 2 + 1))])
    return blocks


def mixer_blocks(width, count):
    return [[(0, width * j)] for j in range(count)]


def window(value, start, width):
    first, end = start // 128, -(-(start + width) // 128)
    part = value[:, first * 128 : end * 128]
    shift = start - first * 128
    if shift:
        part = pltpu.roll(part, (end - first) * 128 - shift, 1)
    return part[:, : -(-width // 128) * 128]


def place(src, flat, width, flat_base, src_base, count):
    stride = GROUP // width
    rows = count // stride
    lane = lanes_of(rows, 128)
    held = {}
    for tile in range(3):
        value = None
        for j in range(stride):
            for part in range(-(-width // 128)):
                low = max(width * j + 128 * part, 128 * tile)
                high = min(width * j + min(width, 128 * part + 128), 128 * tile + 128)
                if low >= high:
                    continue
                if (j, part) not in held:
                    held[j, part] = src[part, pl.ds(src_base + j, rows, stride=stride), :]
                piece = held[j, part]
                shift = (width * j + 128 * part - 128 * tile) % 128
                if shift:
                    piece = pltpu.roll(piece, shift, 1)
                value = piece if value is None else jnp.where(lane >= low - 128 * tile, piece, value)
        flat[pl.ds(flat_base + tile, rows, stride=3), :] = value


def backward_kernel(
    u1_ref, u2_ref, u3_ref, *refs,
):
    far = refs[:LATE]
    outs, near, (late_sems, *rest) = refs[LATE : LATE + 5], refs[LATE + 5 : 2 * LATE + 5], refs[2 * LATE + 5 :]
    copies = [pltpu.make_async_copy(src, dst, late_sems.at[i]) for i, (src, dst) in enumerate(zip(far, near))]
    for copy in copies:
        copy.start()
    backward_stages(copies, u1_ref, u2_ref, u3_ref, *near, *outs, *rest)


def backward_stages(
    late_copies, u1_ref, u2_ref, u3_ref, f1_ref, f2_ref, f3_ref, f4_ref, o1_ref, o2_ref, o3_ref,
    k1_ref, k2_ref, k3_ref, s12_ref, s23_ref, m21_ref, m31_ref, m41_ref, m32_ref, m42_ref, m43_ref,
    rep1_ref, rep2_ref, rep3_ref, rep12_ref, rep23_ref, rep96_ref, rep192_ref, pool1_ref, pool2_ref, pool3_ref,
    g1_ref, g2_ref, g3_ref, g4_ref, share_ref,
    packed_ref, send_rows, send_sides, send_corners, recv_rows, recv_sides, recv_corners, halo_send, halo_recv,
    ext1, ext2, ext3, pp12, pp13, pp23, v1, v2, v3, del1, del2, del3, pad_f2, pad_f3, pad_o1, pad_o2, pad_o3, rows_f4,
    band1, band2, band3, band12, band23, band21, band31, band32, res2, res3, w48, w96, w192, flat, *reduce_refs,
):
    def lanes(g):
        return slice(GROUP * g, GROUP * (g + 1))

    x = lax.axis_index("branch")
    row = lax.axis_index("row")
    col = lax.axis_index("col")
    core, z_hi, y = row % 2, (row // 2) % 2, row // 4
    z = z_hi * 8 + col
    line = x * 16 + row

    def peer(down, right):
        there = (line + down + 64) % 64
        return (there // 16, there % 16, (col + right + 8) % 8)

    routes = (
        (0, 1, 0, send_rows.at[0], recv_rows.at[0]),
        (1, -1, 0, send_rows.at[1], recv_rows.at[1]),
        (2, 0, 1, send_sides.at[0], recv_sides.at[0]),
        (3, 0, -1, send_sides.at[1], recv_sides.at[1]),
        (4, 1, 1, send_corners.at[0], recv_corners.at[0]),
        (5, 1, -1, send_corners.at[1], recv_corners.at[1]),
        (6, -1, 1, send_corners.at[2], recv_corners.at[2]),
        (7, -1, -1, send_corners.at[3], recv_corners.at[3]),
    )

    def line_peer(step):
        there = (z + step) % 16
        return (x, y * 4 + (there // 8) * 2 + core, there % 8)

    def plane_peer(step):
        there = (x * 8 + y * 2 + core + step) % 32
        return (there // 8, (there % 8) // 2 * 4 + z_hi * 2 + there % 2, col)

    def greet(peer):
        pl.semaphore_signal(barrier, inc=1, device_id=peer, device_id_type=MESH)

    barrier = pltpu.get_barrier_semaphore()
    for route in routes:
        greet(peer(route[1], route[2]))
    @pl.loop(1, 16)
    def _(step):
        greet(line_peer(step))

    @pl.loop(1, 32)
    def _(step):
        greet(plane_peer(step))

    u1, u2, u3 = (ref[...].astype(F32) for ref in (u1_ref, u2_ref, u3_ref))
    fill_sides(u1, u2, u3, send_sides)
    for ref in (ext1, ext2, ext3):
        ref[...] = jnp.zeros_like(ref)
    for g in range(CELLS):
        for tile in range(3):
            part = slice(GROUP * g + 128 * tile, GROUP * g + 128 * tile + 128)
            ext1[tile, 16 * g + 20 : 16 * g + 28, :] = u1[:, part]
            ext2[tile, 8 * g + 10 : 8 * g + 14, :] = u2[:, part]
            ext3[tile, 4 * g + 5 : 4 * g + 7, :] = u3[:, part]

    for copy in late_copies:
        copy.wait()

    tall1, tall2, tall3 = 16 * (CELLS + 2), 8 * (CELLS + 2), 4 * (CELLS + 2)
    def tiled_store(ref, value, rows=slice(None)):
        for tile in range(value.shape[1] // 128):
            ref[tile, rows, :] = value[:, 128 * tile : 128 * tile + 128]

    def strided(ref, tiles, start, count, stride):
        parts = [ref[tile, pl.ds(start, count, stride=stride), :] for tile in tiles]
        return parts[0] if len(parts) == 1 else jnp.concatenate(parts, axis=1)

    def strided_sum(ref, picks, count, stride, tiles):
        total = None
        for pick in picks:
            piece = strided(ref, tiles, pick, count, stride)
            total = piece if total is None else total + piece
        return total

    def whole_of(ref, rows):
        return jnp.concatenate([ref[tile, rows, :] for tile in range(ref.shape[0])], axis=1)

    def run_pools():
        tiled_store(v1, dot(whole_of(ext1, slice(0, tall1)).astype(BF16), pool1_ref[...]))
        tiled_store(v2, dot(whole_of(ext2, slice(0, tall2)).astype(BF16), pool2_ref[...]))
        tiled_store(pp12, strided_sum(v1, range(2), tall2, 2, (0, 1)))
        tiled_store(pp13, strided_sum(v1, range(4), tall3, 4, (2,)))
        tiled_store(pp23, strided_sum(v2, range(2), tall3, 2, (0, 1)))

    def pooled():
        return (
            whole_of(pp12, slice(0, tall2)).astype(BF16),
            whole_of(pp13, slice(0, tall3)).astype(BF16),
            whole_of(pp23, slice(0, tall3)).astype(BF16),
        )

    run_pools()
    tiled_store(v3, dot(whole_of(ext3, slice(0, tall3)).astype(BF16), pool3_ref[...]))
    p14 = strided_sum(v1, range(16 + 4, 16 + 12), CELLS, 16, (3,)).astype(BF16)
    p24 = strided_sum(v2, range(8 + 2, 8 + 6), CELLS, 8, (2,)).astype(BF16)
    p34 = strided_sum(v3, range(4 + 1, 4 + 3), CELLS, 4, (0, 1)).astype(BF16)
    p12, p13, p23 = pooled()
    fill_packets((ext1, ext2, ext3, pp12, pp13, pp23), send_rows, send_corners)
    pl.semaphore_wait(barrier, 54)

    def halo_copy(route):
        slot, down, right, src, dst = route
        return pltpu.make_async_remote_copy(
            src_ref=src, dst_ref=dst, send_sem=halo_send.at[slot], recv_sem=halo_recv.at[slot],
            device_id=peer(down, right), device_id_type=MESH,
        )

    for route in routes:
        halo_copy(route).start()

    for ref in (pad_f2, pad_f3, pad_o1, pad_o2, pad_o3):
        ref[...] = jnp.zeros_like(ref)
    f2, f3, o1, o2, o3, f4 = (ref[...].astype(F32) for ref in (f2_ref, f3_ref, o1_ref, o2_ref, o3_ref, f4_ref))
    for g in range(CELLS):
        at = lanes(g)
        pad_f2[8 * g + 2 : 8 * g + 6, :] = f2[:, at]
        pad_f3[4 * g + 1 : 4 * g + 3, :] = f3[:, at]
        for tile in range(3):
            part = slice(GROUP * g + 128 * tile, GROUP * g + 128 * tile + 128)
            pad_o1[tile, 16 * g + 4 : 16 * g + 12, :] = o1[:, part]
            pad_o2[tile, 8 * g + 2 : 8 * g + 6, :] = o2[:, part]
        pad_o3[4 * g + 1 : 4 * g + 3, :] = o3[:, at]
        rows_f4[g : g + 1, :] = f4[:, at]

    for a in range(3):
        banded(k1_ref[144 * a : 144 * a + 144, :], rep1_ref[...], 48, 48, conv_blocks(48, 128), band1.at[a])
        banded(k2_ref[288 * a : 288 * a + 288, :], rep2_ref[...], 96, 96, conv_blocks(96, 128), band2.at[a])
        banded(k3_ref[576 * a : 576 * a + 576, :], rep3_ref[...], 192, 192, conv_blocks(192, 256), band3.at[a])
        banded(s12_ref[144 * a : 144 * a + 144, :], rep12_ref[...], 96, 48, down_blocks(96), band12.at[a])
        banded(s23_ref[288 * a : 288 * a + 288, :], rep23_ref[...], 192, 96, down_blocks(192), band23.at[a])
    banded(m21_ref[...], rep96_ref[...], 96, 48, mixer_blocks(96, 4), band21)
    banded(m31_ref[...], rep192_ref[...], 192, 48, mixer_blocks(192, 2), band31)
    banded(m32_ref[...], rep96_ref[:, :256], 96, 192, mixer_blocks(96, 2), band32)

    def fold_mixer(grads, width, rows, base, dst):
        total = None
        for j in range(GROUP // rows):
            part = window(grads[j * rows : (j + 1) * rows, :], width * j, width)
            total = part if total is None else total + part
        tiled_store(dst, total, slice(base, base + rows))

    o2x = jnp.concatenate([pad_o2[tile] for tile in range(3)], axis=1).astype(BF16)
    o3x = pad_o3[...].astype(BF16)
    f4x = rows_f4[...].astype(BF16)
    inner2, inner3 = slice(8, 8 + 8 * CELLS), slice(4, 4 + 4 * CELLS)
    fold_mixer(dot(o2x, p12[inner2], 0, 0), 48, 96, 432, w48)
    fold_mixer(dot(o3x, p13[inner3], 0, 0), 48, 192, 528, w48)
    fold_mixer(dot(f4x, p14, 0, 0), 48, 384, 720, w48)
    fold_mixer(dot(o3x, p23[inner3], 0, 0), 96, 192, 1296, w96)
    fold_mixer(dot(f4x, p24, 0, 0), 96, 384, 1488, w96)
    fold_mixer(dot(f4x, p34, 0, 0), 192, 384, 2592, w192)
    back4 = (
        dot(p14[:, 0:48], m41_ref[...]) + dot(p24[:, 0:96], m42_ref[...]) + dot(p34[:, 0:192], m43_ref[...])
    )
    for g in range(CELLS):
        g4_ref[:, lanes(g)] = back4[g : g + 1].astype(BF16)

    for route in routes:
        halo_copy(route).wait()
    top, bottom = jnp.where(line > 0, 1.0, 0.0), jnp.where(line < 63, 1.0, 0.0)
    left, right = jnp.where(col > 0, 1.0, 0.0), jnp.where(col < 7, 1.0, 0.0)
    sides = [recv_sides[0].astype(F32) * left, recv_sides[1].astype(F32) * right]
    corners = [
        recv_corners[0].astype(F32) * (top * left), recv_corners[1].astype(F32) * (top * right),
        recv_corners[2].astype(F32) * (bottom * left), recv_corners[3].astype(F32) * (bottom * right),
    ]
    for index, group in enumerate((0, CELLS + 1)):
        for tile in range(3):
            part = sides[index][:, 128 * tile : 128 * tile + 128]
            ext1[tile, 16 * group + 4 : 16 * group + 12, :] = part[0:8]
            ext2[tile, 8 * group + 2 : 8 * group + 6, :] = part[8:12]
            ext3[tile, 4 * group + 1 : 4 * group + 3, :] = part[12:14]

    def fill_rims(refs, first):
        for up, flag in enumerate((top, bottom)):
            packet = recv_rows[up].astype(F32) * flag
            for place_in, (index, tile, rows, leaves, lands) in enumerate(packet_rows(up)):
                if not first <= index < first + 3:
                    continue
                ref = refs[index - first]
                part = packet[CELLS * place_in : CELLS * (place_in + 1)]
                ref[tile, pl.ds(rows + lands, CELLS, stride=rows), :] = part
                ref[tile, lands : lands + 1, :] = corners[2 * up][place_in : place_in + 1]
                last = rows * (CELLS + 1) + lands
                ref[tile, last : last + 1, :] = corners[2 * up + 1][place_in : place_in + 1]

    fill_rims((ext1, ext2, ext3), 0)
    run_pools()
    fill_rims((pp12, pp13, pp23), 3)
    p12, p13, p23 = pooled()

    def fold_down(grads, width, rows, a, base, dst):
        for b in range(3):
            total = None
            for j in range(1 if b != 1 else 0, 2 * (GROUP // width), 2):
                p = (j + 1 - b) // 2
                part = window(grads[j * rows : (j + 1) * rows, :], width * p, width)
                total = part if total is None else total + part
            start = base + (a * 3 + b) * rows
            tiled_store(dst, total, slice(start, start + rows))

    def down_grads(saved, ext, skip, count, head, width, rows, base, dst):
        even = strided(saved, range(3), 0, count, 2).astype(BF16)
        odd = strided(saved, range(3), 1, count, 2).astype(BF16)
        for a in range(3):
            at = skip + (1 if a == 0 else 0)
            xs = jnp.concatenate(
                [ext[tile, at : at + count, :] for tile in range(3)]
                + [ext[tile, at + skip : at + skip + count, :] for tile in range(head // 128)],
                axis=1,
            ).astype(BF16)
            fold_down(dot(even if a == 1 else odd, xs, 0, 0), width, rows, a, base, dst)

    down_grads(pad_o1, ext2, 8, 8 * CELLS, 128, 96, 48, 864, w96)
    down_grads(pad_o2, ext3, 4, 4 * CELLS, 256, 192, 96, 1728, w192)

    reduction = Reduction(packed_ref, (x, row, col), *reduce_refs[:8], reduce_refs[8:18])
    flat[6282:FLAT_ROWS, :] = jnp.zeros((FLAT_ROWS - 6282, 128), F32)

    def settle(pieces, blocks):
        for piece in pieces:
            width, flat_base, src_base, count = PIECES[piece]
            place({48: w48, 96: w96, 192: w192}[width], flat, width, flat_base, src_base, count)
        for block in blocks:
            pack_shares(flat, packed_ref, block)
            reduction.leave(block)

    settle((3, 4, 5, 6, 7, 8, 9, 10), (3,))

    def rim_mask(rows, inner):
        place_row = lax.broadcasted_iota(jnp.int32, (CELLS + 2, rows, GROUP), 1)
        place_col = lax.broadcasted_iota(jnp.int32, (CELLS + 2, rows, GROUP), 0)
        start, end = (rows - inner) // 2, (rows + inner) // 2
        by_row = jnp.where(place_row == start - 1, top, jnp.where(place_row == end, bottom, 1.0))
        by_row = jnp.where(jnp.logical_and(place_row >= start - 1, place_row <= end), by_row, 0.0)
        by_col = jnp.where(place_col == 0, left, jnp.where(place_col == CELLS + 1, right, 1.0))
        return by_row * by_col

    def rolled(value):
        return pltpu.roll(value, value.shape[0] - 1, 0)

    x2 = jnp.concatenate([whole_of(ext2, slice(0, tall2)), ext2[0, 8 : tall2 + 8, :]], axis=1).astype(BF16)
    tiled_store(v1, dot(x2, band12[1], 1, 1), pl.ds(0, tall2, stride=2))
    tiled_store(v1, dot(x2, band12[2], 1, 1) + rolled(dot(x2, band12[0], 1, 1)), pl.ds(1, tall2, stride=2))
    spread1 = jnp.concatenate([v1[tile] for tile in range(3)], axis=1)
    delta1 = (whole_of(ext1, slice(0, tall1)) + spread1).reshape(CELLS + 2, 16, GROUP)
    del1[...] = (delta1 * rim_mask(16, 8)).astype(BF16).astype(F32)

    x3 = jnp.concatenate(
        [whole_of(ext3, slice(0, tall3)), ext3[0, 4 : tall3 + 4, :], ext3[1, 4 : tall3 + 4, :]], axis=1
    ).astype(BF16)
    tiled_store(v2, dot(x3, band23[1], 1, 1), pl.ds(0, tall3, stride=2))
    tiled_store(v2, dot(x3, band23[2], 1, 1) + rolled(dot(x3, band23[0], 1, 1)), pl.ds(1, tall3, stride=2))
    spread2 = jnp.concatenate([v2[tile] for tile in range(3)], axis=1)
    delta2 = whole_of(ext2, slice(0, tall2)) + dot(p12[:, 0:192], band21[...]) + spread2
    del2[8 : 8 + tall2, :] = (delta2 * rim_mask(8, 4).reshape(tall2, GROUP)).astype(BF16).astype(F32)

    delta3 = whole_of(ext3, slice(0, tall3)) + dot(p13[:, 0:96], band31[...]) + dot(p23, band32[...], 1, 1)
    place_row = lax.broadcasted_iota(jnp.int32, (tall3, GROUP), 0)
    in_group = jnp.bitwise_and(place_row, 3)
    by_row = jnp.where(in_group == 0, top, jnp.where(in_group == 3, bottom, 1.0))
    by_col = jnp.where(place_row < 4, left, jnp.where(place_row >= 4 * (CELLS + 1), right, 1.0))
    del3[8 : 8 + tall3, :] = (delta3 * (by_row * by_col)).astype(BF16).astype(F32)
    for ref in (del2, del3):
        ref[0:8, :] = jnp.zeros((8, GROUP), F32)
        ref[ref.shape[0] - 8 :, :] = jnp.zeros((8, GROUP), F32)

    reduction.spread(3)

    def fold(grads, width, base, a, dst):
        total = None
        for n in range(GROUP // width):
            part = window(grads[n * width : (n + 1) * width, :], base + width * (n - 1), 3 * width)
            total = part if total is None else total + part
        for tap in range(3):
            start = (a * 3 + tap) * width
            tiled_store(dst, window(total, width * (2 - tap), width), slice(start, start + width))

    f3x = pad_f3[...].astype(BF16)
    back = None
    for a in range(3):
        at = 8 + 1 - a
        n = 4 * CELLS
        x3d = jnp.concatenate(
            [del3[at : at + n, 128:GROUP], del3[at + 4 : at + 4 + n, :], del3[at + 8 : at + 8 + n, 0:256]], axis=1
        ).astype(BF16)
        part = dot(x3d, band3[a], 1, 1)
        back = part if back is None else back + part
        fold(dot(f3x, x3d, 0, 0), 192, 256, a, w192)
    res3[...] = back
    for g in range(CELLS):
        g3_ref[:, lanes(g)] = res3[4 * g + 1 : 4 * g + 3, :].astype(BF16)

    settle((2,), (2, 1))

    f2x = pad_f2[...].astype(BF16)
    back = None
    for a in range(3):
        at = 8 + 1 - a
        n = 8 * CELLS
        x2d = jnp.concatenate(
            [del2[at : at + n, 256:GROUP], del2[at + 8 : at + 8 + n, :], del2[at + 16 : at + 16 + n, 0:128]], axis=1
        ).astype(BF16)
        part = dot(x2d, band2[a], 1, 1)
        back = part if back is None else back + part
        fold(dot(f2x, x2d, 0, 0), 96, 128, a, w96)
    res2[...] = back
    for g in range(CELLS):
        g2_ref[:, lanes(g)] = res2[8 * g + 2 : 8 * g + 6, :].astype(BF16)

    reduction.spread(2)
    reduction.spread(1)

    f1 = f1_ref[...]
    f1 = jnp.concatenate([f1[:, lanes(g)].astype(F32) for g in range(CELLS)], axis=0).astype(BF16)
    back = None
    for a in range(3):
        at = slice(5 - a, 13 - a)
        x1 = jnp.concatenate(
            [del1[0:CELLS, at, 256:GROUP], del1[1 : CELLS + 1, at, :], del1[2 : CELLS + 2, at, 0:128]], axis=2
        ).reshape(8 * CELLS, 640).astype(BF16)
        part = dot(x1, band1[a], 1, 1)
        back = part if back is None else back + part
        fold(dot(f1, x1, 0, 0), 48, 128, a, w48)
    for g in range(CELLS):
        g1_ref[:, lanes(g)] = back[8 * g : 8 * g + 8].astype(BF16)

    settle((0, 1), (0,))
    reduction.spread(0)
    for block in (3, 2, 1, 0):
        reduction.turn_to_y(block)
    reduction.turn_to_x()
    reduction.plane_sum(reduce_refs[18])
    finish_shares(share_ref, *reduce_refs[18:])
    reduction.close()


def repeats(width, lanes, base=0):
    lane = np.arange(lanes)[None, :]
    return ((lane - base) % width == np.arange(width)[:, None]).astype(np.float32)


def pools(width, factors, parts):
    blocks = []
    for factor, lanes in zip(factors, parts):
        block = np.zeros((GROUP, lanes), np.float32)
        for lane in range(GROUP):
            block[lane, lane // (width * factor) * width + lane % width] = 1.0
        blocks.append(block)
    return np.concatenate(blocks, axis=1)


def local(f1, f2, f3, f4, o1, o2, o3, u1, u2, u3, k1, k2, k3, s12, s23, m21, m31, m41, m32, m42, m43):
    constants = [
        jnp.asarray(value, BF16)
        for value in (
            repeats(48, 640, 128), repeats(96, 640, 128), repeats(192, 896, 256), repeats(96, 512), repeats(192, 640),
            repeats(96, 384), repeats(192, 384),
            pools(48, (2, 4, 8), (256, 128, 128)), pools(96, (2, 4), (256, 128)), pools(192, (2,), (256,)),
        )
    ]
    whole = pl.BlockSpec(memory_space=pltpu.VMEM)
    inputs = [
        u1, u2, u3, f1, f2, f3, f4, o1, o2, o3,
        k1.reshape(432, 48), k2.reshape(864, 96), k3.reshape(1728, 192), s12.reshape(432, 96), s23.reshape(864, 192),
        m21.T, m31.T, m41.T, m32, m42.T, m43.T,
    ] + constants

    def f32(*shape):
        return pltpu.VMEM(shape, F32)

    def bf16(*shape):
        return pltpu.VMEM(shape, BF16)

    ext = CELLS + 2
    dma = pltpu.SemaphoreType.DMA
    packets = ((2, 14 * CELLS, 128), (2, 16, GROUP), (4, 16, 128))
    grad_one, grad_two, grad_three, grad_four, share = pl.pallas_call(
        backward_kernel,
        out_shape=[jax.ShapeDtypeStruct(value.shape, BF16) for value in (f1, f2, f3, f4)]
        + [jax.ShapeDtypeStruct((WINDOW, 128), F32)],
        in_specs=[whole] * 3 + [pl.BlockSpec(memory_space=pl.ANY)] * LATE,
        out_specs=[whole] * 5,
        scratch_shapes=[
            *(pltpu.VMEM(value.shape, BF16) for value in inputs[3:]), dma((LATE,)),
            bf16(128 * WINDOW, 128), *(bf16(*shape) for shape in packets + packets), dma((8,)), dma((8,)),
            f32(3, 16 * ext, 128), f32(3, 8 * ext + 8, 128), f32(3, 4 * ext + 8, 128),
            f32(2, 8 * ext, 128), f32(1, 4 * ext, 128), f32(2, 4 * ext, 128),
            f32(4, 16 * ext, 128), f32(3, 8 * ext, 128), f32(2, 4 * ext, 128),
            f32(ext, 16, GROUP), f32(8 * ext + 16, GROUP), f32(4 * ext + 16, GROUP),
            f32(8 * CELLS, GROUP), f32(4 * CELLS, GROUP), f32(3, 16 * CELLS, 128), f32(3, 8 * CELLS, 128),
            f32(4 * CELLS, GROUP), f32(CELLS, GROUP),
            bf16(3, GROUP, 640), bf16(3, GROUP, 640), bf16(3, GROUP, 896), bf16(3, GROUP, 512), bf16(3, GROUP, 640),
            bf16(192, GROUP), bf16(96, GROUP), bf16(GROUP, 256),
            f32(8 * CELLS, GROUP), f32(4 * CELLS, GROUP),
            f32(1, 1104, 128), f32(1, 1872, 128), f32(2, 2976, 128), f32(FLAT_ROWS, 128),
            bf16(4 * BLOCK, 128), bf16(4 * BLOCK, 128), bf16(12, PART, 128), bf16(4 * PART, 128), bf16(4, PART, 128),
            bf16(4, HALF, 128), bf16(HALF, 128), bf16(3, PART, 128),
            dma((4,)), dma((4,)), dma((12,)), dma((12,)), dma((4,)), dma((4,)), dma((4,)), dma((4,)), dma((3,)), dma((3,)),
            bf16(2 * PART, 128), bf16(15, WINDOW, 128), f32(WINDOW, 128), f32(8, 128), f32(15, 8, 128), f32(8, 128), f32(31, 8, 128),
            dma((4,)), dma((15,)), dma((3,)), dma((1,)), dma((15,)), dma((15,)), dma((31,)), dma((31,)),
        ],
        compiler_params=pltpu.CompilerParams(
            collective_id=0, has_side_effects=True, vmem_limit_bytes=56 * 1024 * 1024
        ),
        name="backward",
    )(*inputs)
    offset = (SHARE * lax.axis_index(("row", "col"))) % 1024
    weight_grads = lax.dynamic_slice(share.reshape(WINDOW * 128), (offset,), (SHARE,))
    return grad_one, grad_two, grad_three, grad_four, weight_grads


def solution(mesh):
    in_specs = (
        P(("branch", "row"), "col"),
        P(("branch", "row"), "col"),
        P(("branch", "row"), "col"),
        P(("branch", "row"), "col"),
        P(("branch", "row"), "col"),
        P(("branch", "row"), "col"),
        P(("branch", "row"), "col"),
        P(("branch", "row"), "col"),
        P(("branch", "row"), "col"),
        P(("branch", "row"), "col"),
        P(),
        P(),
        P(),
        P(),
        P(),
        P(),
        P(),
        P(),
        P(),
        P(),
        P(),
    )
    out_specs = (
        P(("branch", "row"), "col"),
        P(("branch", "row"), "col"),
        P(("branch", "row"), "col"),
        P(("branch", "row"), "col"),
        P(("row", "col")),
    )
    return jax.shard_map(local, mesh=mesh, in_specs=in_specs, out_specs=out_specs, check_vma=False)
```

```python
import jax
import jax.numpy as jnp
import numpy as np
from jax import lax
from jax.experimental import pallas as pl
from jax.experimental.pallas import tpu as pltpu
from jax.sharding import PartitionSpec as P

EPSILON = 1e-06
MESH = pl.DeviceIdType.MESH
BF16 = jnp.bfloat16
F32 = jnp.float32
TOTAL = 804096
SHARE = 6282
WINDOW = 64
FLAT_ROWS = 6296


def share_place(share):
    row, col = divmod(share, 8)
    core, z_hi, y = row % 2, (row // 2) % 2, row // 4
    half, quarter = divmod(col, 4)
    return (((y * 2 + core) * 2 + z_hi) * 4 + quarter) * 2 + half


def pack_shares(flat_ref, packed_ref, block):
    for share in range(32 * block, 32 * block + 32):
        start = SHARE * share // 1024 * 8
        place = share_place(share) * WINDOW
        packed_ref[place : place + WINDOW, :] = flat_ref[start : start + WINDOW, :].astype(jnp.bfloat16)


BLOCK = 16 * WINDOW
HALF = 8 * WINDOW
PART = 2 * WINDOW


class Reduction:
    def __init__(self, packed, where, from_core, sum_core, x_first, sum_x, y_second, y_first, sum_y, x_second, sems):
        self.packed, self.where, self.from_core, self.sum_core = packed, where, from_core, sum_core
        self.x_first, self.sum_x, self.y_second = x_first, sum_x, y_second
        self.y_first, self.sum_y, self.x_second = y_first, sum_y, x_second
        self.sems = sems

    def core_copy(self, block):
        x, row, col = self.where
        start = pl.multiple_of((block * 2 + 1 - row % 2) * BLOCK, BLOCK)
        send, recv = self.sems[0:2]
        return remote(
            self.packed.at[pl.ds(start, BLOCK)], self.from_core.at[pl.ds(block * BLOCK, BLOCK)],
            send.at[block], recv.at[block], (x, row + 1 - 2 * (row % 2), col),
        )

    def x_first_copy(self, block, step):
        x, row, col = self.where
        there = (x + step) % 4
        start = pl.multiple_of(block * BLOCK + there * PART, PART)
        slot = block * 3 + step - 1
        send, recv = self.sems[2:4]
        return remote(
            self.sum_core.at[pl.ds(start, PART)], self.x_first.at[slot], send.at[slot], recv.at[slot], (there, row, col)
        )

    def y_first_copy(self, block):
        x, row, col = self.where
        step = (block - row // 4 + 4) % 4
        send, recv = self.sems[4:6]
        return remote(
            self.sum_core.at[pl.ds(block * BLOCK + HALF, HALF)], self.y_first.at[step], send.at[step], recv.at[step],
            (x, block * 4 + row % 4, col),
        )

    def y_second_copy(self, block):
        x, row, col = self.where
        step = (block - row // 4 + 4) % 4
        send, recv = self.sems[6:8]
        return remote(
            self.sum_x.at[pl.ds(block * PART, PART)], self.y_second.at[step], send.at[step], recv.at[step],
            (x, block * 4 + row % 4, col),
        )

    def x_second_copy(self, step):
        x, row, col = self.where
        there = (x + step) % 4
        send, recv = self.sems[8:10]
        return remote(
            self.sum_y.at[pl.ds(pl.multiple_of(there * PART, PART), PART)], self.x_second.at[step - 1],
            send.at[step - 1], recv.at[step - 1], (there, row, col),
        )

    def leave(self, block):
        self.core_copy(block).start()

    def spread(self, block):
        core, y = self.where[1] % 2, self.where[1] // 4
        self.core_copy(block).wait()
        for half in range(2):

            @pl.loop(0, 2)
            def _(part):
                mine = pl.multiple_of((block * 2 + core) * BLOCK + half * HALF + part * (HALF // 2), HALF // 2)
                place = pl.multiple_of(block * BLOCK + half * HALF + part * (HALF // 2), HALF // 2)
                total = self.packed[pl.ds(mine, HALF // 2), :].astype(F32)
                total = total + self.from_core[pl.ds(place, HALF // 2), :].astype(F32)
                self.sum_core[pl.ds(place, HALF // 2), :] = total.astype(BF16)

            if half == 0:
                for step in range(1, 4):
                    self.x_first_copy(block, step).start()
            else:

                @pl.when(y != block)
                def _():
                    self.y_first_copy(block).start()

    def turn_to_y(self, block):
        x, row, col = self.where
        for step in range(1, 4):
            self.x_first_copy(block, step).wait()
        own = pl.multiple_of(block * BLOCK + x * PART, PART)
        total = self.sum_core[pl.ds(own, PART), :].astype(F32)
        for step in range(3):
            total = total + self.x_first[block * 3 + step].astype(F32)
        self.sum_x[block * PART : (block + 1) * PART, :] = total.astype(BF16)

        @pl.when(row // 4 != block)
        def _():
            self.y_second_copy(block).start()

    def waiting(self, src, slots, step, sems):
        send, recv = sems
        return remote(src, slots.at[step], send.at[step], recv.at[step], self.where)

    def turn_to_x(self):
        y = self.where[1] // 4
        for step in range(1, 4):
            self.waiting(self.sum_core.at[pl.ds(0, HALF)], self.y_first, step, self.sems[4:6]).wait_recv()

        @pl.loop(0, 4)
        def _(part):
            own = pl.multiple_of(y * BLOCK + HALF + part * PART, PART)
            at = pl.ds(pl.multiple_of(part * PART, PART), PART)
            total = self.sum_core[pl.ds(own, PART), :].astype(F32)
            for step in range(1, 4):
                total = total + self.y_first[step, at, :].astype(F32)
            self.sum_y[at, :] = total.astype(BF16)

        for step in range(1, 4):
            self.x_second_copy(step).start()

    def plane_sum(self, sum_plane):
        x, y = self.where[0], self.where[1] // 4
        for step in range(1, 4):
            self.waiting(self.sum_x.at[pl.ds(0, PART)], self.y_second, step, self.sems[6:8]).wait_recv()
        total = self.sum_x[pl.ds(pl.multiple_of(y * PART, PART), PART), :].astype(F32)
        for step in range(1, 4):
            total = total + self.y_second[step].astype(F32)
        sum_plane[0:PART, :] = total.astype(BF16)
        for step in range(1, 4):
            self.x_second_copy(step).wait()
        total = self.sum_y[pl.ds(pl.multiple_of(x * PART, PART), PART), :].astype(F32)
        for step in range(3):
            total = total + self.x_second[step].astype(F32)
        sum_plane[PART:, :] = total.astype(BF16)

    def close(self):
        for step in range(1, 4):
            self.waiting(self.sum_core.at[pl.ds(0, HALF)], self.y_first, step, self.sems[4:6]).wait_send()
            self.waiting(self.sum_x.at[pl.ds(0, PART)], self.y_second, step, self.sems[6:8]).wait_send()


def remote(src, dst, send_sem, recv_sem, peer):
    return pltpu.make_async_remote_copy(
        src_ref=src, dst_ref=dst, send_sem=send_sem, recv_sem=recv_sem, device_id=peer, device_id_type=MESH
    )


def finish_shares(
    out_ref,
    sum_plane,
    from_line,
    share_buf,
    square_buf,
    from_near,
    near_buf,
    from_far,
    far_buf,
    from_cross,
    line_send,
    line_recv,
    share_send,
    share_recv,
    near_send,
    near_recv,
    far_send,
    far_recv,
    cross_send,
    cross_recv,
):
    x = lax.axis_index("branch")
    row = lax.axis_index("row")
    col = lax.axis_index("col")
    core, z_hi, y = row % 2, (row // 2) % 2, row // 4
    z = z_hi * 8 + col
    partner = (x, row + 1 - 2 * core, col)

    def line_peer(step):
        there = (z + step) % 16
        return (x, y * 4 + (there // 8) * 2 + core, there % 8)

    def near_peer(step):
        there = (y * 2 + core + step) % 8
        return (x, there // 2 * 4 + z_hi * 2 + there % 2, col)

    def near_copy(step):
        return remote(square_buf, from_near.at[step - 1], near_send.at[step - 1], near_recv.at[step - 1], near_peer(step))

    def far_copy(step):
        return remote(near_buf, from_far.at[step - 1], far_send.at[step - 1], far_recv.at[step - 1], line_peer(step))

    def line_copy(block):
        target = (block // 2) * 8 + (block % 2) * 4 + x
        step = (z - target + 16) % 16
        slot = (step + 15) % 16
        return step, remote(
            sum_plane.at[pl.ds(pl.multiple_of(block * WINDOW, WINDOW), WINDOW)],
            from_line.at[slot], line_send.at[block], line_recv.at[slot],
            (x, y * 4 + (target // 8) * 2 + core, target % 8),
        )

    for block in range(4):
        step, copy = line_copy(block)

        @pl.when(step != 0)
        def _():
            copy.start()

    owner_x = col % 4
    owner = owner_x == x

    def share_copy(step):
        return remote(
            share_buf, share_buf, share_send.at[step - 1], share_recv.at[0],
            ((x + step) % 4, row, col),
        )

    @pl.when(owner)
    def _():
        @pl.loop(0, 15)
        def _(slot):
            remote(
                sum_plane.at[pl.ds(0, WINDOW)], from_line.at[slot], line_send.at[0], line_recv.at[slot], partner
            ).wait_recv()

        own = pl.multiple_of((z_hi * 2 + col // 4) * WINDOW, WINDOW)
        total = sum_plane[pl.ds(own, WINDOW), :].astype(jnp.float32)
        for slot in range(15):
            total = total + from_line[slot].astype(jnp.float32)
        share_buf[...] = total
        offset = (SHARE * (row * 8 + col)) % 1024
        place = lax.broadcasted_iota(jnp.int32, (WINDOW, 128), 0) * 128 + lax.broadcasted_iota(
            jnp.int32, (WINDOW, 128), 1
        )
        inside = jnp.logical_and(place >= offset, place < offset + SHARE)
        square_buf[...] = jnp.where(inside, total * total, 0.0).reshape(8, 8, 128).sum(axis=0)

        for step in range(1, 8):
            near_copy(step).start()
        for step in range(1, 4):
            share_copy(step).start()
        squares = square_buf[...]
        for step in range(1, 8):
            near_copy(step).wait_recv()
            squares = squares + from_near[step - 1]
        near_buf[...] = squares

        @pl.loop(1, 16)
        def _(step):
            far_copy(step).start()

    @pl.when(jnp.logical_not(owner))
    def _():
        near_buf[...] = jnp.zeros((8, 128), F32)

    far_buf[...] = near_buf[...]
    for index in range(4):
        source = 4 * index + x
        step = (z - source + 16) % 16

        @pl.when(step != 0)
        def _():
            slot = (step + 15) % 16
            remote(near_buf, from_far.at[slot], far_send.at[0], far_recv.at[slot], partner).wait_recv()
            far_buf[...] += from_far[slot]

    def cross_copy(step):
        return remote(
            far_buf, from_cross.at[step - 1], cross_send.at[step - 1], cross_recv.at[step - 1], ((x + step) % 4, row, col)
        )

    for step in range(1, 4):
        cross_copy(step).start()

    @pl.when(jnp.logical_not(owner))
    def _():
        share_copy(1).wait_recv()

    for step in range(1, 4):
        cross_copy(step).wait()

    total_squares = jnp.sum(far_buf[...] + from_cross[...].sum(axis=0), keepdims=True)
    spread_rms = jnp.sqrt(total_squares / TOTAL + EPSILON)
    out_ref[...] = share_buf[...] * jnp.minimum(jnp.float32(1.0), 1.0 / spread_rms)

    for block in range(4):
        step, copy = line_copy(block)

        @pl.when(step != 0)
        def _():
            copy.wait_send()

    @pl.when(owner)
    def _():
        @pl.loop(1, 16)
        def _(step):
            far_copy(step).wait_send()

        for step in range(1, 8):
            near_copy(step).wait_send()
        for step in range(1, 4):
            share_copy(step).wait_send()


GROUP = 384
LATE = 28
CELLS = 24
PIECES = (
    (48, 0, 0, 432), (96, 162, 0, 864), (192, 810, 0, 1728), (96, 3402, 864, 432), (192, 3726, 1728, 864),
    (48, 5022, 432, 96), (48, 5058, 528, 192), (48, 5130, 720, 384), (96, 5274, 1296, 192),
    (96, 5418, 1488, 384), (192, 5706, 2592, 384),
)


def dot(left, right, left_dim=1, right_dim=0):
    return lax.dot_general(left, right, (((left_dim,), (right_dim,)), ((), ())), preferred_element_type=F32)


def lanes_of(rows, lanes):
    return lax.broadcasted_iota(jnp.int32, (rows, lanes), 1)


def packet_rows(up):
    maps = (
        (0, 3, 16, (11, 4), (3, 12)), (1, 3, 8, (5, 2), (1, 6)), (2, 3, 4, (2, 1), (0, 3)),
        (3, 2, 8, (5, 2), (1, 6)), (4, 1, 4, (2, 1), (0, 3)), (5, 2, 4, (2, 1), (0, 3)),
    )
    return [
        (index, tile, rows, leaves[up], lands[up]) for index, tiles, rows, leaves, lands in maps for tile in range(tiles)
    ]


def fill_packets(maps, send_rows, send_corners):
    for up in range(2):
        parts = [
            maps[index][tile, pl.ds(rows + leaves, CELLS, stride=rows), :]
            for index, tile, rows, leaves, lands in packet_rows(up)
        ]
        send_rows[up] = jnp.concatenate(parts, axis=0).astype(BF16)
        blank = [jnp.zeros((2, 128), F32)]
        send_corners[2 * up] = jnp.concatenate([part[CELLS - 1 : CELLS] for part in parts] + blank, axis=0).astype(BF16)
        send_corners[2 * up + 1] = jnp.concatenate([part[0:1] for part in parts] + blank, axis=0).astype(BF16)


def fill_sides(u1, u2, u3, send_sides):
    for index, start in enumerate(((CELLS - 1) * GROUP, 0)):
        parts = [value[:, start : start + GROUP] for value in (u1, u2, u3)] + [jnp.zeros((2, GROUP), F32)]
        send_sides[index] = jnp.concatenate(parts, axis=0).astype(BF16)


def banded(weights, repeat, width, rows, blocks, dst):
    wide = dot(weights, repeat)
    lane = lanes_of(rows, repeat.shape[1])
    for block, pieces in enumerate(blocks):
        value = jnp.zeros((rows, repeat.shape[1]), F32)
        for tap, start in pieces:
            inside = jnp.logical_and(lane >= start, lane < start + width)
            value = jnp.where(inside, wide[tap * rows : (tap + 1) * rows], value)
        dst[block * rows : (block + 1) * rows, :] = value.astype(BF16)


def conv_blocks(width, base):
    return [[(tap, base + width * (n + 1 - tap)) for tap in range(3)] for n in range(GROUP // width)]


def down_blocks(width):
    blocks = []
    for j in range(2 * (GROUP // width)):
        if j % 2 == 0:
            blocks.append([(1, width * (j // 2))])
        else:
            blocks.append([(2, width * (j // 2)), (0, width * (j // 2 + 1))])
    return blocks


def mixer_blocks(width, count):
    return [[(0, width * j)] for j in range(count)]


def window(value, start, width):
    first, end = start // 128, -(-(start + width) // 128)
    part = value[:, first * 128 : end * 128]
    shift = start - first * 128
    if shift:
        part = pltpu.roll(part, (end - first) * 128 - shift, 1)
    return part[:, : -(-width // 128) * 128]


def place(src, flat, width, flat_base, src_base, count):
    stride = GROUP // width
    rows = count // stride
    lane = lanes_of(rows, 128)
    held = {}
    for tile in range(3):
        value = None
        for j in range(stride):
            for part in range(-(-width // 128)):
                low = max(width * j + 128 * part, 128 * tile)
                high = min(width * j + min(width, 128 * part + 128), 128 * tile + 128)
                if low >= high:
                    continue
                if (j, part) not in held:
                    held[j, part] = src[part, pl.ds(src_base + j, rows, stride=stride), :]
                piece = held[j, part]
                shift = (width * j + 128 * part - 128 * tile) % 128
                if shift:
                    piece = pltpu.roll(piece, shift, 1)
                value = piece if value is None else jnp.where(lane >= low - 128 * tile, piece, value)
        flat[pl.ds(flat_base + tile, rows, stride=3), :] = value


def backward_kernel(
    u1_ref, u2_ref, u3_ref, *refs,
):
    far = refs[:LATE]
    outs, near, (late_sems, *rest) = refs[LATE : LATE + 5], refs[LATE + 5 : 2 * LATE + 5], refs[2 * LATE + 5 :]
    copies = [pltpu.make_async_copy(src, dst, late_sems.at[i]) for i, (src, dst) in enumerate(zip(far, near))]
    for copy in copies:
        copy.start()
    backward_stages(copies, u1_ref, u2_ref, u3_ref, *near, *outs, *rest)


def backward_stages(
    late_copies, u1_ref, u2_ref, u3_ref, f1_ref, f2_ref, f3_ref, f4_ref, o1_ref, o2_ref, o3_ref,
    k1_ref, k2_ref, k3_ref, s12_ref, s23_ref, m21_ref, m31_ref, m41_ref, m32_ref, m42_ref, m43_ref,
    rep1_ref, rep2_ref, rep3_ref, rep12_ref, rep23_ref, rep96_ref, rep192_ref, pool1_ref, pool2_ref, pool3_ref,
    g1_ref, g2_ref, g3_ref, g4_ref, share_ref,
    packed_ref, send_rows, send_sides, send_corners, recv_rows, recv_sides, recv_corners, halo_send, halo_recv,
    ext1, ext2, ext3, pp12, pp13, pp23, v1, v2, v3, del1, del2, del3, pad_f2, pad_f3, pad_o1, pad_o2, pad_o3, rows_f4,
    band1, band2, band3, band12, band23, band21, band31, band32, res2, res3, w48, w96, w192, flat, *reduce_refs,
):
    def lanes(g):
        return slice(GROUP * g, GROUP * (g + 1))

    x = lax.axis_index("branch")
    row = lax.axis_index("row")
    col = lax.axis_index("col")
    core, z_hi, y = row % 2, (row // 2) % 2, row // 4
    z = z_hi * 8 + col
    line = x * 16 + row

    def peer(down, right):
        there = (line + down + 64) % 64
        return (there // 16, there % 16, (col + right + 8) % 8)

    routes = (
        (0, 1, 0, send_rows.at[0], recv_rows.at[0]),
        (1, -1, 0, send_rows.at[1], recv_rows.at[1]),
        (2, 0, 1, send_sides.at[0], recv_sides.at[0]),
        (3, 0, -1, send_sides.at[1], recv_sides.at[1]),
        (4, 1, 1, send_corners.at[0], recv_corners.at[0]),
        (5, 1, -1, send_corners.at[1], recv_corners.at[1]),
        (6, -1, 1, send_corners.at[2], recv_corners.at[2]),
        (7, -1, -1, send_corners.at[3], recv_corners.at[3]),
    )

    def line_peer(step):
        there = (z + step) % 16
        return (x, y * 4 + (there // 8) * 2 + core, there % 8)

    def near_peer(step):
        there = (y * 2 + core + step) % 8
        return (x, there // 2 * 4 + z_hi * 2 + there % 2, col)

    def greet(peer):
        pl.semaphore_signal(barrier, inc=1, device_id=peer, device_id_type=MESH)

    barrier = pltpu.get_barrier_semaphore()
    for route in routes:
        greet(peer(route[1], route[2]))
    @pl.loop(1, 16)
    def _(step):
        greet(line_peer(step))

    for step in range(1, 4):
        greet(((x + step) % 4, row, col))
    for step in range(1, 8):
        greet(near_peer(step))

    u1, u2, u3 = (ref[...].astype(F32) for ref in (u1_ref, u2_ref, u3_ref))
    fill_sides(u1, u2, u3, send_sides)
    for ref in (ext1, ext2, ext3):
        ref[...] = jnp.zeros_like(ref)
    for g in range(CELLS):
        for tile in range(3):
            part = slice(GROUP * g + 128 * tile, GROUP * g + 128 * tile + 128)
            ext1[tile, 16 * g + 20 : 16 * g + 28, :] = u1[:, part]
            ext2[tile, 8 * g + 10 : 8 * g + 14, :] = u2[:, part]
            ext3[tile, 4 * g + 5 : 4 * g + 7, :] = u3[:, part]

    for copy in late_copies:
        copy.wait()

    tall1, tall2, tall3 = 16 * (CELLS + 2), 8 * (CELLS + 2), 4 * (CELLS + 2)
    def tiled_store(ref, value, rows=slice(None)):
        for tile in range(value.shape[1] // 128):
            ref[tile, rows, :] = value[:, 128 * tile : 128 * tile + 128]

    def strided(ref, tiles, start, count, stride):
        parts = [ref[tile, pl.ds(start, count, stride=stride), :] for tile in tiles]
        return parts[0] if len(parts) == 1 else jnp.concatenate(parts, axis=1)

    def strided_sum(ref, picks, count, stride, tiles):
        total = None
        for pick in picks:
            piece = strided(ref, tiles, pick, count, stride)
            total = piece if total is None else total + piece
        return total

    def whole_of(ref, rows):
        return jnp.concatenate([ref[tile, rows, :] for tile in range(ref.shape[0])], axis=1)

    def run_pools():
        tiled_store(v1, dot(whole_of(ext1, slice(0, tall1)).astype(BF16), pool1_ref[...]))
        tiled_store(v2, dot(whole_of(ext2, slice(0, tall2)).astype(BF16), pool2_ref[...]))
        tiled_store(pp12, strided_sum(v1, range(2), tall2, 2, (0, 1)))
        tiled_store(pp13, strided_sum(v1, range(4), tall3, 4, (2,)))
        tiled_store(pp23, strided_sum(v2, range(2), tall3, 2, (0, 1)))

    def pooled():
        return (
            whole_of(pp12, slice(0, tall2)).astype(BF16),
            whole_of(pp13, slice(0, tall3)).astype(BF16),
            whole_of(pp23, slice(0, tall3)).astype(BF16),
        )

    run_pools()
    tiled_store(v3, dot(whole_of(ext3, slice(0, tall3)).astype(BF16), pool3_ref[...]))
    p14 = strided_sum(v1, range(16 + 4, 16 + 12), CELLS, 16, (3,)).astype(BF16)
    p24 = strided_sum(v2, range(8 + 2, 8 + 6), CELLS, 8, (2,)).astype(BF16)
    p34 = strided_sum(v3, range(4 + 1, 4 + 3), CELLS, 4, (0, 1)).astype(BF16)
    p12, p13, p23 = pooled()
    fill_packets((ext1, ext2, ext3, pp12, pp13, pp23), send_rows, send_corners)
    pl.semaphore_wait(barrier, 33)

    def halo_copy(route):
        slot, down, right, src, dst = route
        return pltpu.make_async_remote_copy(
            src_ref=src, dst_ref=dst, send_sem=halo_send.at[slot], recv_sem=halo_recv.at[slot],
            device_id=peer(down, right), device_id_type=MESH,
        )

    for route in routes:
        halo_copy(route).start()

    for ref in (pad_f2, pad_f3, pad_o1, pad_o2, pad_o3):
        ref[...] = jnp.zeros_like(ref)
    f2, f3, o1, o2, o3, f4 = (ref[...].astype(F32) for ref in (f2_ref, f3_ref, o1_ref, o2_ref, o3_ref, f4_ref))
    for g in range(CELLS):
        at = lanes(g)
        pad_f2[8 * g + 2 : 8 * g + 6, :] = f2[:, at]
        pad_f3[4 * g + 1 : 4 * g + 3, :] = f3[:, at]
        for tile in range(3):
            part = slice(GROUP * g + 128 * tile, GROUP * g + 128 * tile + 128)
            pad_o1[tile, 16 * g + 4 : 16 * g + 12, :] = o1[:, part]
            pad_o2[tile, 8 * g + 2 : 8 * g + 6, :] = o2[:, part]
        pad_o3[4 * g + 1 : 4 * g + 3, :] = o3[:, at]
        rows_f4[g : g + 1, :] = f4[:, at]

    for a in range(3):
        banded(k1_ref[144 * a : 144 * a + 144, :], rep1_ref[...], 48, 48, conv_blocks(48, 128), band1.at[a])
        banded(k2_ref[288 * a : 288 * a + 288, :], rep2_ref[...], 96, 96, conv_blocks(96, 128), band2.at[a])
        banded(k3_ref[576 * a : 576 * a + 576, :], rep3_ref[...], 192, 192, conv_blocks(192, 256), band3.at[a])
        banded(s12_ref[144 * a : 144 * a + 144, :], rep12_ref[...], 96, 48, down_blocks(96), band12.at[a])
        banded(s23_ref[288 * a : 288 * a + 288, :], rep23_ref[...], 192, 96, down_blocks(192), band23.at[a])
    banded(m21_ref[...], rep96_ref[...], 96, 48, mixer_blocks(96, 4), band21)
    banded(m31_ref[...], rep192_ref[...], 192, 48, mixer_blocks(192, 2), band31)
    banded(m32_ref[...], rep96_ref[:, :256], 96, 192, mixer_blocks(96, 2), band32)

    def fold_mixer(grads, width, rows, base, dst):
        total = None
        for j in range(GROUP // rows):
            part = window(grads[j * rows : (j + 1) * rows, :], width * j, width)
            total = part if total is None else total + part
        tiled_store(dst, total, slice(base, base + rows))

    o2x = jnp.concatenate([pad_o2[tile] for tile in range(3)], axis=1).astype(BF16)
    o3x = pad_o3[...].astype(BF16)
    f4x = rows_f4[...].astype(BF16)
    inner2, inner3 = slice(8, 8 + 8 * CELLS), slice(4, 4 + 4 * CELLS)
    fold_mixer(dot(o2x, p12[inner2], 0, 0), 48, 96, 432, w48)
    fold_mixer(dot(o3x, p13[inner3], 0, 0), 48, 192, 528, w48)
    fold_mixer(dot(f4x, p14, 0, 0), 48, 384, 720, w48)
    fold_mixer(dot(o3x, p23[inner3], 0, 0), 96, 192, 1296, w96)
    fold_mixer(dot(f4x, p24, 0, 0), 96, 384, 1488, w96)
    fold_mixer(dot(f4x, p34, 0, 0), 192, 384, 2592, w192)
    back4 = (
        dot(p14[:, 0:48], m41_ref[...]) + dot(p24[:, 0:96], m42_ref[...]) + dot(p34[:, 0:192], m43_ref[...])
    )
    for g in range(CELLS):
        g4_ref[:, lanes(g)] = back4[g : g + 1].astype(BF16)

    for route in routes:
        halo_copy(route).wait()
    top, bottom = jnp.where(line > 0, 1.0, 0.0), jnp.where(line < 63, 1.0, 0.0)
    left, right = jnp.where(col > 0, 1.0, 0.0), jnp.where(col < 7, 1.0, 0.0)
    sides = [recv_sides[0].astype(F32) * left, recv_sides[1].astype(F32) * right]
    corners = [
        recv_corners[0].astype(F32) * (top * left), recv_corners[1].astype(F32) * (top * right),
        recv_corners[2].astype(F32) * (bottom * left), recv_corners[3].astype(F32) * (bottom * right),
    ]
    for index, group in enumerate((0, CELLS + 1)):
        for tile in range(3):
            part = sides[index][:, 128 * tile : 128 * tile + 128]
            ext1[tile, 16 * group + 4 : 16 * group + 12, :] = part[0:8]
            ext2[tile, 8 * group + 2 : 8 * group + 6, :] = part[8:12]
            ext3[tile, 4 * group + 1 : 4 * group + 3, :] = part[12:14]

    def fill_rims(refs, first):
        for up, flag in enumerate((top, bottom)):
            packet = recv_rows[up].astype(F32) * flag
            for place_in, (index, tile, rows, leaves, lands) in enumerate(packet_rows(up)):
                if not first <= index < first + 3:
                    continue
                ref = refs[index - first]
                part = packet[CELLS * place_in : CELLS * (place_in + 1)]
                ref[tile, pl.ds(rows + lands, CELLS, stride=rows), :] = part
                ref[tile, lands : lands + 1, :] = corners[2 * up][place_in : place_in + 1]
                last = rows * (CELLS + 1) + lands
                ref[tile, last : last + 1, :] = corners[2 * up + 1][place_in : place_in + 1]

    fill_rims((ext1, ext2, ext3), 0)
    run_pools()
    fill_rims((pp12, pp13, pp23), 3)
    p12, p13, p23 = pooled()

    def fold_down(grads, width, rows, a, base, dst):
        for b in range(3):
            total = None
            for j in range(1 if b != 1 else 0, 2 * (GROUP // width), 2):
                p = (j + 1 - b) // 2
                part = window(grads[j * rows : (j + 1) * rows, :], width * p, width)
                total = part if total is None else total + part
            start = base + (a * 3 + b) * rows
            tiled_store(dst, total, slice(start, start + rows))

    def down_grads(saved, ext, skip, count, head, width, rows, base, dst):
        even = strided(saved, range(3), 0, count, 2).astype(BF16)
        odd = strided(saved, range(3), 1, count, 2).astype(BF16)
        for a in range(3):
            at = skip + (1 if a == 0 else 0)
            xs = jnp.concatenate(
                [ext[tile, at : at + count, :] for tile in range(3)]
                + [ext[tile, at + skip : at + skip + count, :] for tile in range(head // 128)],
                axis=1,
            ).astype(BF16)
            fold_down(dot(even if a == 1 else odd, xs, 0, 0), width, rows, a, base, dst)

    down_grads(pad_o1, ext2, 8, 8 * CELLS, 128, 96, 48, 864, w96)
    down_grads(pad_o2, ext3, 4, 4 * CELLS, 256, 192, 96, 1728, w192)

    reduction = Reduction(packed_ref, (x, row, col), *reduce_refs[:8], reduce_refs[8:18])
    flat[6282:FLAT_ROWS, :] = jnp.zeros((FLAT_ROWS - 6282, 128), F32)

    def settle(pieces, blocks):
        for piece in pieces:
            width, flat_base, src_base, count = PIECES[piece]
            place({48: w48, 96: w96, 192: w192}[width], flat, width, flat_base, src_base, count)
        for block in blocks:
            pack_shares(flat, packed_ref, block)
            reduction.leave(block)

    settle((3, 4, 5, 6, 7, 8, 9, 10), (3,))

    def rim_mask(rows, inner):
        place_row = lax.broadcasted_iota(jnp.int32, (CELLS + 2, rows, GROUP), 1)
        place_col = lax.broadcasted_iota(jnp.int32, (CELLS + 2, rows, GROUP), 0)
        start, end = (rows - inner) // 2, (rows + inner) // 2
        by_row = jnp.where(place_row == start - 1, top, jnp.where(place_row == end, bottom, 1.0))
        by_row = jnp.where(jnp.logical_and(place_row >= start - 1, place_row <= end), by_row, 0.0)
        by_col = jnp.where(place_col == 0, left, jnp.where(place_col == CELLS + 1, right, 1.0))
        return by_row * by_col

    def rolled(value):
        return pltpu.roll(value, value.shape[0] - 1, 0)

    x2 = jnp.concatenate([whole_of(ext2, slice(0, tall2)), ext2[0, 8 : tall2 + 8, :]], axis=1).astype(BF16)
    tiled_store(v1, dot(x2, band12[1], 1, 1), pl.ds(0, tall2, stride=2))
    tiled_store(v1, dot(x2, band12[2], 1, 1) + rolled(dot(x2, band12[0], 1, 1)), pl.ds(1, tall2, stride=2))
    spread1 = jnp.concatenate([v1[tile] for tile in range(3)], axis=1)
    delta1 = (whole_of(ext1, slice(0, tall1)) + spread1).reshape(CELLS + 2, 16, GROUP)
    del1[...] = (delta1 * rim_mask(16, 8)).astype(BF16).astype(F32)

    x3 = jnp.concatenate(
        [whole_of(ext3, slice(0, tall3)), ext3[0, 4 : tall3 + 4, :], ext3[1, 4 : tall3 + 4, :]], axis=1
    ).astype(BF16)
    tiled_store(v2, dot(x3, band23[1], 1, 1), pl.ds(0, tall3, stride=2))
    tiled_store(v2, dot(x3, band23[2], 1, 1) + rolled(dot(x3, band23[0], 1, 1)), pl.ds(1, tall3, stride=2))
    spread2 = jnp.concatenate([v2[tile] for tile in range(3)], axis=1)
    delta2 = whole_of(ext2, slice(0, tall2)) + dot(p12[:, 0:192], band21[...]) + spread2
    del2[8 : 8 + tall2, :] = (delta2 * rim_mask(8, 4).reshape(tall2, GROUP)).astype(BF16).astype(F32)

    delta3 = whole_of(ext3, slice(0, tall3)) + dot(p13[:, 0:96], band31[...]) + dot(p23, band32[...], 1, 1)
    place_row = lax.broadcasted_iota(jnp.int32, (tall3, GROUP), 0)
    in_group = jnp.bitwise_and(place_row, 3)
    by_row = jnp.where(in_group == 0, top, jnp.where(in_group == 3, bottom, 1.0))
    by_col = jnp.where(place_row < 4, left, jnp.where(place_row >= 4 * (CELLS + 1), right, 1.0))
    del3[8 : 8 + tall3, :] = (delta3 * (by_row * by_col)).astype(BF16).astype(F32)
    for ref in (del2, del3):
        ref[0:8, :] = jnp.zeros((8, GROUP), F32)
        ref[ref.shape[0] - 8 :, :] = jnp.zeros((8, GROUP), F32)

    reduction.spread(3)

    def fold(grads, width, base, a, dst):
        total = None
        for n in range(GROUP // width):
            part = window(grads[n * width : (n + 1) * width, :], base + width * (n - 1), 3 * width)
            total = part if total is None else total + part
        for tap in range(3):
            start = (a * 3 + tap) * width
            tiled_store(dst, window(total, width * (2 - tap), width), slice(start, start + width))

    f3x = pad_f3[...].astype(BF16)
    back = None
    for a in range(3):
        at = 8 + 1 - a
        n = 4 * CELLS
        x3d = jnp.concatenate(
            [del3[at : at + n, 128:GROUP], del3[at + 4 : at + 4 + n, :], del3[at + 8 : at + 8 + n, 0:256]], axis=1
        ).astype(BF16)
        part = dot(x3d, band3[a], 1, 1)
        back = part if back is None else back + part
        fold(dot(f3x, x3d, 0, 0), 192, 256, a, w192)
    res3[...] = back
    for g in range(CELLS):
        g3_ref[:, lanes(g)] = res3[4 * g + 1 : 4 * g + 3, :].astype(BF16)

    settle((2,), (2, 1))

    f2x = pad_f2[...].astype(BF16)
    back = None
    for a in range(3):
        at = 8 + 1 - a
        n = 8 * CELLS
        x2d = jnp.concatenate(
            [del2[at : at + n, 256:GROUP], del2[at + 8 : at + 8 + n, :], del2[at + 16 : at + 16 + n, 0:128]], axis=1
        ).astype(BF16)
        part = dot(x2d, band2[a], 1, 1)
        back = part if back is None else back + part
        fold(dot(f2x, x2d, 0, 0), 96, 128, a, w96)
    res2[...] = back
    for g in range(CELLS):
        g2_ref[:, lanes(g)] = res2[8 * g + 2 : 8 * g + 6, :].astype(BF16)

    reduction.spread(2)
    reduction.spread(1)

    f1 = f1_ref[...]
    f1 = jnp.concatenate([f1[:, lanes(g)].astype(F32) for g in range(CELLS)], axis=0).astype(BF16)
    back = None
    for a in range(3):
        at = slice(5 - a, 13 - a)
        x1 = jnp.concatenate(
            [del1[0:CELLS, at, 256:GROUP], del1[1 : CELLS + 1, at, :], del1[2 : CELLS + 2, at, 0:128]], axis=2
        ).reshape(8 * CELLS, 640).astype(BF16)
        part = dot(x1, band1[a], 1, 1)
        back = part if back is None else back + part
        fold(dot(f1, x1, 0, 0), 48, 128, a, w48)
    for g in range(CELLS):
        g1_ref[:, lanes(g)] = back[8 * g : 8 * g + 8].astype(BF16)

    settle((0, 1), (0,))
    reduction.spread(0)
    for block in (3, 2, 1, 0):
        reduction.turn_to_y(block)
    reduction.turn_to_x()
    reduction.plane_sum(reduce_refs[18])
    finish_shares(share_ref, *reduce_refs[18:])
    reduction.close()


def repeats(width, lanes, base=0):
    lane = np.arange(lanes)[None, :]
    return ((lane - base) % width == np.arange(width)[:, None]).astype(np.float32)


def pools(width, factors, parts):
    blocks = []
    for factor, lanes in zip(factors, parts):
        block = np.zeros((GROUP, lanes), np.float32)
        for lane in range(GROUP):
            block[lane, lane // (width * factor) * width + lane % width] = 1.0
        blocks.append(block)
    return np.concatenate(blocks, axis=1)


def hand_over_kernel(*refs):
    share_ref, out_ref = refs[4], refs[9]
    for source, target in zip(refs[0:4], refs[5:9]):
        target[...] = source[...]
    offset = (SHARE * (lax.axis_index("row") * 8 + lax.axis_index("col"))) % 1024
    rows, lanes = offset // 128, offset % 128
    share = share_ref[...]
    first = pltpu.roll(pltpu.roll(share, (WINDOW - rows) % WINDOW, 0), (128 - lanes) % 128, 1)
    then = pltpu.roll(pltpu.roll(share, WINDOW - 1 - rows, 0), (128 - lanes) % 128, 1)
    out_ref[...] = jnp.where(lanes_of(WINDOW, 128) < 128 - lanes, first, then)[0:56]


def hand_over(*results):
    whole = pl.BlockSpec(memory_space=pltpu.VMEM)
    return pl.pallas_call(
        hand_over_kernel,
        out_shape=[jax.ShapeDtypeStruct(value.shape, BF16) for value in results[:4]]
        + [jax.ShapeDtypeStruct((56, 128), F32)],
        in_specs=[whole] * 5,
        out_specs=[whole] * 5,
        compiler_params=pltpu.CompilerParams(vmem_limit_bytes=56 * 1024 * 1024),
        name="hand_over",
    )(*results)


def local(f1, f2, f3, f4, o1, o2, o3, u1, u2, u3, k1, k2, k3, s12, s23, m21, m31, m41, m32, m42, m43):
    constants = [
        jnp.asarray(value, BF16)
        for value in (
            repeats(48, 640, 128), repeats(96, 640, 128), repeats(192, 896, 256), repeats(96, 512), repeats(192, 640),
            repeats(96, 384), repeats(192, 384),
            pools(48, (2, 4, 8), (256, 128, 128)), pools(96, (2, 4), (256, 128)), pools(192, (2,), (256,)),
        )
    ]
    whole = pl.BlockSpec(memory_space=pltpu.VMEM)
    inputs = [
        u1, u2, u3, f1, f2, f3, f4, o1, o2, o3,
        k1.reshape(432, 48), k2.reshape(864, 96), k3.reshape(1728, 192), s12.reshape(432, 96), s23.reshape(864, 192),
        m21.T, m31.T, m41.T, m32, m42.T, m43.T,
    ] + constants

    def f32(*shape):
        return pltpu.VMEM(shape, F32)

    def bf16(*shape):
        return pltpu.VMEM(shape, BF16)

    ext = CELLS + 2
    dma = pltpu.SemaphoreType.DMA
    packets = ((2, 14 * CELLS, 128), (2, 16, GROUP), (4, 16, 128))
    grad_one, grad_two, grad_three, grad_four, share = pl.pallas_call(
        backward_kernel,
        out_shape=[jax.ShapeDtypeStruct(value.shape, BF16) for value in (f1, f2, f3, f4)]
        + [jax.ShapeDtypeStruct((WINDOW, 128), F32)],
        in_specs=[whole] * 3 + [pl.BlockSpec(memory_space=pl.ANY)] * LATE,
        out_specs=[whole] * 5,
        scratch_shapes=[
            *(pltpu.VMEM(value.shape, BF16) for value in inputs[3:]), dma((LATE,)),
            bf16(128 * WINDOW, 128), *(bf16(*shape) for shape in packets + packets), dma((8,)), dma((8,)),
            f32(3, 16 * ext, 128), f32(3, 8 * ext + 8, 128), f32(3, 4 * ext + 8, 128),
            f32(2, 8 * ext, 128), f32(1, 4 * ext, 128), f32(2, 4 * ext, 128),
            f32(4, 16 * ext, 128), f32(3, 8 * ext, 128), f32(2, 4 * ext, 128),
            f32(ext, 16, GROUP), f32(8 * ext + 16, GROUP), f32(4 * ext + 16, GROUP),
            f32(8 * CELLS, GROUP), f32(4 * CELLS, GROUP), f32(3, 16 * CELLS, 128), f32(3, 8 * CELLS, 128),
            f32(4 * CELLS, GROUP), f32(CELLS, GROUP),
            bf16(3, GROUP, 640), bf16(3, GROUP, 640), bf16(3, GROUP, 896), bf16(3, GROUP, 512), bf16(3, GROUP, 640),
            bf16(192, GROUP), bf16(96, GROUP), bf16(GROUP, 256),
            f32(8 * CELLS, GROUP), f32(4 * CELLS, GROUP),
            f32(1, 1104, 128), f32(1, 1872, 128), f32(2, 2976, 128), f32(FLAT_ROWS, 128),
            bf16(4 * BLOCK, 128), bf16(4 * BLOCK, 128), bf16(12, PART, 128), bf16(4 * PART, 128), bf16(4, PART, 128),
            bf16(4, HALF, 128), bf16(HALF, 128), bf16(3, PART, 128),
            dma((4,)), dma((4,)), dma((12,)), dma((12,)), dma((4,)), dma((4,)), dma((4,)), dma((4,)), dma((3,)), dma((3,)),
            bf16(2 * PART, 128), bf16(15, WINDOW, 128), f32(WINDOW, 128), f32(8, 128), f32(7, 8, 128), f32(8, 128),
            f32(15, 8, 128), f32(8, 128), f32(3, 8, 128),
            dma((4,)), dma((15,)), dma((3,)), dma((1,)), dma((7,)), dma((7,)), dma((15,)), dma((15,)), dma((3,)), dma((3,)),
        ],
        compiler_params=pltpu.CompilerParams(
            collective_id=0, has_side_effects=True, vmem_limit_bytes=56 * 1024 * 1024
        ),
        name="backward",
    )(*inputs)
    *grads, weight_grads = hand_over(grad_one, grad_two, grad_three, grad_four, share)
    return *grads, weight_grads.reshape(56 * 128)[:SHARE]


def solution(mesh):
    in_specs = (
        P(("branch", "row"), "col"),
        P(("branch", "row"), "col"),
        P(("branch", "row"), "col"),
        P(("branch", "row"), "col"),
        P(("branch", "row"), "col"),
        P(("branch", "row"), "col"),
        P(("branch", "row"), "col"),
        P(("branch", "row"), "col"),
        P(("branch", "row"), "col"),
        P(("branch", "row"), "col"),
        P(),
        P(),
        P(),
        P(),
        P(),
        P(),
        P(),
        P(),
        P(),
        P(),
        P(),
    )
    out_specs = (
        P(("branch", "row"), "col"),
        P(("branch", "row"), "col"),
        P(("branch", "row"), "col"),
        P(("branch", "row"), "col"),
        P(("row", "col")),
    )
    return jax.shard_map(local, mesh=mesh, in_specs=in_specs, out_specs=out_specs, check_vma=False)
```

```python
import jax
import jax.numpy as jnp
import numpy as np
from jax import lax
from jax.experimental import pallas as pl
from jax.experimental.pallas import tpu as pltpu
from jax.sharding import PartitionSpec as P

EPSILON = 1e-06
MESH = pl.DeviceIdType.MESH
BF16 = jnp.bfloat16
F32 = jnp.float32
TOTAL = 804096
SHARE = 6282
WINDOW = 64
FLAT_ROWS = 6296


def share_place(share):
    row, col = divmod(share, 8)
    core, z_hi, y = row % 2, (row // 2) % 2, row // 4
    half, quarter = divmod(col, 4)
    return (((y * 2 + core) * 2 + z_hi) * 4 + quarter) * 2 + half


def pack_shares(flat_ref, packed_ref, block, half):
    for share in range(32 * block + 16 * half, 32 * block + 16 * half + 16):
        start = SHARE * share // 1024 * 8
        place = share_place(share) * WINDOW
        packed_ref[place : place + WINDOW, :] = flat_ref[start : start + WINDOW, :].astype(jnp.bfloat16)


BLOCK = 16 * WINDOW
HALF = 8 * WINDOW
PART = 2 * WINDOW


class Reduction:
    def __init__(self, packed, where, from_core, sum_core, x_first, sum_x, y_second, y_first, sum_y, x_second, sems):
        self.packed, self.where, self.from_core, self.sum_core = packed, where, from_core, sum_core
        self.x_first, self.sum_x, self.y_second = x_first, sum_x, y_second
        self.y_first, self.sum_y, self.x_second = y_first, sum_y, x_second
        self.sems = sems

    def core_copy(self, block, half):
        x, row, col = self.where
        start = pl.multiple_of((block * 2 + 1 - row % 2) * BLOCK + half * HALF, HALF)
        send, recv = self.sems[0:2]
        return remote(
            self.packed.at[pl.ds(start, HALF)], self.from_core.at[pl.ds(block * BLOCK + half * HALF, HALF)],
            send.at[block * 2 + half], recv.at[block * 2 + half], (x, row + 1 - 2 * (row % 2), col),
        )

    def x_first_copy(self, block, step):
        x, row, col = self.where
        there = (x + step) % 4
        start = pl.multiple_of(block * BLOCK + there * PART, PART)
        slot = block * 3 + step - 1
        send, recv = self.sems[2:4]
        return remote(
            self.sum_core.at[pl.ds(start, PART)], self.x_first.at[slot], send.at[slot], recv.at[slot], (there, row, col)
        )

    def y_first_copy(self, block):
        x, row, col = self.where
        step = (block - row // 4 + 4) % 4
        send, recv = self.sems[4:6]
        return remote(
            self.sum_core.at[pl.ds(block * BLOCK + HALF, HALF)], self.y_first.at[step], send.at[step], recv.at[step],
            (x, block * 4 + row % 4, col),
        )

    def y_second_copy(self, block):
        x, row, col = self.where
        step = (block - row // 4 + 4) % 4
        send, recv = self.sems[6:8]
        return remote(
            self.sum_x.at[pl.ds(block * PART, PART)], self.y_second.at[step], send.at[step], recv.at[step],
            (x, block * 4 + row % 4, col),
        )

    def x_second_copy(self, step):
        x, row, col = self.where
        there = (x + step) % 4
        send, recv = self.sems[8:10]
        return remote(
            self.sum_y.at[pl.ds(pl.multiple_of(there * PART, PART), PART)], self.x_second.at[step - 1],
            send.at[step - 1], recv.at[step - 1], (there, row, col),
        )

    def leave(self, block, half):
        self.core_copy(block, half).start()

    def spread(self, block, half):
        core, y = self.where[1] % 2, self.where[1] // 4
        self.core_copy(block, half).wait()

        @pl.loop(0, 2)
        def _(part):
            mine = pl.multiple_of((block * 2 + core) * BLOCK + half * HALF + part * (HALF // 2), HALF // 2)
            place = pl.multiple_of(block * BLOCK + half * HALF + part * (HALF // 2), HALF // 2)
            total = self.packed[pl.ds(mine, HALF // 2), :].astype(F32)
            total = total + self.from_core[pl.ds(place, HALF // 2), :].astype(F32)
            self.sum_core[pl.ds(place, HALF // 2), :] = total.astype(BF16)

        if half == 0:
            for step in range(1, 4):
                self.x_first_copy(block, step).start()
        else:

            @pl.when(y != block)
            def _():
                self.y_first_copy(block).start()

    def turn_to_y(self, block):
        x, row, col = self.where
        for step in range(1, 4):
            self.x_first_copy(block, step).wait()
        own = pl.multiple_of(block * BLOCK + x * PART, PART)
        total = self.sum_core[pl.ds(own, PART), :].astype(F32)
        for step in range(3):
            total = total + self.x_first[block * 3 + step].astype(F32)
        self.sum_x[block * PART : (block + 1) * PART, :] = total.astype(BF16)

        @pl.when(row // 4 != block)
        def _():
            self.y_second_copy(block).start()

    def waiting(self, src, slots, step, sems):
        send, recv = sems
        return remote(src, slots.at[step], send.at[step], recv.at[step], self.where)

    def turn_to_x(self):
        y = self.where[1] // 4
        for step in range(1, 4):
            self.waiting(self.sum_core.at[pl.ds(0, HALF)], self.y_first, step, self.sems[4:6]).wait_recv()

        @pl.loop(0, 4)
        def _(part):
            own = pl.multiple_of(y * BLOCK + HALF + part * PART, PART)
            at = pl.ds(pl.multiple_of(part * PART, PART), PART)
            total = self.sum_core[pl.ds(own, PART), :].astype(F32)
            for step in range(1, 4):
                total = total + self.y_first[step, at, :].astype(F32)
            self.sum_y[at, :] = total.astype(BF16)

        for step in range(1, 4):
            self.x_second_copy(step).start()

    def plane_sum(self, sum_plane):
        x, y = self.where[0], self.where[1] // 4
        for step in range(1, 4):
            self.waiting(self.sum_x.at[pl.ds(0, PART)], self.y_second, step, self.sems[6:8]).wait_recv()
        total = self.sum_x[pl.ds(pl.multiple_of(y * PART, PART), PART), :].astype(F32)
        for step in range(1, 4):
            total = total + self.y_second[step].astype(F32)
        sum_plane[0:PART, :] = total.astype(BF16)
        for step in range(1, 4):
            self.x_second_copy(step).wait()
        total = self.sum_y[pl.ds(pl.multiple_of(x * PART, PART), PART), :].astype(F32)
        for step in range(3):
            total = total + self.x_second[step].astype(F32)
        sum_plane[PART:, :] = total.astype(BF16)

    def close(self):
        for step in range(1, 4):
            self.waiting(self.sum_core.at[pl.ds(0, HALF)], self.y_first, step, self.sems[4:6]).wait_send()
            self.waiting(self.sum_x.at[pl.ds(0, PART)], self.y_second, step, self.sems[6:8]).wait_send()


def remote(src, dst, send_sem, recv_sem, peer):
    return pltpu.make_async_remote_copy(
        src_ref=src, dst_ref=dst, send_sem=send_sem, recv_sem=recv_sem, device_id=peer, device_id_type=MESH
    )


def finish_shares(
    out_ref,
    sum_plane,
    from_line,
    share_buf,
    square_buf,
    from_near,
    near_buf,
    from_far,
    far_buf,
    from_cross,
    line_send,
    line_recv,
    share_send,
    share_recv,
    near_send,
    near_recv,
    far_send,
    far_recv,
    cross_send,
    cross_recv,
):
    x = lax.axis_index("branch")
    row = lax.axis_index("row")
    col = lax.axis_index("col")
    core, z_hi, y = row % 2, (row // 2) % 2, row // 4
    z = z_hi * 8 + col
    partner = (x, row + 1 - 2 * core, col)

    def line_peer(step):
        there = (z + step) % 16
        return (x, y * 4 + (there // 8) * 2 + core, there % 8)

    def near_peer(step):
        there = (y * 2 + core + step) % 8
        return (x, there // 2 * 4 + z_hi * 2 + there % 2, col)

    def near_copy(step):
        return remote(square_buf, from_near.at[step - 1], near_send.at[step - 1], near_recv.at[step - 1], near_peer(step))

    def far_copy(step):
        return remote(near_buf, from_far.at[step - 1], far_send.at[step - 1], far_recv.at[step - 1], line_peer(step))

    def line_copy(block):
        target = (block // 2) * 8 + (block % 2) * 4 + x
        step = (z - target + 16) % 16
        slot = (step + 14) % 15
        return step, remote(
            sum_plane.at[pl.ds(pl.multiple_of(block * WINDOW, WINDOW), WINDOW)],
            from_line.at[slot], line_send.at[block], line_recv.at[slot],
            (x, y * 4 + (target // 8) * 2 + core, target % 8),
        )

    for block in range(4):
        step, copy = line_copy(block)

        @pl.when(step != 0)
        def _():
            copy.start()

    owner_x = col % 4
    owner = owner_x == x

    def share_copy(step):
        return remote(
            share_buf, share_buf, share_send.at[step - 1], share_recv.at[0],
            ((x + step) % 4, row, col),
        )

    @pl.when(owner)
    def _():
        @pl.loop(0, 15)
        def _(slot):
            remote(
                sum_plane.at[pl.ds(0, WINDOW)], from_line.at[slot], line_send.at[0], line_recv.at[slot], partner
            ).wait_recv()

        own = pl.multiple_of((z_hi * 2 + col // 4) * WINDOW, WINDOW)
        total = sum_plane[pl.ds(own, WINDOW), :].astype(jnp.float32)
        for slot in range(15):
            total = total + from_line[slot].astype(jnp.float32)
        share_buf[...] = total
        offset = (SHARE * (row * 8 + col)) % 1024
        place = lax.broadcasted_iota(jnp.int32, (WINDOW, 128), 0) * 128 + lax.broadcasted_iota(
            jnp.int32, (WINDOW, 128), 1
        )
        inside = jnp.logical_and(place >= offset, place < offset + SHARE)
        square_buf[...] = jnp.where(inside, total * total, 0.0).reshape(8, 8, 128).sum(axis=0)

        for step in range(1, 8):
            near_copy(step).start()
        for step in range(1, 4):
            share_copy(step).start()
        squares = square_buf[...]
        for step in range(1, 8):
            near_copy(step).wait_recv()
            squares = squares + from_near[step - 1]
        near_buf[...] = squares

        @pl.loop(1, 16)
        def _(step):
            far_copy(step).start()

    @pl.when(jnp.logical_not(owner))
    def _():
        near_buf[...] = jnp.zeros((8, 128), F32)

    far_buf[...] = near_buf[...]
    for index in range(4):
        source = 4 * index + x
        step = (z - source + 16) % 16

        @pl.when(step != 0)
        def _():
            slot = (step + 14) % 15
            remote(near_buf, from_far.at[slot], far_send.at[0], far_recv.at[slot], partner).wait_recv()
            far_buf[...] += from_far[slot]

    def cross_copy(step):
        return remote(
            far_buf, from_cross.at[step - 1], cross_send.at[step - 1], cross_recv.at[step - 1], ((x + step) % 4, row, col)
        )

    for step in range(1, 4):
        cross_copy(step).start()

    @pl.when(jnp.logical_not(owner))
    def _():
        share_copy(1).wait_recv()

    for step in range(1, 4):
        cross_copy(step).wait()

    total_squares = jnp.sum(far_buf[...] + from_cross[...].sum(axis=0), keepdims=True)
    spread_rms = jnp.sqrt(total_squares / TOTAL + EPSILON)
    out_ref[...] = share_buf[...] * jnp.minimum(jnp.float32(1.0), 1.0 / spread_rms)

    for block in range(4):
        step, copy = line_copy(block)

        @pl.when(step != 0)
        def _():
            copy.wait_send()

    @pl.when(owner)
    def _():
        @pl.loop(1, 16)
        def _(step):
            far_copy(step).wait_send()

        for step in range(1, 8):
            near_copy(step).wait_send()
        for step in range(1, 4):
            share_copy(step).wait_send()


GROUP = 384
LATE = 28
CELLS = 24
PIECES = (
    (48, 0, 0, 432), (96, 162, 0, 864), (192, 810, 0, 1728), (96, 3402, 864, 432), (192, 3726, 1728, 864),
    (48, 5022, 432, 96), (48, 5058, 528, 192), (48, 5130, 720, 384), (96, 5274, 1296, 192),
    (96, 5418, 1488, 384), (192, 5706, 2592, 384),
)


def dot(left, right, left_dim=1, right_dim=0):
    return lax.dot_general(left, right, (((left_dim,), (right_dim,)), ((), ())), preferred_element_type=F32)


def lanes_of(rows, lanes):
    return lax.broadcasted_iota(jnp.int32, (rows, lanes), 1)


def packet_rows(up):
    maps = (
        (0, 3, 16, (11, 4), (3, 12)), (1, 3, 8, (5, 2), (1, 6)), (2, 3, 4, (2, 1), (0, 3)),
        (3, 2, 8, (5, 2), (1, 6)), (4, 1, 4, (2, 1), (0, 3)), (5, 2, 4, (2, 1), (0, 3)),
    )
    return [
        (index, tile, rows, leaves[up], lands[up]) for index, tiles, rows, leaves, lands in maps for tile in range(tiles)
    ]


def fill_packets(maps, send_rows, send_corners):
    for up in range(2):
        parts = [
            maps[index][tile, pl.ds(rows + leaves, CELLS, stride=rows), :]
            for index, tile, rows, leaves, lands in packet_rows(up)
        ]
        send_rows[up] = jnp.concatenate(parts, axis=0).astype(BF16)
        blank = [jnp.zeros((2, 128), F32)]
        send_corners[2 * up] = jnp.concatenate([part[CELLS - 1 : CELLS] for part in parts] + blank, axis=0).astype(BF16)
        send_corners[2 * up + 1] = jnp.concatenate([part[0:1] for part in parts] + blank, axis=0).astype(BF16)


def fill_sides(u1, u2, u3, send_sides):
    for index, start in enumerate(((CELLS - 1) * GROUP, 0)):
        parts = [value[:, start : start + GROUP] for value in (u1, u2, u3)] + [jnp.zeros((2, GROUP), F32)]
        send_sides[index] = jnp.concatenate(parts, axis=0).astype(BF16)


def banded(weights, repeat, width, rows, blocks, dst):
    wide = dot(weights, repeat)
    lane = lanes_of(rows, repeat.shape[1])
    for block, pieces in enumerate(blocks):
        value = jnp.zeros((rows, repeat.shape[1]), F32)
        for tap, start in pieces:
            inside = jnp.logical_and(lane >= start, lane < start + width)
            value = jnp.where(inside, wide[tap * rows : (tap + 1) * rows], value)
        dst[block * rows : (block + 1) * rows, :] = value.astype(BF16)


def conv_blocks(width, base):
    return [[(tap, base + width * (n + 1 - tap)) for tap in range(3)] for n in range(GROUP // width)]


def down_blocks(width):
    blocks = []
    for j in range(2 * (GROUP // width)):
        if j % 2 == 0:
            blocks.append([(1, width * (j // 2))])
        else:
            blocks.append([(2, width * (j // 2)), (0, width * (j // 2 + 1))])
    return blocks


def mixer_blocks(width, count):
    return [[(0, width * j)] for j in range(count)]


def window(value, start, width):
    first, end = start // 128, -(-(start + width) // 128)
    part = value[:, first * 128 : end * 128]
    shift = start - first * 128
    if shift:
        part = pltpu.roll(part, (end - first) * 128 - shift, 1)
    return part[:, : -(-width // 128) * 128]


def place(src, flat, width, flat_base, src_base, count):
    stride = GROUP // width
    rows = count // stride
    lane = lanes_of(rows, 128)
    held = {}
    for tile in range(3):
        value = None
        for j in range(stride):
            for part in range(-(-width // 128)):
                low = max(width * j + 128 * part, 128 * tile)
                high = min(width * j + min(width, 128 * part + 128), 128 * tile + 128)
                if low >= high:
                    continue
                if (j, part) not in held:
                    held[j, part] = src[part, pl.ds(src_base + j, rows, stride=stride), :]
                piece = held[j, part]
                shift = (width * j + 128 * part - 128 * tile) % 128
                if shift:
                    piece = pltpu.roll(piece, shift, 1)
                value = piece if value is None else jnp.where(lane >= low - 128 * tile, piece, value)
        flat[pl.ds(flat_base + tile, rows, stride=3), :] = value


def backward_kernel(
    u1_ref, u2_ref, u3_ref, *refs,
):
    far = refs[:LATE]
    outs, near, (late_sems, *rest) = refs[LATE : LATE + 5], refs[LATE + 5 : 2 * LATE + 5], refs[2 * LATE + 5 :]
    copies = [pltpu.make_async_copy(src, dst, late_sems.at[i]) for i, (src, dst) in enumerate(zip(far, near))]
    for copy in copies:
        copy.start()
    backward_stages(copies, u1_ref, u2_ref, u3_ref, *near, *outs, *rest)


def backward_stages(
    late_copies, u1_ref, u2_ref, u3_ref, f1_ref, f2_ref, f3_ref, f4_ref, o1_ref, o2_ref, o3_ref,
    k1_ref, k2_ref, k3_ref, s12_ref, s23_ref, m21_ref, m31_ref, m41_ref, m32_ref, m42_ref, m43_ref,
    rep1_ref, rep2_ref, rep3_ref, rep12_ref, rep23_ref, rep96_ref, rep192_ref, pool1_ref, pool2_ref, pool3_ref,
    g1_ref, g2_ref, g3_ref, g4_ref, share_ref,
    packed_ref, send_rows, send_sides, send_corners, recv_rows, recv_sides, recv_corners, halo_send, halo_recv,
    ext1, ext2, ext3, pp12, pp13, pp23, v1, v2, v3, del1, del2, del3, pad_f2, pad_f3, pad_o1, pad_o2, pad_o3, rows_f4,
    band1, band2, band3, band12, band23, band21, band31, band32, res2, res3, w48, w96, w192, flat, *reduce_refs,
):
    def lanes(g):
        return slice(GROUP * g, GROUP * (g + 1))

    x = lax.axis_index("branch")
    row = lax.axis_index("row")
    col = lax.axis_index("col")
    core, z_hi, y = row % 2, (row // 2) % 2, row // 4
    z = z_hi * 8 + col
    line = x * 16 + row

    def peer(down, right):
        there = (line + down + 64) % 64
        return (there // 16, there % 16, (col + right + 8) % 8)

    routes = (
        (0, 1, 0, send_rows.at[0], recv_rows.at[0]),
        (1, -1, 0, send_rows.at[1], recv_rows.at[1]),
        (2, 0, 1, send_sides.at[0], recv_sides.at[0]),
        (3, 0, -1, send_sides.at[1], recv_sides.at[1]),
        (4, 1, 1, send_corners.at[0], recv_corners.at[0]),
        (5, 1, -1, send_corners.at[1], recv_corners.at[1]),
        (6, -1, 1, send_corners.at[2], recv_corners.at[2]),
        (7, -1, -1, send_corners.at[3], recv_corners.at[3]),
    )

    def line_peer(step):
        there = (z + step) % 16
        return (x, y * 4 + (there // 8) * 2 + core, there % 8)

    def near_peer(step):
        there = (y * 2 + core + step) % 8
        return (x, there // 2 * 4 + z_hi * 2 + there % 2, col)

    def greet(peer):
        pl.semaphore_signal(barrier, inc=1, device_id=peer, device_id_type=MESH)

    barrier = pltpu.get_barrier_semaphore()
    for route in routes:
        greet(peer(route[1], route[2]))
    @pl.loop(1, 16)
    def _(step):
        greet(line_peer(step))

    for step in range(1, 4):
        greet(((x + step) % 4, row, col))
    for step in range(1, 8):
        greet(near_peer(step))

    u1, u2, u3 = (ref[...].astype(F32) for ref in (u1_ref, u2_ref, u3_ref))
    fill_sides(u1, u2, u3, send_sides)
    for ref in (ext1, ext2, ext3):
        ref[...] = jnp.zeros_like(ref)
    for g in range(CELLS):
        for tile in range(3):
            part = slice(GROUP * g + 128 * tile, GROUP * g + 128 * tile + 128)
            ext1[tile, 16 * g + 20 : 16 * g + 28, :] = u1[:, part]
            ext2[tile, 8 * g + 10 : 8 * g + 14, :] = u2[:, part]
            ext3[tile, 4 * g + 5 : 4 * g + 7, :] = u3[:, part]

    for copy in late_copies:
        copy.wait()

    tall1, tall2, tall3 = 16 * (CELLS + 2), 8 * (CELLS + 2), 4 * (CELLS + 2)
    def tiled_store(ref, value, rows=slice(None)):
        for tile in range(value.shape[1] // 128):
            ref[tile, rows, :] = value[:, 128 * tile : 128 * tile + 128]

    def strided(ref, tiles, start, count, stride):
        parts = [ref[tile, pl.ds(start, count, stride=stride), :] for tile in tiles]
        return parts[0] if len(parts) == 1 else jnp.concatenate(parts, axis=1)

    def strided_sum(ref, picks, count, stride, tiles):
        total = None
        for pick in picks:
            piece = strided(ref, tiles, pick, count, stride)
            total = piece if total is None else total + piece
        return total

    def whole_of(ref, rows):
        return jnp.concatenate([ref[tile, rows, :] for tile in range(ref.shape[0])], axis=1)

    def run_pools():
        tiled_store(v1, dot(whole_of(ext1, slice(0, tall1)).astype(BF16), pool1_ref[...]))
        tiled_store(v2, dot(whole_of(ext2, slice(0, tall2)).astype(BF16), pool2_ref[...]))
        tiled_store(pp12, strided_sum(v1, range(2), tall2, 2, (0, 1)))
        tiled_store(pp13, strided_sum(v1, range(4), tall3, 4, (2,)))
        tiled_store(pp23, strided_sum(v2, range(2), tall3, 2, (0, 1)))

    def pooled():
        return (
            whole_of(pp12, slice(0, tall2)).astype(BF16),
            whole_of(pp13, slice(0, tall3)).astype(BF16),
            whole_of(pp23, slice(0, tall3)).astype(BF16),
        )

    run_pools()
    tiled_store(v3, dot(whole_of(ext3, slice(0, tall3)).astype(BF16), pool3_ref[...]))
    p14 = strided_sum(v1, range(16 + 4, 16 + 12), CELLS, 16, (3,)).astype(BF16)
    p24 = strided_sum(v2, range(8 + 2, 8 + 6), CELLS, 8, (2,)).astype(BF16)
    p34 = strided_sum(v3, range(4 + 1, 4 + 3), CELLS, 4, (0, 1)).astype(BF16)
    p12, p13, p23 = pooled()
    fill_packets((ext1, ext2, ext3, pp12, pp13, pp23), send_rows, send_corners)
    pl.semaphore_wait(barrier, 33)

    def halo_copy(route):
        slot, down, right, src, dst = route
        return pltpu.make_async_remote_copy(
            src_ref=src, dst_ref=dst, send_sem=halo_send.at[slot], recv_sem=halo_recv.at[slot],
            device_id=peer(down, right), device_id_type=MESH,
        )

    for route in routes:
        halo_copy(route).start()

    for ref in (pad_f2, pad_f3, pad_o1, pad_o2, pad_o3):
        ref[...] = jnp.zeros_like(ref)
    f2, f3, o1, o2, o3, f4 = (ref[...].astype(F32) for ref in (f2_ref, f3_ref, o1_ref, o2_ref, o3_ref, f4_ref))
    for g in range(CELLS):
        at = lanes(g)
        pad_f2[8 * g + 2 : 8 * g + 6, :] = f2[:, at]
        pad_f3[4 * g + 1 : 4 * g + 3, :] = f3[:, at]
        for tile in range(3):
            part = slice(GROUP * g + 128 * tile, GROUP * g + 128 * tile + 128)
            pad_o1[tile, 16 * g + 4 : 16 * g + 12, :] = o1[:, part]
            pad_o2[tile, 8 * g + 2 : 8 * g + 6, :] = o2[:, part]
        pad_o3[4 * g + 1 : 4 * g + 3, :] = o3[:, at]
        rows_f4[g : g + 1, :] = f4[:, at]

    for a in range(3):
        banded(k1_ref[144 * a : 144 * a + 144, :], rep1_ref[...], 48, 48, conv_blocks(48, 128), band1.at[a])
        banded(k2_ref[288 * a : 288 * a + 288, :], rep2_ref[...], 96, 96, conv_blocks(96, 128), band2.at[a])
        banded(k3_ref[576 * a : 576 * a + 576, :], rep3_ref[...], 192, 192, conv_blocks(192, 256), band3.at[a])
        banded(s12_ref[144 * a : 144 * a + 144, :], rep12_ref[...], 96, 48, down_blocks(96), band12.at[a])
        banded(s23_ref[288 * a : 288 * a + 288, :], rep23_ref[...], 192, 96, down_blocks(192), band23.at[a])
    banded(m21_ref[...], rep96_ref[...], 96, 48, mixer_blocks(96, 4), band21)
    banded(m31_ref[...], rep192_ref[...], 192, 48, mixer_blocks(192, 2), band31)
    banded(m32_ref[...], rep96_ref[:, :256], 96, 192, mixer_blocks(96, 2), band32)

    reduction = Reduction(packed_ref, (x, row, col), *reduce_refs[:8], reduce_refs[8:18])
    flat[6282:FLAT_ROWS, :] = jnp.zeros((FLAT_ROWS - 6282, 128), F32)

    def settle(pieces, halves):
        for piece in pieces:
            width, flat_base, src_base, count = PIECES[piece]
            place({48: w48, 96: w96, 192: w192}[width], flat, width, flat_base, src_base, count)
        for block, half in halves:
            pack_shares(flat, packed_ref, block, half)
            reduction.leave(block, half)

    def fold_mixer(grads, width, rows, base, dst):
        total = None
        for j in range(GROUP // rows):
            part = window(grads[j * rows : (j + 1) * rows, :], width * j, width)
            total = part if total is None else total + part
        tiled_store(dst, total, slice(base, base + rows))

    o2x = jnp.concatenate([pad_o2[tile] for tile in range(3)], axis=1).astype(BF16)
    o3x = pad_o3[...].astype(BF16)
    f4x = rows_f4[...].astype(BF16)
    inner2, inner3 = slice(8, 8 + 8 * CELLS), slice(4, 4 + 4 * CELLS)
    fold_mixer(dot(o2x, p12[inner2], 0, 0), 48, 96, 432, w48)
    fold_mixer(dot(o3x, p13[inner3], 0, 0), 48, 192, 528, w48)
    fold_mixer(dot(f4x, p14, 0, 0), 48, 384, 720, w48)
    fold_mixer(dot(o3x, p23[inner3], 0, 0), 96, 192, 1296, w96)
    fold_mixer(dot(f4x, p24, 0, 0), 96, 384, 1488, w96)
    fold_mixer(dot(f4x, p34, 0, 0), 192, 384, 2592, w192)
    back4 = (
        dot(p14[:, 0:48], m41_ref[...]) + dot(p24[:, 0:96], m42_ref[...]) + dot(p34[:, 0:192], m43_ref[...])
    )
    for g in range(CELLS):
        g4_ref[:, lanes(g)] = back4[g : g + 1].astype(BF16)

    settle((5, 6, 7, 8, 9, 10), ((3, 1),))

    for route in routes:
        halo_copy(route).wait()
    top, bottom = jnp.where(line > 0, 1.0, 0.0), jnp.where(line < 63, 1.0, 0.0)
    left, right = jnp.where(col > 0, 1.0, 0.0), jnp.where(col < 7, 1.0, 0.0)
    sides = [recv_sides[0].astype(F32) * left, recv_sides[1].astype(F32) * right]
    corners = [
        recv_corners[0].astype(F32) * (top * left), recv_corners[1].astype(F32) * (top * right),
        recv_corners[2].astype(F32) * (bottom * left), recv_corners[3].astype(F32) * (bottom * right),
    ]
    for index, group in enumerate((0, CELLS + 1)):
        for tile in range(3):
            part = sides[index][:, 128 * tile : 128 * tile + 128]
            ext1[tile, 16 * group + 4 : 16 * group + 12, :] = part[0:8]
            ext2[tile, 8 * group + 2 : 8 * group + 6, :] = part[8:12]
            ext3[tile, 4 * group + 1 : 4 * group + 3, :] = part[12:14]

    def fill_rims(refs, first):
        for up, flag in enumerate((top, bottom)):
            packet = recv_rows[up].astype(F32) * flag
            for place_in, (index, tile, rows, leaves, lands) in enumerate(packet_rows(up)):
                if not first <= index < first + 3:
                    continue
                ref = refs[index - first]
                part = packet[CELLS * place_in : CELLS * (place_in + 1)]
                ref[tile, pl.ds(rows + lands, CELLS, stride=rows), :] = part
                ref[tile, lands : lands + 1, :] = corners[2 * up][place_in : place_in + 1]
                last = rows * (CELLS + 1) + lands
                ref[tile, last : last + 1, :] = corners[2 * up + 1][place_in : place_in + 1]

    fill_rims((ext1, ext2, ext3), 0)
    run_pools()
    fill_rims((pp12, pp13, pp23), 3)
    p12, p13, p23 = pooled()

    def fold_down(grads, width, rows, a, base, dst):
        for b in range(3):
            total = None
            for j in range(1 if b != 1 else 0, 2 * (GROUP // width), 2):
                p = (j + 1 - b) // 2
                part = window(grads[j * rows : (j + 1) * rows, :], width * p, width)
                total = part if total is None else total + part
            start = base + (a * 3 + b) * rows
            tiled_store(dst, total, slice(start, start + rows))

    def down_grads(saved, ext, skip, count, head, width, rows, base, dst):
        even = strided(saved, range(3), 0, count, 2).astype(BF16)
        odd = strided(saved, range(3), 1, count, 2).astype(BF16)
        for a in range(3):
            at = skip + (1 if a == 0 else 0)
            xs = jnp.concatenate(
                [ext[tile, at : at + count, :] for tile in range(3)]
                + [ext[tile, at + skip : at + skip + count, :] for tile in range(head // 128)],
                axis=1,
            ).astype(BF16)
            fold_down(dot(even if a == 1 else odd, xs, 0, 0), width, rows, a, base, dst)

    down_grads(pad_o1, ext2, 8, 8 * CELLS, 128, 96, 48, 864, w96)
    down_grads(pad_o2, ext3, 4, 4 * CELLS, 256, 192, 96, 1728, w192)

    settle((3, 4), ((3, 0),))
    reduction.spread(3, 1)

    def rim_mask(rows, inner):
        place_row = lax.broadcasted_iota(jnp.int32, (CELLS + 2, rows, GROUP), 1)
        place_col = lax.broadcasted_iota(jnp.int32, (CELLS + 2, rows, GROUP), 0)
        start, end = (rows - inner) // 2, (rows + inner) // 2
        by_row = jnp.where(place_row == start - 1, top, jnp.where(place_row == end, bottom, 1.0))
        by_row = jnp.where(jnp.logical_and(place_row >= start - 1, place_row <= end), by_row, 0.0)
        by_col = jnp.where(place_col == 0, left, jnp.where(place_col == CELLS + 1, right, 1.0))
        return by_row * by_col

    def rolled(value):
        return pltpu.roll(value, value.shape[0] - 1, 0)

    x2 = jnp.concatenate([whole_of(ext2, slice(0, tall2)), ext2[0, 8 : tall2 + 8, :]], axis=1).astype(BF16)
    tiled_store(v1, dot(x2, band12[1], 1, 1), pl.ds(0, tall2, stride=2))
    tiled_store(v1, dot(x2, band12[2], 1, 1) + rolled(dot(x2, band12[0], 1, 1)), pl.ds(1, tall2, stride=2))
    spread1 = jnp.concatenate([v1[tile] for tile in range(3)], axis=1)
    delta1 = (whole_of(ext1, slice(0, tall1)) + spread1).reshape(CELLS + 2, 16, GROUP)
    del1[...] = (delta1 * rim_mask(16, 8)).astype(BF16).astype(F32)

    x3 = jnp.concatenate(
        [whole_of(ext3, slice(0, tall3)), ext3[0, 4 : tall3 + 4, :], ext3[1, 4 : tall3 + 4, :]], axis=1
    ).astype(BF16)
    tiled_store(v2, dot(x3, band23[1], 1, 1), pl.ds(0, tall3, stride=2))
    tiled_store(v2, dot(x3, band23[2], 1, 1) + rolled(dot(x3, band23[0], 1, 1)), pl.ds(1, tall3, stride=2))
    spread2 = jnp.concatenate([v2[tile] for tile in range(3)], axis=1)
    delta2 = whole_of(ext2, slice(0, tall2)) + dot(p12[:, 0:192], band21[...]) + spread2
    del2[8 : 8 + tall2, :] = (delta2 * rim_mask(8, 4).reshape(tall2, GROUP)).astype(BF16).astype(F32)

    delta3 = whole_of(ext3, slice(0, tall3)) + dot(p13[:, 0:96], band31[...]) + dot(p23, band32[...], 1, 1)
    place_row = lax.broadcasted_iota(jnp.int32, (tall3, GROUP), 0)
    in_group = jnp.bitwise_and(place_row, 3)
    by_row = jnp.where(in_group == 0, top, jnp.where(in_group == 3, bottom, 1.0))
    by_col = jnp.where(place_row < 4, left, jnp.where(place_row >= 4 * (CELLS + 1), right, 1.0))
    del3[8 : 8 + tall3, :] = (delta3 * (by_row * by_col)).astype(BF16).astype(F32)
    for ref in (del2, del3):
        ref[0:8, :] = jnp.zeros((8, GROUP), F32)
        ref[ref.shape[0] - 8 :, :] = jnp.zeros((8, GROUP), F32)

    reduction.spread(3, 0)

    def fold(grads, width, base, a, dst):
        total = None
        for n in range(GROUP // width):
            part = window(grads[n * width : (n + 1) * width, :], base + width * (n - 1), 3 * width)
            total = part if total is None else total + part
        for tap in range(3):
            start = (a * 3 + tap) * width
            tiled_store(dst, window(total, width * (2 - tap), width), slice(start, start + width))

    f3x = pad_f3[...].astype(BF16)
    back = None
    for a in range(3):
        at = 8 + 1 - a
        n = 4 * CELLS
        x3d = jnp.concatenate(
            [del3[at : at + n, 128:GROUP], del3[at + 4 : at + 4 + n, :], del3[at + 8 : at + 8 + n, 0:256]], axis=1
        ).astype(BF16)
        part = dot(x3d, band3[a], 1, 1)
        back = part if back is None else back + part
        fold(dot(f3x, x3d, 0, 0), 192, 256, a, w192)
    res3[...] = back
    for g in range(CELLS):
        g3_ref[:, lanes(g)] = res3[4 * g + 1 : 4 * g + 3, :].astype(BF16)

    settle((2,), ((2, 0), (2, 1), (1, 0), (1, 1)))

    f2x = pad_f2[...].astype(BF16)
    back = None
    for a in range(3):
        at = 8 + 1 - a
        n = 8 * CELLS
        x2d = jnp.concatenate(
            [del2[at : at + n, 256:GROUP], del2[at + 8 : at + 8 + n, :], del2[at + 16 : at + 16 + n, 0:128]], axis=1
        ).astype(BF16)
        part = dot(x2d, band2[a], 1, 1)
        back = part if back is None else back + part
        fold(dot(f2x, x2d, 0, 0), 96, 128, a, w96)
    res2[...] = back
    for g in range(CELLS):
        g2_ref[:, lanes(g)] = res2[8 * g + 2 : 8 * g + 6, :].astype(BF16)

    settle((1,), ((0, 1),))
    for block, half in ((2, 0), (2, 1), (1, 0), (1, 1)):
        reduction.spread(block, half)

    f1 = f1_ref[...]
    f1 = jnp.concatenate([f1[:, lanes(g)].astype(F32) for g in range(CELLS)], axis=0).astype(BF16)
    back = None
    for a in range(3):
        at = slice(5 - a, 13 - a)
        x1 = jnp.concatenate(
            [del1[0:CELLS, at, 256:GROUP], del1[1 : CELLS + 1, at, :], del1[2 : CELLS + 2, at, 0:128]], axis=2
        ).reshape(8 * CELLS, 640).astype(BF16)
        part = dot(x1, band1[a], 1, 1)
        back = part if back is None else back + part
        fold(dot(f1, x1, 0, 0), 48, 128, a, w48)
    for g in range(CELLS):
        g1_ref[:, lanes(g)] = back[8 * g : 8 * g + 8].astype(BF16)

    settle((0,), ((0, 0),))
    reduction.spread(0, 1)
    reduction.spread(0, 0)
    for block in (3, 2, 1, 0):
        reduction.turn_to_y(block)
    reduction.turn_to_x()
    reduction.plane_sum(reduce_refs[18])
    finish_shares(share_ref, *reduce_refs[18:])
    reduction.close()


def repeats(width, lanes, base=0):
    lane = np.arange(lanes)[None, :]
    return ((lane - base) % width == np.arange(width)[:, None]).astype(np.float32)


def pools(width, factors, parts):
    blocks = []
    for factor, lanes in zip(factors, parts):
        block = np.zeros((GROUP, lanes), np.float32)
        for lane in range(GROUP):
            block[lane, lane // (width * factor) * width + lane % width] = 1.0
        blocks.append(block)
    return np.concatenate(blocks, axis=1)


def hand_over_kernel(*refs):
    share_ref, out_ref = refs[4], refs[9]
    for source, target in zip(refs[0:4], refs[5:9]):
        target[...] = source[...]
    offset = (SHARE * (lax.axis_index("row") * 8 + lax.axis_index("col"))) % 1024
    rows, lanes = offset // 128, offset % 128
    share = share_ref[...]
    first = pltpu.roll(pltpu.roll(share, (WINDOW - rows) % WINDOW, 0), (128 - lanes) % 128, 1)
    then = pltpu.roll(pltpu.roll(share, WINDOW - 1 - rows, 0), (128 - lanes) % 128, 1)
    out_ref[...] = jnp.where(lanes_of(WINDOW, 128) < 128 - lanes, first, then)[0:56]


def hand_over(*results):
    whole = pl.BlockSpec(memory_space=pltpu.VMEM)
    return pl.pallas_call(
        hand_over_kernel,
        out_shape=[jax.ShapeDtypeStruct(value.shape, BF16) for value in results[:4]]
        + [jax.ShapeDtypeStruct((56, 128), F32)],
        in_specs=[whole] * 5,
        out_specs=[whole] * 5,
        compiler_params=pltpu.CompilerParams(vmem_limit_bytes=56 * 1024 * 1024),
        name="hand_over",
    )(*results)


def local(f1, f2, f3, f4, o1, o2, o3, u1, u2, u3, k1, k2, k3, s12, s23, m21, m31, m41, m32, m42, m43):
    constants = [
        jnp.asarray(value, BF16)
        for value in (
            repeats(48, 640, 128), repeats(96, 640, 128), repeats(192, 896, 256), repeats(96, 512), repeats(192, 640),
            repeats(96, 384), repeats(192, 384),
            pools(48, (2, 4, 8), (256, 128, 128)), pools(96, (2, 4), (256, 128)), pools(192, (2,), (256,)),
        )
    ]
    whole = pl.BlockSpec(memory_space=pltpu.VMEM)
    inputs = [
        u1, u2, u3, f1, f2, f3, f4, o1, o2, o3,
        k1.reshape(432, 48), k2.reshape(864, 96), k3.reshape(1728, 192), s12.reshape(432, 96), s23.reshape(864, 192),
        m21.T, m31.T, m41.T, m32, m42.T, m43.T,
    ] + constants

    def f32(*shape):
        return pltpu.VMEM(shape, F32)

    def bf16(*shape):
        return pltpu.VMEM(shape, BF16)

    ext = CELLS + 2
    dma = pltpu.SemaphoreType.DMA
    packets = ((2, 14 * CELLS, 128), (2, 16, GROUP), (4, 16, 128))
    grad_one, grad_two, grad_three, grad_four, share = pl.pallas_call(
        backward_kernel,
        out_shape=[jax.ShapeDtypeStruct(value.shape, BF16) for value in (f1, f2, f3, f4)]
        + [jax.ShapeDtypeStruct((WINDOW, 128), F32)],
        in_specs=[whole] * 3 + [pl.BlockSpec(memory_space=pl.ANY)] * LATE,
        out_specs=[whole] * 5,
        scratch_shapes=[
            *(pltpu.VMEM(value.shape, BF16) for value in inputs[3:]), dma((LATE,)),
            bf16(128 * WINDOW, 128), *(bf16(*shape) for shape in packets + packets), dma((8,)), dma((8,)),
            f32(3, 16 * ext, 128), f32(3, 8 * ext + 8, 128), f32(3, 4 * ext + 8, 128),
            f32(2, 8 * ext, 128), f32(1, 4 * ext, 128), f32(2, 4 * ext, 128),
            f32(4, 16 * ext, 128), f32(3, 8 * ext, 128), f32(2, 4 * ext, 128),
            f32(ext, 16, GROUP), f32(8 * ext + 16, GROUP), f32(4 * ext + 16, GROUP),
            f32(8 * CELLS, GROUP), f32(4 * CELLS, GROUP), f32(3, 16 * CELLS, 128), f32(3, 8 * CELLS, 128),
            f32(4 * CELLS, GROUP), f32(CELLS, GROUP),
            bf16(3, GROUP, 640), bf16(3, GROUP, 640), bf16(3, GROUP, 896), bf16(3, GROUP, 512), bf16(3, GROUP, 640),
            bf16(192, GROUP), bf16(96, GROUP), bf16(GROUP, 256),
            f32(8 * CELLS, GROUP), f32(4 * CELLS, GROUP),
            f32(1, 1104, 128), f32(1, 1872, 128), f32(2, 2976, 128), f32(FLAT_ROWS, 128),
            bf16(4 * BLOCK, 128), bf16(4 * BLOCK, 128), bf16(12, PART, 128), bf16(4 * PART, 128), bf16(4, PART, 128),
            bf16(4, HALF, 128), bf16(HALF, 128), bf16(3, PART, 128),
            dma((8,)), dma((8,)), dma((12,)), dma((12,)), dma((4,)), dma((4,)), dma((4,)), dma((4,)), dma((3,)), dma((3,)),
            bf16(2 * PART, 128), bf16(15, WINDOW, 128), f32(WINDOW, 128), f32(8, 128), f32(7, 8, 128), f32(8, 128),
            f32(15, 8, 128), f32(8, 128), f32(3, 8, 128),
            dma((4,)), dma((15,)), dma((3,)), dma((1,)), dma((7,)), dma((7,)), dma((15,)), dma((15,)), dma((3,)), dma((3,)),
        ],
        compiler_params=pltpu.CompilerParams(
            collective_id=0, has_side_effects=True, vmem_limit_bytes=56 * 1024 * 1024
        ),
        name="backward",
    )(*inputs)
    *grads, weight_grads = hand_over(grad_one, grad_two, grad_three, grad_four, share)
    return *grads, weight_grads.reshape(56 * 128)[:SHARE]


def solution(mesh):
    in_specs = (
        P(("branch", "row"), "col"),
        P(("branch", "row"), "col"),
        P(("branch", "row"), "col"),
        P(("branch", "row"), "col"),
        P(("branch", "row"), "col"),
        P(("branch", "row"), "col"),
        P(("branch", "row"), "col"),
        P(("branch", "row"), "col"),
        P(("branch", "row"), "col"),
        P(("branch", "row"), "col"),
        P(),
        P(),
        P(),
        P(),
        P(),
        P(),
        P(),
        P(),
        P(),
        P(),
        P(),
    )
    out_specs = (
        P(("branch", "row"), "col"),
        P(("branch", "row"), "col"),
        P(("branch", "row"), "col"),
        P(("branch", "row"), "col"),
        P(("row", "col")),
    )
    return jax.shard_map(local, mesh=mesh, in_specs=in_specs, out_specs=out_specs, check_vma=False)
```
